128 devices in a mesh: dp: 32 (over y, z, x_hi), pb: 4 (over x_lo, core).
Axes of the slice: x: 4 (x_hi: 2, x_lo: 2; x = x_hi * 2 + x_lo), y: 4, z: 4, core: 2. Of those that a mesh axis runs over, the one named last changes fastest.
Arguments:
- media: bfloat16 [64, 576, 1024], P('dp', 'pb'), may hold values from -6 to 6
- latents: bfloat16 [64, 64, 1024], P('dp', 'pb'), may hold values from -6 to 6
- counts: int32 [64], P('dp'), may hold values from 256 to 576, as said below
- media_gain: float32 [1024], replicated, may hold values from 0.1 to 1.9
- media_shift: float32 [1024], replicated, may hold values from -3 to 3
- latent_gain: float32 [1024], replicated, may hold values from 0.1 to 1.9
- latent_shift: float32 [1024], replicated, may hold values from -3 to 3
- ff_gain: float32 [1024], replicated, may hold values from 0.1 to 1.9
- ff_shift: float32 [1024], replicated, may hold values from -3 to 3
- query_weight: bfloat16 [1024, 512], replicated, may hold values from -0.1875 to 0.1875
- w_key: bfloat16 [1024, 512], replicated, may hold values from -0.1875 to 0.1875
- w_value: bfloat16 [1024, 512], replicated, may hold values from -0.1875 to 0.1875
- output_weight: bfloat16 [512, 1024], replicated, may hold values from -1.5 to 1.5
- up_weight: bfloat16 [1024, 4096], replicated, may hold values from -0.1875 to 0.1875
- down_weight: bfloat16 [4096, 1024], replicated, may hold values from -0.09375 to 0.09375
- latent_output_cotangent: bfloat16 [64, 64, 1024], P('dp', 'pb'), may hold values from -6 to 6
Outputs:
- mixed: bfloat16 [64, 64, 1024], P('dp', 'pb')
- grad_media: float32 [64, 576, 1024], P('dp', 'pb')
- grad_latents: float32 [64, 64, 1024], P('dp', 'pb')
- grad_media_gain: float32 [1024], P(('dp', 'pb'))
- grad_media_shift: float32 [1024], P(('dp', 'pb'))
- grad_latent_gain: float32 [1024], P(('dp', 'pb'))
- grad_latent_shift: float32 [1024], P(('dp', 'pb'))
- grad_ff_gain: float32 [1024], P(('dp', 'pb'))
- grad_ff_shift: float32 [1024], P(('dp', 'pb'))
- grad_query: float32 [1024, 512], P(('dp', 'pb'))
- grad_key: float32 [1024, 512], P(('dp', 'pb'))
- grad_value: float32 [1024, 512], P(('dp', 'pb'))
- output_weight_gradient: float32 [512, 1024], P(None, ('dp', 'pb'))
- up_weight_gradient: float32 [1024, 4096], P(('dp', 'pb'))
- down_weight_gradient: float32 [4096, 1024], P(None, ('dp', 'pb'))
The draws below stay inside these ranges and needn't reach their ends.
Inputs may be any that keep to these rules, and one draw needn't show every extreme that they name: `counts`: each image has 256 or 576 patches, in its first patch slots; among the 2 images of one index of dp a seed-drawn one has 576.
All inputs are finite; a program needn't handle non-finite values.
Results may differ from the reference program's by a relative error of at most 0.015.
Values may be sent and summed in bfloat16 or wider, within the bound.
A program may use at most 192 MiB of HBM per device.

```python
from functools import partial
import jax
import jax.numpy as jnp
from jax import lax

D = 1024
HEADS = 8
HEAD_DIM = 64
FF = 4096
LAT = 64
PATCH = 576
SHORT = 256
IMG_GRP = 2
IMAGES = 64
INNER = 512
N_DP = 32


def draw_counts(key, part):
    key = jax.random.fold_in(key, 11)
    coin_key, pick_key = jax.random.split(key)
    group_count = IMAGES // IMG_GRP
    coins = jax.random.randint(coin_key, (group_count, IMG_GRP), 0, 2)
    chosen = jax.random.randint(pick_key, (group_count, 1), 0, IMG_GRP)
    slot_index = jnp.arange(IMG_GRP)[None, :]
    longer = (coins == 1) | (slot_index == chosen)
    return jnp.where(longer, PATCH, SHORT).reshape(IMAGES).astype(jnp.int32)


def strengthened(entries, own_key, source, target, parts, factor):
    def block_of(dim):
        return (jnp.arange(entries.shape[dim]) // (entries.shape[dim] // parts)).reshape((-1,) + (1,) * (entries.ndim - 1 - dim))

    near = jax.random.permutation(own_key, parts)[block_of(target)]
    other_side = (block_of(target) + parts // 2) % parts
    return jnp.where((block_of(source) == near) | (block_of(source) == other_side), factor * entries, entries)


def block_levels(key, shape, cuts, low, largest):
    level = 1.0
    for dim, shards_of in cuts:
        heights = jax.random.uniform(jax.random.fold_in(jax.random.fold_in(key, 6), dim), (shards_of,), jnp.float32, low / len(cuts), largest / len(cuts))
        level = level * jnp.repeat(jnp.exp(heights), shape[dim] // shards_of).reshape((-1,) + (1,) * (len(shape) - 1 - dim))
    return level


def bell_draw(own_key, shape, width, reach, cuts=(), dtype=jnp.bfloat16):
    result = width * jax.random.normal(own_key, shape, jnp.float32)
    if cuts:
        result = result * block_levels(own_key, shape, cuts, -0.22, 0.18)
    return jnp.clip(result, -reach, reach).astype(dtype)


def bell_draw_with(stream_key, dims, deviation, most, pieces, heavy, held_as=jnp.bfloat16):
    result = deviation * jax.random.normal(stream_key, dims, jnp.float32)
    if pieces:
        result = result * block_levels(stream_key, dims, pieces, -0.22, 0.18)
    return jnp.clip(strengthened(result, jax.random.fold_in(stream_key, 3), *heavy), -most, most).astype(held_as)


def setup_inputs(seed: int = 0) -> dict:
    streams_of = jax.random.split(jax.random.key(seed), 17)
    media = bell_draw(streams_of[0], (IMAGES, PATCH, D), 1.0, 6.0, ((0, 32), (1, 4)))
    latents = bell_draw(streams_of[1], (IMAGES, LAT, D), 1.0, 6.0, ((0, 32), (1, 4)))
    counts = draw_counts(jax.random.fold_in(streams_of[16], 71), 0)
    media_gain = jnp.clip(1.0 + 0.18 * jax.random.normal(streams_of[3], (D,), jnp.float32), 0.1, 1.9)
    media_shift = bell_draw(streams_of[4], (D,), 0.3, 3.0, (), jnp.float32)
    latent_gain = jnp.clip(1.0 + 0.18 * jax.random.normal(streams_of[5], (D,), jnp.float32), 0.1, 1.9)
    latent_shift = bell_draw(streams_of[6], (D,), 0.3, 3.0, (), jnp.float32)
    ff_gain = jnp.clip(1.0 + 0.18 * jax.random.normal(streams_of[7], (D,), jnp.float32), 0.1, 1.9)
    ff_shift = bell_draw(streams_of[8], (D,), 0.3, 3.0, (), jnp.float32)
    query_weight = bell_draw(streams_of[9], (D, INNER), D ** -0.5, 0.1875)
    w_key = bell_draw(streams_of[10], (D, INNER), D ** -0.5, 0.1875)
    w_value = bell_draw(streams_of[11], (D, INNER), D ** -0.5, 0.1875)
    output_weight = bell_draw(streams_of[12], (INNER, D), (INNER // 32) ** -0.5, 1.5)
    up_weight = bell_draw(streams_of[13], (D, FF), D ** -0.5, 0.1875)
    down_weight = bell_draw(streams_of[14], (FF, D), FF ** -0.5, 0.09375)
    latent_output_cotangent = bell_draw_with(streams_of[15], (IMAGES, LAT, D), 1.0, 6.0, ((0, 32), (1, 4)), (0, 2, 32, 2.75))
    return {"media": media, "latents": latents, "counts": counts, "media_gain": media_gain, "media_shift": media_shift, "latent_gain": latent_gain, "latent_shift": latent_shift, "ff_gain": ff_gain, "ff_shift": ff_shift, "query_weight": query_weight, "w_key": w_key, "w_value": w_value, "output_weight": output_weight, "up_weight": up_weight, "down_weight": down_weight, "latent_output_cotangent": latent_output_cotangent}


@jax.custom_vjp
def reduced_precision(v):
    return lax.optimization_barrier(v.astype(jnp.bfloat16)).astype(jnp.float32)

@jax.custom_vjp
def reduced_backward(v):
    return v

def low_keep(v):
    return (reduced_precision(v), None)

def low_pass(kept, grad):
    return (grad,)

def back_keep(v):
    return (v, None)

def back_low(kept, grad):
    return (reduced_precision(grad),)
reduced_precision.defvjp(low_keep, low_pass)
reduced_backward.defvjp(back_keep, back_low)
EPSILON = 1e-05
NEG_FILL = -1e+30
EXACT_PRECISION = lax.Precision.HIGHEST

def layer_norm(source, gain_vec, shift_vec):
    average = lax.optimization_barrier(jnp.mean(source, axis=-1, keepdims=True))
    centered = source - average
    variance = lax.optimization_barrier(jnp.mean(centered * centered, axis=-1, keepdims=True))
    return centered * lax.rsqrt(variance + EPSILON) * gain_vec + shift_vec

def forward(valid, media, latents, media_gain, media_shift, latent_gain, latent_shift, ff_gain, ff_shift, query_weight, w_key, w_value, output_weight, up_weight, down_weight):
    images = media.shape[0]
    attention_score_scale = HEAD_DIM ** (-0.5)
    norm_media = reduced_precision(layer_norm(media, media_gain, media_shift))
    latent_norm = reduced_precision(layer_norm(latents, latent_gain, latent_shift))
    query_matrix = reduced_precision(reduced_backward(jnp.einsum('zlm,mb->zlb', latent_norm, query_weight, precision=EXACT_PRECISION) * attention_score_scale))
    joined = jnp.concatenate([norm_media, latent_norm], axis=1)
    keys_all = reduced_precision(reduced_backward(jnp.einsum('ird,de->ire', joined, w_key, precision=EXACT_PRECISION)))
    values_all = reduced_precision(reduced_backward(jnp.einsum('ird,de->ire', joined, w_value, precision=EXACT_PRECISION)))
    query4 = query_matrix.reshape(images, LAT, HEADS, HEAD_DIM)
    key4 = keys_all.reshape(images, PATCH + LAT, HEADS, HEAD_DIM)
    value4 = values_all.reshape(images, PATCH + LAT, HEADS, HEAD_DIM)
    scores = reduced_backward(jnp.einsum('iahe,ijhe->ihaj', query4, key4, precision=EXACT_PRECISION))
    masked = jnp.where(valid[:, None, None, :], scores, NEG_FILL)
    peak = lax.optimization_barrier(jnp.max(masked, axis=-1, keepdims=True))
    log_total = peak + jnp.log(lax.optimization_barrier(jnp.sum(jnp.exp(masked - peak), axis=-1, keepdims=True)))
    probs = jnp.exp(masked - log_total)
    attended_rows = reduced_precision(reduced_backward(jnp.einsum('ihaj,ijhe->iahe', reduced_precision(probs), value4, precision=EXACT_PRECISION)))
    attended_rows = attended_rows.reshape(images, LAT, HEADS * HEAD_DIM)
    hidden_state = latents + reduced_backward(jnp.einsum('ulw,wb->ulb', attended_rows, output_weight, precision=EXACT_PRECISION))
    feedforward_norm = reduced_precision(layer_norm(hidden_state, ff_gain, ff_shift))
    upper_projection = reduced_backward(jnp.einsum('lcg,gr->lcr', feedforward_norm, up_weight, precision=EXACT_PRECISION))
    activated_rows = reduced_precision(jax.nn.gelu(upper_projection, approximate=False))
    return hidden_state + reduced_backward(jnp.einsum('oqn,nc->oqc', activated_rows, down_weight, precision=EXACT_PRECISION))

def reference(media, latents, counts, media_gain, media_shift, latent_gain, latent_shift, ff_gain, ff_shift, query_weight, w_key, w_value, output_weight, up_weight, down_weight, latent_output_cotangent):
    params = (media_gain, media_shift, latent_gain, latent_shift, ff_gain, ff_shift, query_weight.astype(jnp.float32), w_key.astype(jnp.float32), w_value.astype(jnp.float32), output_weight.astype(jnp.float32), up_weight.astype(jnp.float32), down_weight.astype(jnp.float32))
    media_blocks = media.astype(jnp.float32).reshape(N_DP, IMG_GRP, PATCH, D)
    lat_blocks = latents.astype(jnp.float32).reshape(N_DP, IMG_GRP, LAT, D)
    count_blocks = counts.reshape(N_DP, IMG_GRP)
    cot_blocks = latent_output_cotangent.astype(jnp.float32).reshape(N_DP, IMG_GRP, LAT, D)
    row_index = jnp.arange(PATCH + LAT)

    def one_block(totals, block):
        media_blk, lat_blk, count_blk, cot_blk = block
        valid = (row_index[None, :] < count_blk[:, None]) | (row_index[None, :] >= PATCH)
        layer_result, pullback = jax.vjp(partial(forward, valid), media_blk, lat_blk, *params)
        grads = pullback(cot_blk)
        totals = tuple((running + added for running, added in zip(totals, grads[2:])))
        return (totals, (layer_result.astype(jnp.bfloat16), grads[0], grads[1]))
    zero_grads = tuple((jnp.zeros(param.shape, jnp.float32) for param in params))
    totals, outputs = lax.scan(one_block, zero_grads, (media_blocks, lat_blocks, count_blocks, cot_blocks))
    mixed = outputs[0].reshape(IMAGES, LAT, D)
    grad_media = outputs[1].reshape(IMAGES, PATCH, D)
    grad_latents = outputs[2].reshape(IMAGES, LAT, D)
    return (mixed, grad_media, grad_latents, totals[0], totals[1], totals[2], totals[3], totals[4], totals[5], totals[6], totals[7], totals[8], totals[9], totals[10], totals[11])
```

```python
import functools
import itertools

import jax
import jax.numpy as jnp
from jax import lax
from jax.experimental import pallas as pl
from jax.experimental.pallas import tpu as pltpu
from jax.sharding import PartitionSpec as P

MESH = pl.DeviceIdType.MESH
BF = jnp.bfloat16
F32 = jnp.float32
D = 1024
INNER = 512
FF = 4096
MED = 144
LATD = 16
ROWS = MED + LATD
SLICE = FF // 8
EPSILON = 1e-05
NEG_FILL = -1e30
SCALE = 0.125
N_SEMS = 160


def mm(a, b):
    return jnp.dot(a, b, preferred_element_type=F32)


def mm_nt(a, b):
    return lax.dot_general(a, b, (((1,), (1,)), ((), ())), preferred_element_type=F32)


def mm_tn(a, b):
    return lax.dot_general(a, b, (((0,), (0,)), ((), ())), preferred_element_type=F32)


def normalised(v):
    cen = v - jnp.mean(v, axis=-1, keepdims=True)
    rstd = lax.rsqrt(jnp.mean(cen * cen, axis=-1, keepdims=True) + EPSILON)
    return cen * rstd, rstd


def ln_back(dn, xhat, rstd, gain):
    dx = dn * gain
    return rstd * (
        dx - jnp.mean(dx, axis=-1, keepdims=True) - xhat * jnp.mean(dx * xhat, axis=-1, keepdims=True)
    )


SCRATCH = dict(
    media=((2, MED, D), BF),
    lc=((2, 4, 4, LATD, D), BF),
    wq=((D, INNER), BF),
    wk=((D, INNER), BF),
    wv=((D, INNER), BF),
    wo=((INNER, D), BF),
    ups=((D, SLICE), BF),
    downs=((SLICE, D), BF),
    xj=((2, ROWS, D), BF),
    xt=((D, 2 * ROWS), BF),
    kv=((2, ROWS, 2 * INNER), BF),
    qg=((4, 32, INNER), BF),
    qm=((8, 128, 128), BF),
    st=((8, ROWS, 128), F32),
    o_send=((4, 32, INNER), BF),
    o_all=((4, 32, INNER), BF),
    stats=((4, 16, 128), F32),
    sct=((128, 128), F32),
    lt=((8, 128), F32),
    attg=((2, 4, 32, INNER), BF),
    hid=((2, 4, 32, D), F32),
    nf=((256, D), BF),
    cott=((D, 256), BF),
    dact=((256, SLICE), F32),
    act=((2, 128, SLICE), BF),
    dup=((2, 128, SLICE), BF),
    dn_s=((128, D), BF),
    dn_r=((128, D), BF),
    dn_f=((4, 32, D), F32),
    dn_x=((4, 32, D), BF),
    dn_xr=((3, 32, D), BF),
    mx_s=((128, D), BF),
    mx_r=((128, D), BF),
    mx_f=((4, 32, D), F32),
    mx_x=((4, 32, D), BF),
    mx_xr=((3, 32, D), BF),
    dhid=((32, D), F32),
    dag=((4, 32, INNER), BF),
    dkv=((2, ROWS, 2 * INNER), BF),
    dq_send=((4, 32, INNER), BF),
    dq_all=((4, 32, INNER), BF),
    dj=((2, ROWS, D), F32),
    gm=((2, MED, D), F32),
    vec=((8, D), F32),
    vec_r1=((8, D), F32),
    vec_rx=((3, 8, D), F32),
    vec_ry=((3, 8, D), F32),
    vec_rz=((3, 8, D), F32),
    vec_a=((8, D), F32),
    vec_b=((8, D), F32),
    vec_c=((8, D), F32),
    gu=((4, 4, 64, SLICE), BF),
    gu_r1=((3, 4, 64, SLICE), BF),
    gu_s=((4, 64, SLICE), BF),
    gu_r2=((3, 64, SLICE), BF),
    gu_f=((8, 8, SLICE), F32),
    upo=((8, FF), F32),
    gd=((4, 4, 64, SLICE), BF),
    gd_r1=((3, 4, 64, SLICE), BF),
    gd_s=((4, 64, SLICE), BF),
    gd_r2=((3, 64, SLICE), BF),
    gd_f=((8, 8, SLICE), F32),
    dno=((8, FF), F32),
    g_send=((D, INNER), BF),
    g_recv=((D, INNER), BF),
    g_own=((D, INNER), F32),
    w5=((4, 4, 4, 16, INNER), BF),
    gqo=((2, D, INNER), BF),
    gqo_r=((D, INNER), BF),
    v5=((4, 4, 4, 16, INNER), BF),
    fin1=((2, 8, INNER), F32),
    fin1_r=((8, INNER), F32),
    fin2=((2, 8, INNER), F32),
    fin2_r=((8, INNER), F32),
)
CHAINS = ((0, 256, ("x", "y", "z")), (256, 128, ("y", "z", "x")), (384, 128, ("z", "x", "y")))
AXIS_DIM = {"y": 0, "z": 1, "x": 2}
for _w in ("w", "v"):
    for _i, (_, _n, _) in enumerate(CHAINS):
        SCRATCH[f"{_w}r1_{_i}"] = ((3, 4, 4, 16, _n), BF)
        SCRATCH[f"{_w}s1_{_i}"] = ((4, 4, 16, _n), BF)
        SCRATCH[f"{_w}r2_{_i}"] = ((3, 4, 16, _n), BF)
        SCRATCH[f"{_w}s2_{_i}"] = ((4, 16, _n), BF)
        SCRATCH[f"{_w}r3_{_i}"] = ((3, 16, _n), BF)
N_IN = 16
N_OUT = 9


class Refs:
    def __init__(self, names, refs):
        self.__dict__.update(zip(names, refs))

    def __getitem__(self, name):
        return self.__dict__[name]


def layer_kernel(*refs):
    (media_h, lat_h, cot_h, counts, mg, ms, lg, ls, fg, fs, wq_h, wk_h, wv_h, wo_h, up_h, down_h) = refs[:N_IN]
    (mixed_o, gmedia_o, glat_o, vec_o, gqkv_o, go_o, gup_o, gdown_o, _unused_o) = refs[N_IN : N_IN + N_OUT]
    r = Refs(SCRATCH, refs[N_IN + N_OUT : N_IN + N_OUT + len(SCRATCH)])
    ssem, rsem, lsem = refs[N_IN + N_OUT + len(SCRATCH) :]

    dp = lax.axis_index("dp")
    pb = lax.axis_index("pb")
    y = dp // 8
    z = (dp // 2) % 4
    xh = dp % 2
    xl = pb // 2
    c = pb % 2
    x = xh * 2 + xl
    g = x * 2 + c
    s = pb
    oc = 1 - c
    me = {"x": x, "y": y, "z": z}

    def dev(yy, zz, xx, cc):
        return ((yy * 4 + zz) * 2 + xx // 2, (xx % 2) * 2 + cc)

    def along(axis, d):
        at = dict(me)
        at[axis] = (me[axis] + d) % 4
        return dev(at["y"], at["z"], at["x"], c)

    def sub(k):
        xl2 = (xl + (k >> 1)) % 2
        c2 = (c + (k & 1)) % 2
        return dev(y, z, xh * 2 + xl2, c2), xl2 * 2 + c2

    def grp(k):
        x2 = (x + (k >> 1)) % 4
        c2 = (c + (k & 1)) % 2
        return dev(y, z, x2, c2), x2 * 2 + c2

    partner = dev(y, z, x, oc)
    counter = itertools.count()
    pending = []

    def send(src, dst, target):
        i = next(counter)
        copy = pltpu.make_async_remote_copy(
            src_ref=src,
            dst_ref=dst,
            send_sem=ssem.at[i],
            recv_sem=rsem.at[i],
            device_id=target,
            device_id_type=MESH,
        )
        copy.start()
        pending.append(copy)
        return copy

    local_counter = itertools.count()

    def fetch(src, dst):
        copy = pltpu.make_async_copy(src, dst, lsem.at[next(local_counter)])
        copy.start()
        return copy

    barrier = pltpu.get_barrier_semaphore()
    greeted = [grp(k)[0] for k in range(1, 8)]
    greeted += [along(a, d) for a in ("y", "z") for d in (1, 2, 3)]
    for target in greeted:
        pl.semaphore_signal(barrier, inc=1, device_id=target, device_id_type=MESH)

    f_lat = fetch(lat_h, r.lc.at[c, x, pl.ds(0, 2)])
    f_wq = fetch(wq_h, r.wq)
    f_cot = fetch(cot_h, r.lc.at[c, x, pl.ds(2, 2)])
    f_media = fetch(media_h, r.media)
    f_wk = fetch(wk_h, r.wk)
    f_wv = fetch(wv_h, r.wv)
    f_wo = fetch(wo_h, r.wo)
    f_down = fetch(down_h.at[pl.ds(g * SLICE, SLICE), :], r.downs)
    f_up = fetch(up_h.at[:, pl.ds(g * SLICE, SLICE)], r.ups)

    f_lat.wait()
    lat_own = r.lc[c, x, pl.ds(0, 2)].astype(F32).reshape(32, D)
    xhat, _ = normalised(lat_own)
    nl = (xhat * lg[...] + ls[...]).astype(BF)
    r.xj[0, pl.ds(MED, LATD), :] = nl[:16]
    r.xj[1, pl.ds(MED, LATD), :] = nl[16:]
    f_wq.wait()
    r.qg[s] = (mm(nl, r.wq[...]) * SCALE).astype(BF)

    f_cot.wait()
    pl.semaphore_wait(barrier, len(greeted))
    q_copies = [send(r.qg.at[s], r.qg.at[s], sub(k)[0]) for k in (1, 2, 3)]
    lc_copies = [send(r.lc.at[c, x], r.lc.at[c, x], along("x", d)) for d in (1, 2, 3)]

    f_media.wait()
    for i in range(2):

        def norm_rows(t, carry, i=i):
            at = pl.ds(pl.multiple_of(t * 16, 16), 16)
            xh_, _ = normalised(r.media[i, at, :].astype(F32))
            r.xj[i, at, :] = (xh_ * mg[...] + ms[...]).astype(BF)
            return carry

        lax.fori_loop(0, MED // 16, norm_rows, 0, unroll=3)
    f_wk.wait()
    f_wv.wait()
    xj = r.xj[...].reshape(2 * ROWS, D)
    for n in range(0, INNER, 256):
        r.kv[:, :, n : n + 256] = mm(xj, r.wk[:, n : n + 256]).astype(BF).reshape(2, ROWS, 256)
        r.kv[:, :, INNER + n : INNER + n + 256] = (
            mm(xj, r.wv[:, n : n + 256]).astype(BF).reshape(2, ROWS, 256)
        )
    r.xt[...] = jnp.transpose(xj)

    for copy in q_copies:
        copy.wait_recv()
    low = lax.broadcasted_iota(jnp.int32, (64, 128), 1) < 64
    row = lax.broadcasted_iota(jnp.int32, (ROWS, 128), 0)

    def by_head(v):
        v = v.astype(F32)
        return jnp.concatenate([jnp.where(low, v, 0.0), jnp.where(low, 0.0, v)], axis=0).astype(BF)

    def merged(v):
        return jnp.where(low, v[:64], v[64:])

    tops, sums = [], []
    for i in range(2):
        q_i = jnp.concatenate([r.qg[k, pl.ds(i * 16, 16), :] for k in range(4)], axis=0)
        valid = (row >= MED) | (row + pb * MED < counts[i])
        for hp in range(4):
            ih = i * 4 + hp
            cols = slice(hp * 128, hp * 128 + 128)
            qm = by_head(q_i[:, cols])
            r.qm[ih] = qm
            st = jnp.where(valid, mm_nt(r.kv[i, :, cols], qm), NEG_FILL)
            r.st[ih] = st
            top = jnp.max(st, axis=0, keepdims=True)
            p = jnp.exp(st - top)
            tops.append(top)
            sums.append(jnp.sum(p, axis=0, keepdims=True))
            o = merged(mm_tn(p.astype(BF), r.kv[i, :, INNER + hp * 128 : INNER + hp * 128 + 128])).astype(BF)
            for k in range(4):
                r.o_send[k, pl.ds(i * 16, 16), cols] = o[k * 16 : k * 16 + 16]
    r.stats[s] = jnp.concatenate(tops + sums, axis=0)
    st_copies = [send(r.stats.at[s], r.stats.at[s], sub(k)[0]) for k in (1, 2, 3)]
    o_copies = []
    for k in (1, 2, 3):
        target, s2 = sub(k)
        o_copies.append(send(r.o_send.at[s2], r.o_all.at[s], target))
    r.o_all[s] = r.o_send[s]

    for copy in lc_copies:
        copy.wait_recv()
    lc_half = send(r.lc.at[c], r.lc.at[c], partner)
    lc_half.wait_recv()
    f_down.wait()
    cot_all = r.lc[:, :, pl.ds(2, 2)].reshape(256, D)
    r.dact[...] = mm_nt(cot_all, r.downs[...])
    r.cott[...] = jnp.transpose(cot_all)

    for copy in st_copies + o_copies:
        copy.wait_recv()
    stats = r.stats[...]
    peak = jnp.max(stats[:, :8], axis=0)
    weight = jnp.exp(stats[:, :8] - peak[None])
    total = jnp.sum(weight * stats[:, 8:], axis=0)
    r.lt[...] = peak + jnp.log(total)
    share = (weight / total[None]).reshape(32, 128)
    r.sct[...] = jnp.transpose(jnp.concatenate([share, jnp.zeros((96, 128), F32)], axis=0))
    low16 = low[:16]
    sc0 = r.sct[pl.ds(pl.multiple_of(s * 16, 16), 16), :]
    sc1 = r.sct[pl.ds(pl.multiple_of(64 + s * 16, 16), 16), :]
    att_rows = []
    for i in range(2):
        pairs = []
        for hp in range(4):
            ih = i * 4 + hp
            acc = jnp.zeros((16, 128), F32)
            for k in range(4):
                col = k * 8 + ih
                factor = jnp.where(low16, sc0[:, col : col + 1], sc1[:, col : col + 1])
                acc += r.o_all[k, pl.ds(i * 16, 16), hp * 128 : hp * 128 + 128].astype(F32) * factor
            pairs.append(acc)
        att_rows.append(jnp.concatenate(pairs, axis=1))
    att_own = jnp.concatenate(att_rows, axis=0).astype(BF)
    r.attg[c, x] = att_own
    mine = r.attg.at[c, x]
    att_copies = [send(mine, mine, along("x", d)) for d in (1, 2, 3)]
    arrivals = [send(mine, mine, partner)]
    for d, copy in zip((1, 2, 3), att_copies):
        copy.wait_recv()
        part = r.attg.at[c, (x + 4 - d) % 4]
        arrivals.append(send(part, part, partner))

    f_wo.wait()
    f_up.wait()
    for copy in arrivals:
        copy.wait_recv()
    lat_all = r.lc[:, :, pl.ds(0, 2)].reshape(256, D)
    att_all = r.attg[...].reshape(256, INNER)
    for n in range(0, D, 256):
        part = lat_all[:, n : n + 256].astype(F32) + mm(att_all, r.wo[:, n : n + 256])
        r.hid[:, :, :, n : n + 256] = part.reshape(2, 4, 32, 256)

    def norm_ff_rows(t, carry):
        xh_, _ = normalised(r.hid[t // 4, t % 4])
        r.nf[pl.ds(pl.multiple_of(t * 32, 32), 32), :] = (xh_ * fg[...] + fs[...]).astype(BF)
        return carry

    lax.fori_loop(0, 8, norm_ff_rows, 0)
    for n in range(0, SLICE, 256):
        u = mm(r.nf[...], r.ups[:, n : n + 256])
        cdf = 0.5 * (1.0 + lax.erf(u * 0.7071067811865476))
        slope = cdf + u * (jnp.exp(-0.5 * u * u) * 0.3989422804014327)
        r.act[:, :, n : n + 256] = (u * cdf).astype(BF).reshape(2, 128, 256)
        r.dup[:, :, n : n + 256] = (r.dact[:, n : n + 256] * slope).astype(BF).reshape(2, 128, 256)
    r.dn_s[...] = mm_nt(r.dup[oc], r.ups[...]).astype(BF)
    dn_pair = send(r.dn_s, r.dn_r, partner)
    r.dn_f[...] = mm_nt(r.dup[c], r.ups[...]).reshape(4, 32, D)
    act_all = r.act[...].reshape(256, SLICE)
    for n in range(4):
        r.gd[n] = mm(r.cott[n * 256 : n * 256 + 256, :], act_all).astype(BF).reshape(4, 64, SLICE)
    dn_pair.wait_recv()
    dn_sum = r.dn_f[...] + r.dn_r[...].astype(F32).reshape(4, 32, D)
    r.dn_f[...] = dn_sum
    r.dn_x[...] = dn_sum.astype(BF)
    dn_copies = [send(r.dn_x.at[(x + d) % 4], r.dn_xr.at[d - 1], along("x", d)) for d in (1, 2, 3)]
    gd_1 = [send(r.gd.at[:, (z + d) % 4], r.gd_r1.at[d - 1], along("z", d)) for d in (1, 2, 3)]
    dup_all = r.dup[...].reshape(256, SLICE)
    for n in range(4):
        r.gu[n] = mm_tn(r.nf[:, n * 256 : n * 256 + 256], dup_all).astype(BF).reshape(4, 64, SLICE)
    gu_1 = [send(r.gu.at[(y + d) % 4], r.gu_r1.at[d - 1], along("y", d)) for d in (1, 2, 3)]
    r.mx_s[...] = mm(r.act[oc], r.downs[...]).astype(BF)
    mx_pair = send(r.mx_s, r.mx_r, partner)
    r.mx_f[...] = mm(r.act[c], r.downs[...]).reshape(4, 32, D)

    for copy in dn_copies:
        copy.wait_recv()
    dn = r.dn_f[x]
    for k in range(3):
        dn += r.dn_xr[k].astype(F32)
    xhat, rstd = normalised(r.hid[c, x])
    r.vec[pl.ds(4, 1), :] = jnp.sum(dn * xhat, axis=0, keepdims=True)
    r.vec[pl.ds(5, 1), :] = jnp.sum(dn, axis=0, keepdims=True)
    cot_own = r.lc[c, x, pl.ds(2, 2)].astype(F32).reshape(32, D)
    d_hidden = cot_own + ln_back(dn, xhat, rstd, fg[...])
    r.dhid[...] = d_hidden
    branch = d_hidden.astype(BF)
    r.dag[s] = mm_nt(branch, r.wo[...]).astype(BF)
    da_copies = [send(r.dag.at[s], r.dag.at[s], sub(k)[0]) for k in (1, 2, 3)]
    mx_pair.wait_recv()
    mx_sum = r.mx_f[...] + r.mx_r[...].astype(F32).reshape(4, 32, D)
    r.mx_f[...] = mx_sum
    r.mx_x[...] = mx_sum.astype(BF)
    mx_copies = [send(r.mx_x.at[(x + d) % 4], r.mx_xr.at[d - 1], along("x", d)) for d in (1, 2, 3)]
    att_own = r.attg[c, x]
    for n in range(0, D, 256):
        r.gqo[1, pl.ds(n, 256), :] = mm_tn(branch[:, n : n + 256], att_own).astype(BF)

    for copy in da_copies:
        copy.wait_recv()
    deltas = []
    for i in range(2):
        da_i = jnp.concatenate([r.dag[k, pl.ds(i * 16, 16), :] for k in range(4)], axis=0)
        at_i = jnp.concatenate(
            [r.attg[k % 2, xh * 2 + k // 2, pl.ds(i * 16, 16), :] for k in range(4)], axis=0
        )
        prod = da_i.astype(F32) * at_i.astype(F32)
        for hp in range(4):
            both = prod[:, hp * 128 : hp * 128 + 128]
            first = jnp.sum(jnp.where(low, both, 0.0), axis=1, keepdims=True)
            second = jnp.sum(jnp.where(low, 0.0, both), axis=1, keepdims=True)
            deltas.append(jnp.concatenate([first, second], axis=0))
    lane = lax.broadcasted_iota(jnp.int32, (128, 128), 1)
    spread = jnp.zeros((128, 128), F32)
    for ih in range(8):
        spread = jnp.where(lane == ih, deltas[ih], spread)
    r.sct[...] = jnp.transpose(spread)
    for i in range(2):
        da_i = jnp.concatenate([r.dag[k, pl.ds(i * 16, 16), :] for k in range(4)], axis=0)
        for hp in range(4):
            ih = i * 4 + hp
            cols = slice(hp * 128, hp * 128 + 128)
            vcols = slice(INNER + hp * 128, INNER + hp * 128 + 128)
            dam = by_head(da_i[:, cols])
            dpt = mm_nt(r.kv[i, :, vcols], dam)
            pt = jnp.exp(r.st[ih] - r.lt[pl.ds(ih, 1), :])
            dst = (pt * (dpt - r.sct[pl.ds(ih, 1), :])).astype(BF)
            r.dkv[i, :, cols] = mm(dst, r.qm[ih]).astype(BF)
            r.dkv[i, :, vcols] = mm(pt.astype(BF), dam).astype(BF)
            dq = merged(mm_tn(dst, r.kv[i, :, cols])).astype(BF)
            for k in range(4):
                r.dq_send[k, pl.ds(i * 16, 16), cols] = dq[k * 16 : k * 16 + 16]
    dq_copies = []
    for k in (1, 2, 3):
        target, s2 = sub(k)
        dq_copies.append(send(r.dq_send.at[s2], r.dq_all.at[s], target))
    r.dq_all[s] = r.dq_send[s]

    def kv_gradient(n, col):
        d_rows = r.dkv[:, :, pl.ds(pl.multiple_of(col, INNER), INNER)].reshape(2 * ROWS, INNER)
        return mm(r.xt[n * 256 : n * 256 + 256, :], d_rows)

    for n in range(4):
        r.g_send[n * 256 : n * 256 + 256, :] = kv_gradient(n, oc * INNER).astype(BF)
    g_pair = send(r.g_send, r.g_recv, partner)
    for n in range(4):
        r.g_own[n * 256 : n * 256 + 256, :] = kv_gradient(n, c * INNER)

    def index(axes, axis, at):
        return tuple(at if a == axis else slice(None) for a in axes)

    def stage_one(name, ref):
        copies = []
        for i, (start, width, order) in enumerate(CHAINS):
            axis = order[0]
            for d in (1, 2, 3):
                where = index("yzx", axis, (me[axis] + d) % 4)
                src = ref.at[where + (slice(None), pl.ds(start, width))]
                copies.append(send(src, r[f"{name}r1_{i}"].at[d - 1], along(axis, d)))
        return copies

    def stage_two(name, ref, before):
        for copy in before:
            copy.wait_recv()
        copies = []
        for i, (start, width, order) in enumerate(CHAINS):
            axis = order[0]
            where = index("yzx", axis, me[axis])
            part = ref[where + (slice(None), pl.ds(start, width))].astype(F32)
            got = r[f"{name}r1_{i}"]
            for k in range(3):
                part += got[k].astype(F32)
            out = r[f"{name}s1_{i}"]
            out[...] = part.astype(BF)
            left = [a for a in "yzx" if a != axis]
            axis = order[1]
            for d in (1, 2, 3):
                src = out.at[index(left, axis, (me[axis] + d) % 4)]
                copies.append(send(src, r[f"{name}r2_{i}"].at[d - 1], along(axis, d)))
        return copies

    def stage_three(name, before):
        for copy in before:
            copy.wait_recv()
        copies = []
        for i, (start, width, order) in enumerate(CHAINS):
            left = [a for a in "yzx" if a != order[0]]
            part = r[f"{name}s1_{i}"][index(left, order[1], me[order[1]])].astype(F32)
            got = r[f"{name}r2_{i}"]
            for k in range(3):
                part += got[k].astype(F32)
            out = r[f"{name}s2_{i}"]
            out[...] = part.astype(BF)
            axis = order[2]
            for d in (1, 2, 3):
                src = out.at[(me[axis] + d) % 4]
                copies.append(send(src, r[f"{name}r3_{i}"].at[d - 1], along(axis, d)))
        return copies

    def last_stage(name, before, fin, fin_r):
        for copy in before:
            copy.wait_recv()
        for i, (start, width, order) in enumerate(CHAINS):
            part = r[f"{name}s2_{i}"][me[order[2]]].astype(F32)
            got = r[f"{name}r3_{i}"]
            for k in range(3):
                part += got[k].astype(F32)
            fin[:, :, start : start + width] = part.reshape(2, 8, width)
        return send(fin.at[oc], fin_r, partner)

    g_pair.wait_recv()
    for n in range(4):
        at = pl.ds(n * 256, 256)
        both = r.g_own[at, :] + r.g_recv[at, :].astype(F32)
        r.w5[n] = both.astype(BF).reshape(4, 4, 16, INNER)
    w_1 = stage_one("w", r.w5)

    for i in range(2):
        for n in range(0, D, 256):
            r.dj[i, :, n : n + 256] = mm_nt(r.dkv[i, :, :INNER], r.wk[n : n + 256, :]) + mm_nt(
                r.dkv[i, :, INNER:], r.wv[n : n + 256, :]
            )
    zero = jnp.zeros((8, D), F32)
    sums_of = (zero, zero)
    for i in range(2):

        def back_rows(t, carry, i=i):
            gain_sum, shift_sum = carry
            at = pl.ds(pl.multiple_of(t * 16, 16), 16)
            xh_, rs_ = normalised(r.media[i, at, :].astype(F32))
            dn_ = r.dj[i, at, :]
            r.gm[i, at, :] = ln_back(dn_, xh_, rs_, mg[...])
            prod_ = dn_ * xh_
            return gain_sum + (prod_[:8] + prod_[8:]), shift_sum + (dn_[:8] + dn_[8:])

        sums_of = lax.fori_loop(0, MED // 16, back_rows, sums_of)
    gm_out = fetch(r.gm, gmedia_o)
    r.vec[pl.ds(0, 1), :] = jnp.sum(sums_of[0], axis=0, keepdims=True)
    r.vec[pl.ds(1, 1), :] = jnp.sum(sums_of[1], axis=0, keepdims=True)

    for copy in dq_copies:
        copy.wait_recv()
    dq = r.dq_all[0].astype(F32)
    for k in range(1, 4):
        dq += r.dq_all[k].astype(F32)
    dq = dq.astype(BF)
    dj_lat = jnp.concatenate([r.dj[0, pl.ds(MED, LATD), :], r.dj[1, pl.ds(MED, LATD), :]], axis=0)
    dnl = mm_nt(dq, r.wq[...]) * SCALE + dj_lat
    xhat, rstd = normalised(r.lc[c, x, pl.ds(0, 2)].astype(F32).reshape(32, D))
    r.vec[pl.ds(2, 1), :] = jnp.sum(dnl * xhat, axis=0, keepdims=True)
    r.vec[pl.ds(3, 1), :] = jnp.sum(dnl, axis=0, keepdims=True)
    r.vec[pl.ds(6, 2), :] = jnp.zeros((2, D), F32)
    glat_o[...] = (r.dhid[...] + ln_back(dnl, xhat, rstd, lg[...])).reshape(2, 16, D)
    vec_1 = send(r.vec, r.vec_r1, partner)
    nl = jnp.concatenate([r.xj[0, pl.ds(MED, LATD), :], r.xj[1, pl.ds(MED, LATD), :]], axis=0)
    for n in range(0, D, 256):
        r.gqo[0, pl.ds(n, 256), :] = (mm_tn(nl[:, n : n + 256], dq) * SCALE).astype(BF)
    qo_pair = send(r.gqo.at[oc], r.gqo_r, partner)

    for copy in gd_1 + gu_1:
        copy.wait_recv()
    part = r.gd[:, z].astype(F32)
    for k in range(3):
        part += r.gd_r1[k].astype(F32)
    r.gd_s[...] = part.astype(BF)
    gd_2 = [send(r.gd_s.at[(y + d) % 4], r.gd_r2.at[d - 1], along("y", d)) for d in (1, 2, 3)]
    part = r.gu[y].astype(F32)
    for k in range(3):
        part += r.gu_r1[k].astype(F32)
    r.gu_s[...] = part.astype(BF)
    gu_2 = [send(r.gu_s.at[(z + d) % 4], r.gu_r2.at[d - 1], along("z", d)) for d in (1, 2, 3)]

    qo_pair.wait_recv()
    for n in range(4):
        at = pl.ds(n * 256, 256)
        both = r.gqo[c, at, :].astype(F32) + r.gqo_r[at, :].astype(F32)
        r.v5[n] = both.astype(BF).reshape(4, 4, 16, INNER)
    w_2 = stage_two("w", r.w5, w_1)
    v_1 = stage_one("v", r.v5)

    vec_1.wait_recv()
    r.vec_a[...] = r.vec[...] + r.vec_r1[...]
    vec_x = [send(r.vec_a, r.vec_rx.at[d - 1], along("x", d)) for d in (1, 2, 3)]

    for copy in mx_copies:
        copy.wait_recv()
    mixed = r.hid[c, x] + r.mx_f[x]
    for k in range(3):
        mixed += r.mx_xr[k].astype(F32)
    mixed_o[...] = mixed.astype(BF).reshape(2, 16, D)

    w_3 = stage_three("w", w_2)

    def ff_end(r2, own, fin, out, before):
        for copy in before:
            copy.wait_recv()
        part = own.astype(F32)
        for k in range(3):
            part += r2[k].astype(F32)
        fin[...] = part.reshape(8, 8, SLICE)
        copies = []
        cols = pl.ds(pl.multiple_of(g * SLICE, SLICE), SLICE)
        for k in range(1, 8):
            target, g2 = grp(k)
            copies.append(send(fin.at[g2], out.at[:, cols], target))
        out[:, cols] = fin[g]
        return copies

    gd_3 = ff_end(r.gd_r2, r.gd_s[y], r.gd_f, r.dno, gd_2)
    gu_3 = ff_end(r.gu_r2, r.gu_s[z], r.gu_f, r.upo, gu_2)

    for copy in vec_x:
        copy.wait_recv()
    r.vec_b[...] = r.vec_a[...] + r.vec_rx[0] + r.vec_rx[1] + r.vec_rx[2]
    vec_y = [send(r.vec_b, r.vec_ry.at[d - 1], along("y", d)) for d in (1, 2, 3)]
    w_4 = last_stage("w", w_3, r.fin1, r.fin1_r)
    v_2 = stage_two("v", r.v5, v_1)
    for copy in vec_y:
        copy.wait_recv()
    r.vec_c[...] = r.vec_b[...] + r.vec_ry[0] + r.vec_ry[1] + r.vec_ry[2]
    vec_z = [send(r.vec_c, r.vec_rz.at[d - 1], along("z", d)) for d in (1, 2, 3)]
    v_3 = stage_three("v", v_2)
    for copy in vec_z:
        copy.wait_recv()
    vec_o[...] = r.vec_c[...] + r.vec_rz[0] + r.vec_rz[1] + r.vec_rz[2]
    v_4 = last_stage("v", v_3, r.fin2, r.fin2_r)
    for copy in gd_3 + gu_3:
        copy.wait_recv()
    gup_o[...] = r.upo[...]
    gdown_o[...] = r.dno[...]
    w_4.wait_recv()
    first = c == 0
    gqkv_o[1] = jnp.where(first, r.fin1[c], r.fin1_r[...])
    gqkv_o[2] = jnp.where(first, r.fin1_r[...], r.fin1[c])
    v_4.wait_recv()
    gqkv_o[0] = jnp.where(first, r.fin2[c], r.fin2_r[...])
    go_o[...] = jnp.where(first, r.fin2_r[...], r.fin2[c])
    _unused_o[...] = jnp.zeros((8, 128), F32)
    for copy in pending:
        copy.wait_send()
    gm_out.wait()


def per_device(*args):
    args = list(args)
    for i in range(3, 9):
        args[i] = args[i].reshape(1, D)
    hbm = pl.BlockSpec(memory_space=pl.ANY)
    vmem = pl.BlockSpec(memory_space=pltpu.VMEM)
    smem = pl.BlockSpec(memory_space=pltpu.SMEM)
    order = [0, 1, 15, 2, 3, 4, 5, 6, 7, 8, 9, 10, 11, 12, 13, 14]
    outs = pl.pallas_call(
        layer_kernel,
        out_shape=(
            jax.ShapeDtypeStruct((2, 16, D), BF),
            jax.ShapeDtypeStruct((2, MED, D), F32),
            jax.ShapeDtypeStruct((2, 16, D), F32),
            jax.ShapeDtypeStruct((8, D), F32),
            jax.ShapeDtypeStruct((3, 8, INNER), F32),
            jax.ShapeDtypeStruct((8, INNER), F32),
            jax.ShapeDtypeStruct((8, FF), F32),
            jax.ShapeDtypeStruct((8, FF), F32),
            jax.ShapeDtypeStruct((8, 128), F32),
        ),
        in_specs=[hbm, hbm, hbm, smem] + [vmem] * 6 + [hbm] * 6,
        out_specs=(vmem, hbm) + (vmem,) * 7,
        scratch_shapes=[pltpu.VMEM(shape, dtype) for shape, dtype in SCRATCH.values()]
        + [
            pltpu.SemaphoreType.DMA((N_SEMS,)),
            pltpu.SemaphoreType.DMA((N_SEMS,)),
            pltpu.SemaphoreType.DMA((16,)),
        ],
        compiler_params=pltpu.CompilerParams(
            collective_id=0, has_side_effects=True, vmem_limit_bytes=56 * 2**20
        ),
    )(*[args[i] for i in order])
    mixed, gmedia, glat, vec, gqkv, go, gup, gdown, _ = outs
    flat = lax.axis_index("dp") * 4 + lax.axis_index("pb")
    mine = lax.dynamic_slice(vec, (0, flat * 8), (8, 8))
    return (
        mixed,
        gmedia,
        glat,
        mine[0],
        mine[1],
        mine[2],
        mine[3],
        mine[4],
        mine[5],
        gqkv[0],
        gqkv[1],
        gqkv[2],
        go.T,
        gup,
        gdown.T,
    )


def solution(mesh):
    tokens = P("dp", "pb", None)
    return jax.shard_map(
        per_device,
        mesh=mesh,
        in_specs=(tokens, tokens, P("dp")) + (P(),) * 12 + (tokens,),
        out_specs=(tokens, tokens, tokens)
        + (P(("dp", "pb")),) * 6
        + (P(("dp", "pb"), None),) * 3
        + (P(None, ("dp", "pb")), P(("dp", "pb"), None), P(None, ("dp", "pb"))),
        check_vma=False,
    )
```

```python
import functools
import itertools

import jax
import jax.numpy as jnp
from jax import lax
from jax.experimental import pallas as pl
from jax.experimental.pallas import tpu as pltpu
from jax.sharding import PartitionSpec as P

MESH = pl.DeviceIdType.MESH
BF = jnp.bfloat16
F32 = jnp.float32
D = 1024
INNER = 512
FF = 4096
MED = 144
LATD = 16
ROWS = MED + LATD
SLICE = FF // 8
EPSILON = 1e-05
NEG_FILL = -1e30
SCALE = 0.125
N_SEMS = 160


def mm(a, b):
    return jnp.dot(a, b, preferred_element_type=F32)


def mm_nt(a, b):
    return lax.dot_general(a, b, (((1,), (1,)), ((), ())), preferred_element_type=F32)


def mm_tn(a, b):
    return lax.dot_general(a, b, (((0,), (0,)), ((), ())), preferred_element_type=F32)


def normalised(v):
    cen = v - jnp.mean(v, axis=-1, keepdims=True)
    rstd = lax.rsqrt(jnp.mean(cen * cen, axis=-1, keepdims=True) + EPSILON)
    return cen * rstd, rstd


def ln_back(dn, xhat, rstd, gain):
    dx = dn * gain
    return rstd * (
        dx - jnp.mean(dx, axis=-1, keepdims=True) - xhat * jnp.mean(dx * xhat, axis=-1, keepdims=True)
    )


SCRATCH = dict(
    media=((2, MED, D), BF),
    mxhat=((2, MED, D), F32),
    mrstd=((2, MED, 128), F32),
    lc=((2, 4, 4, LATD, D), BF),
    wq=((D, INNER), BF),
    wk=((D, INNER), BF),
    wv=((D, INNER), BF),
    wo=((INNER, D), BF),
    ups=((D, SLICE), BF),
    downs=((SLICE, D), BF),
    xj=((2, ROWS, D), BF),
    xt=((D, 2 * ROWS), BF),
    kv=((2, ROWS, 2 * INNER), BF),
    qg=((4, 32, INNER), BF),
    qm=((8, 128, 128), BF),
    st=((8, ROWS, 128), F32),
    o_send=((4, 32, INNER), BF),
    o_all=((4, 32, INNER), BF),
    stats=((4, 16, 128), F32),
    sct=((128, 128), F32),
    lt=((8, 128), F32),
    attg=((2, 4, 32, INNER), BF),
    hid=((2, 4, 32, D), F32),
    nf=((2, 128, D), BF),
    cott=((D, 256), BF),
    dact=((2, 128, SLICE), F32),
    act=((2, 128, SLICE), BF),
    dup=((2, 128, SLICE), BF),
    nl=((128, D), BF),
    dn_s=((128, D), BF),
    dn_r=((128, D), BF),
    dn_f=((4, 32, D), F32),
    dn_x=((4, 32, D), BF),
    dn_xr=((3, 32, D), BF),
    mx_s=((128, D), BF),
    mx_r=((128, D), BF),
    mx_f=((4, 32, D), F32),
    mx_x=((4, 32, D), BF),
    mx_xr=((3, 32, D), BF),
    hxhat=((32, D), F32),
    hrstd=((32, 128), F32),
    dhid=((32, D), F32),
    dbg=((4, 32, D), BF),
    dag=((4, 32, INNER), BF),
    dkv=((2, ROWS, 2 * INNER), BF),
    dq_send=((2, 2, 32, INNER), BF),
    dq_all=((4, 32, INNER), BF),
    dq_part=((2, 4, 2, 32, 128), BF),
    dj=((2, ROWS, D), F32),
    gm=((2, MED, D), F32),
    vec=((8, D), F32),
    vec_r=((8, D), F32),
    vec_a=((4, 8, 256), F32),
    vec_y=((3, 8, 256), F32),
    vec_b=((8, 256), F32),
    vec_z=((3, 8, 256), F32),
    vec_c=((8, 256), F32),
    vec_x=((3, 8, 256), F32),
    gu=((4, 4, 64, SLICE), BF),
    gu_r1=((3, 4, 64, SLICE), BF),
    gu_s=((4, 64, SLICE), BF),
    gu_r2=((3, 64, SLICE), BF),
    gd=((4, 4, 64, SLICE), BF),
    gd_r1=((3, 4, 64, SLICE), BF),
    gd_s=((4, 64, SLICE), BF),
    gd_r2=((3, 64, SLICE), BF),
    gff=((8, 2, 8, SLICE), F32),
    ffo=((2, 8, FF), F32),
    g_send=((2, D, 256), BF),
    g_recv=((2, D, 256), BF),
    g_own=((D, INNER), F32),
    fin=((2, 8, INNER), F32),
    fin_r=((8, INNER), F32),
    qo=((2, D, 128), BF),
    qo_r=((D, 128), BF),
    qo_w=((4, 4, 64, 128), BF),
    qo_r1=((3, 4, 64, 128), BF),
    qo_s=((4, 64, 128), BF),
    qo_r2=((3, 64, 128), BF),
    qo_f=((8, 8, 128), F32),
    qoo=((2, 8, INNER), F32),
)
CHAINS = ((0, 256, ("x", "y", "z")), (256, 128, ("y", "z", "x")), (384, 128, ("z", "x", "y")))
for _i, (_, _n, _) in enumerate(CHAINS):
    SCRATCH[f"w_{_i}"] = ((4, 4, 4, 16, _n), BF)
    SCRATCH[f"r1_{_i}"] = ((3, 4, 4, 16, _n), BF)
    SCRATCH[f"s1_{_i}"] = ((4, 4, 16, _n), BF)
    SCRATCH[f"r2_{_i}"] = ((3, 4, 16, _n), BF)
    SCRATCH[f"s2_{_i}"] = ((4, 16, _n), BF)
    SCRATCH[f"r3_{_i}"] = ((3, 16, _n), BF)
N_IN = 16
N_OUT = 9


class Refs:
    def __init__(self, names, refs):
        self.__dict__.update(zip(names, refs))

    def __getitem__(self, name):
        return self.__dict__[name]


def layer_kernel(*refs):
    (media_h, lat_h, cot_h, counts, mg, ms, lg, ls, fg, fs, wq_h, wk_h, wv_h, wo_h, up_h, down_h) = refs[:N_IN]
    (mixed_o, gmedia_o, glat_o, vec_o, gk_o, gv_o, gqo_o, gup_o, gdown_o) = refs[N_IN : N_IN + N_OUT]
    r = Refs(SCRATCH, refs[N_IN + N_OUT : N_IN + N_OUT + len(SCRATCH)])
    ssem, rsem, lsem = refs[N_IN + N_OUT + len(SCRATCH) :]

    dp = lax.axis_index("dp")
    pb = lax.axis_index("pb")
    y = dp // 8
    z = (dp // 2) % 4
    xh = dp % 2
    xl = pb // 2
    c = pb % 2
    x = xh * 2 + xl
    g = x * 2 + c
    s = pb
    oc = 1 - c
    me = {"x": x, "y": y, "z": z}

    def dev(yy, zz, xx, cc):
        return ((yy * 4 + zz) * 2 + xx // 2, (xx % 2) * 2 + cc)

    def along(axis, d):
        at = dict(me)
        at[axis] = (me[axis] + d) % 4
        return dev(at["y"], at["z"], at["x"], c)

    def sub(k):
        xl2 = (xl + (k >> 1)) % 2
        c2 = (c + (k & 1)) % 2
        return dev(y, z, xh * 2 + xl2, c2), xl2 * 2 + c2

    def grp(k):
        x2 = (x + (k >> 1)) % 4
        c2 = (c + (k & 1)) % 2
        return dev(y, z, x2, c2), x2 * 2 + c2

    partner = dev(y, z, x, oc)
    counter = itertools.count()
    pending = []

    def send(src, dst, target):
        i = next(counter)
        copy = pltpu.make_async_remote_copy(
            src_ref=src,
            dst_ref=dst,
            send_sem=ssem.at[i],
            recv_sem=rsem.at[i],
            device_id=target,
            device_id_type=MESH,
        )
        copy.start()
        pending.append(copy)
        return copy

    local_counter = itertools.count()

    def fetch(src, dst):
        copy = pltpu.make_async_copy(src, dst, lsem.at[next(local_counter)])
        copy.start()
        return copy

    barrier = pltpu.get_barrier_semaphore()
    greeted = [grp(k)[0] for k in range(1, 8)]
    greeted += [along(a, d) for a in ("y", "z") for d in (1, 2, 3)]
    for target in greeted:
        pl.semaphore_signal(barrier, inc=1, device_id=target, device_id_type=MESH)

    f_lat = fetch(lat_h, r.lc.at[c, x, pl.ds(0, 2)])
    f_wq = fetch(wq_h, r.wq)
    f_cot = fetch(cot_h, r.lc.at[c, x, pl.ds(2, 2)])
    f_media = fetch(media_h, r.media)
    f_wk = fetch(wk_h, r.wk)
    f_wv = fetch(wv_h, r.wv)
    f_wo = fetch(wo_h, r.wo)
    f_down = fetch(down_h.at[pl.ds(g * SLICE, SLICE), :], r.downs)
    f_up = fetch(up_h.at[:, pl.ds(g * SLICE, SLICE)], r.ups)

    f_lat.wait()
    lat_own = r.lc[c, x, pl.ds(0, 2)].astype(F32).reshape(32, D)
    xhat, _ = normalised(lat_own)
    nl = (xhat * lg[...] + ls[...]).astype(BF)
    r.xj[0, pl.ds(MED, LATD), :] = nl[:16]
    r.xj[1, pl.ds(MED, LATD), :] = nl[16:]
    f_wq.wait()
    r.qg[s] = (mm(nl, r.wq[...]) * SCALE).astype(BF)

    f_cot.wait()
    pl.semaphore_wait(barrier, len(greeted))
    q_copies = [send(r.qg.at[s], r.qg.at[s], sub(k)[0]) for k in (1, 2, 3)]
    lc_copies = [send(r.lc.at[c, x], r.lc.at[c, x], along("x", d)) for d in (1, 2, 3)]

    f_media.wait()
    for i in range(2):

        def norm_rows(t, carry, i=i):
            at = pl.ds(pl.multiple_of(t * 48, 48), 48)
            xh_, rs_ = normalised(r.media[i, at, :].astype(F32))
            r.mxhat[i, at, :] = xh_
            r.mrstd[i, at, :] = jnp.broadcast_to(rs_, (48, 128))
            r.xj[i, at, :] = (xh_ * mg[...] + ms[...]).astype(BF)
            return carry

        lax.fori_loop(0, MED // 48, norm_rows, 0)
    f_wk.wait()
    f_wv.wait()
    xj = r.xj[...].reshape(2 * ROWS, D)
    for n in range(0, INNER, 256):
        r.kv[:, :, n : n + 256] = mm(xj, r.wk[:, n : n + 256]).astype(BF).reshape(2, ROWS, 256)
        r.kv[:, :, INNER + n : INNER + n + 256] = (
            mm(xj, r.wv[:, n : n + 256]).astype(BF).reshape(2, ROWS, 256)
        )
    r.xt[...] = jnp.transpose(xj)

    for copy in q_copies:
        copy.wait_recv()
    low = lax.broadcasted_iota(jnp.int32, (64, 128), 1) < 64
    row = lax.broadcasted_iota(jnp.int32, (ROWS, 128), 0)

    def by_head(v):
        v = v.astype(F32)
        return jnp.concatenate([jnp.where(low, v, 0.0), jnp.where(low, 0.0, v)], axis=0).astype(BF)

    def merged(v):
        return jnp.where(low, v[:64], v[64:])

    tops, sums = [], []
    for i in range(2):
        q_i = jnp.concatenate([r.qg[k, pl.ds(i * 16, 16), :] for k in range(4)], axis=0)
        valid = (row >= MED) | (row + pb * MED < counts[i])
        for hp in range(4):
            ih = i * 4 + hp
            cols = slice(hp * 128, hp * 128 + 128)
            qm = by_head(q_i[:, cols])
            r.qm[ih] = qm
            st = jnp.where(valid, mm_nt(r.kv[i, :, cols], qm), NEG_FILL)
            r.st[ih] = st
            top = jnp.max(st, axis=0, keepdims=True)
            p = jnp.exp(st - top)
            tops.append(top)
            sums.append(jnp.sum(p, axis=0, keepdims=True))
            o = merged(mm_tn(p.astype(BF), r.kv[i, :, INNER + hp * 128 : INNER + hp * 128 + 128])).astype(BF)
            for k in range(4):
                r.o_send[k, pl.ds(i * 16, 16), cols] = o[k * 16 : k * 16 + 16]
    r.stats[s] = jnp.concatenate(tops + sums, axis=0)
    st_copies = [send(r.stats.at[s], r.stats.at[s], sub(k)[0]) for k in (1, 2, 3)]
    o_copies = []
    for k in (1, 2, 3):
        target, s2 = sub(k)
        o_copies.append(send(r.o_send.at[s2], r.o_all.at[s], target))
    r.o_all[s] = r.o_send[s]

    for copy in lc_copies:
        copy.wait_recv()
    lc_half = send(r.lc.at[c], r.lc.at[c], partner)
    lc_half.wait_recv()
    f_down.wait()
    cot_all = r.lc[:, :, pl.ds(2, 2)].reshape(256, D)
    r.dact[...] = mm_nt(cot_all, r.downs[...]).reshape(2, 128, SLICE)
    r.cott[...] = jnp.transpose(cot_all)
    xhat, _ = normalised(r.lc[c, :, pl.ds(0, 2)].astype(F32).reshape(128, D))
    r.nl[...] = (xhat * lg[...] + ls[...]).astype(BF)

    for copy in st_copies + o_copies:
        copy.wait_recv()
    stats = r.stats[...]
    peak = jnp.max(stats[:, :8], axis=0)
    weight = jnp.exp(stats[:, :8] - peak[None])
    total = jnp.sum(weight * stats[:, 8:], axis=0)
    r.lt[...] = peak + jnp.log(total)
    share = (weight / total[None]).reshape(32, 128)
    r.sct[...] = jnp.transpose(jnp.concatenate([share, jnp.zeros((96, 128), F32)], axis=0))
    low16 = low[:16]
    sc0 = r.sct[pl.ds(pl.multiple_of(s * 16, 16), 16), :]
    sc1 = r.sct[pl.ds(pl.multiple_of(64 + s * 16, 16), 16), :]
    att_rows = []
    for i in range(2):
        pairs = []
        for hp in range(4):
            ih = i * 4 + hp
            acc = jnp.zeros((16, 128), F32)
            for k in range(4):
                col = k * 8 + ih
                factor = jnp.where(low16, sc0[:, col : col + 1], sc1[:, col : col + 1])
                acc += r.o_all[k, pl.ds(i * 16, 16), hp * 128 : hp * 128 + 128].astype(F32) * factor
            pairs.append(acc)
        att_rows.append(jnp.concatenate(pairs, axis=1))
    att_own = jnp.concatenate(att_rows, axis=0).astype(BF)
    r.attg[c, x] = att_own
    mine = r.attg.at[c, x]
    att_copies = [send(mine, mine, along("x", d)) for d in (1, 2, 3)]
    arrivals = [send(mine, mine, partner)]
    for d, copy in zip((1, 2, 3), att_copies):
        copy.wait_recv()
        part = r.attg.at[c, (x + 4 - d) % 4]
        arrivals.append(send(part, part, partner))

    f_wo.wait()
    f_up.wait()

    def feed_forward(h):
        lat_h_ = r.lc[h, :, pl.ds(0, 2)].astype(F32).reshape(128, D)
        hidden = lat_h_ + mm(r.attg[h].reshape(128, INNER), r.wo[...])
        r.hid[h] = hidden.reshape(4, 32, D)
        xh_, _ = normalised(hidden)
        nf = (xh_ * fg[...] + fs[...]).astype(BF)
        r.nf[h] = nf
        u = mm(nf, r.ups[...])
        cdf = 0.5 * (1.0 + lax.erf(u * 0.7071067811865476))
        slope = cdf + u * (jnp.exp(-0.5 * u * u) * 0.3989422804014327)
        r.act[h] = (u * cdf).astype(BF)
        dup = (r.dact[h] * slope).astype(BF)
        r.dup[h] = dup
        return mm_nt(dup, r.ups[...])

    r.dn_f[...] = feed_forward(c).reshape(4, 32, D)
    for copy in arrivals:
        copy.wait_recv()
    r.dn_s[...] = feed_forward(oc).astype(BF)
    dn_pair = send(r.dn_s, r.dn_r, partner)
    act_all = r.act[...].reshape(256, SLICE)
    for n in range(4):
        r.gd[n] = mm(r.cott[n * 256 : n * 256 + 256, :], act_all).astype(BF).reshape(4, 64, SLICE)
    xhat, rstd = normalised(r.hid[c, x])
    r.hxhat[...] = xhat
    r.hrstd[...] = jnp.broadcast_to(rstd, (32, 128))
    dn_pair.wait_recv()
    dn_sum = r.dn_f[...] + r.dn_r[...].astype(F32).reshape(4, 32, D)
    r.dn_f[...] = dn_sum
    r.dn_x[...] = dn_sum.astype(BF)
    dn_copies = [send(r.dn_x.at[(x + d) % 4], r.dn_xr.at[d - 1], along("x", d)) for d in (1, 2, 3)]
    gd_1 = [send(r.gd.at[:, (z + d) % 4], r.gd_r1.at[d - 1], along("z", d)) for d in (1, 2, 3)]
    nf_all = r.nf[...].reshape(256, D)
    dup_all = r.dup[...].reshape(256, SLICE)
    for n in range(4):
        r.gu[n] = mm_tn(nf_all[:, n * 256 : n * 256 + 256], dup_all).astype(BF).reshape(4, 64, SLICE)
    gu_1 = [send(r.gu.at[(y + d) % 4], r.gu_r1.at[d - 1], along("y", d)) for d in (1, 2, 3)]
    r.mx_s[...] = mm(r.act[oc], r.downs[...]).astype(BF)
    mx_pair = send(r.mx_s, r.mx_r, partner)
    r.mx_f[...] = mm(r.act[c], r.downs[...]).reshape(4, 32, D)

    for copy in dn_copies:
        copy.wait_recv()
    dn = r.dn_f[x]
    for k in range(3):
        dn += r.dn_xr[k].astype(F32)
    xhat = r.hxhat[...]
    cot_own = r.lc[c, x, pl.ds(2, 2)].astype(F32).reshape(32, D)
    d_hidden = cot_own + ln_back(dn, xhat, r.hrstd[:, :1], fg[...])
    branch = d_hidden.astype(BF)
    r.dag[s] = mm_nt(branch, r.wo[...]).astype(BF)
    da_copies = [send(r.dag.at[s], r.dag.at[s], sub(k)[0]) for k in (1, 2, 3)]
    r.dbg[x] = branch
    db_copies = [send(r.dbg.at[x], r.dbg.at[x], along("x", d)) for d in (1, 2, 3)]
    r.dhid[...] = d_hidden
    r.vec[pl.ds(4, 1), :] = jnp.sum(dn * xhat, axis=0, keepdims=True)
    r.vec[pl.ds(5, 1), :] = jnp.sum(dn, axis=0, keepdims=True)
    r.vec[pl.ds(6, 2), :] = jnp.zeros((2, D), F32)
    mx_pair.wait_recv()
    mx_sum = r.mx_f[...] + r.mx_r[...].astype(F32).reshape(4, 32, D)
    r.mx_f[...] = mx_sum
    r.mx_x[...] = mx_sum.astype(BF)
    mx_copies = [send(r.mx_x.at[(x + d) % 4], r.mx_xr.at[d - 1], along("x", d)) for d in (1, 2, 3)]

    for copy in da_copies:
        copy.wait_recv()
    deltas = []
    for i in range(2):
        da_i = jnp.concatenate([r.dag[k, pl.ds(i * 16, 16), :] for k in range(4)], axis=0)
        at_i = jnp.concatenate(
            [r.attg[k % 2, xh * 2 + k // 2, pl.ds(i * 16, 16), :] for k in range(4)], axis=0
        )
        prod = da_i.astype(F32) * at_i.astype(F32)
        for hp in range(4):
            both = prod[:, hp * 128 : hp * 128 + 128]
            first = jnp.sum(jnp.where(low, both, 0.0), axis=1, keepdims=True)
            second = jnp.sum(jnp.where(low, 0.0, both), axis=1, keepdims=True)
            deltas.append(jnp.concatenate([first, second], axis=0))
    lane = lax.broadcasted_iota(jnp.int32, (128, 128), 1)
    spread = jnp.zeros((128, 128), F32)
    for ih in range(8):
        spread = jnp.where(lane == ih, deltas[ih], spread)
    r.sct[...] = jnp.transpose(spread)
    for i in range(2):
        da_i = jnp.concatenate([r.dag[k, pl.ds(i * 16, 16), :] for k in range(4)], axis=0)
        for hp in range(4):
            ih = i * 4 + hp
            cols = slice(hp * 128, hp * 128 + 128)
            vcols = slice(INNER + hp * 128, INNER + hp * 128 + 128)
            dam = by_head(da_i[:, cols])
            dpt = mm_nt(r.kv[i, :, vcols], dam)
            pt = jnp.exp(r.st[ih] - r.lt[pl.ds(ih, 1), :])
            dst = (pt * (dpt - r.sct[pl.ds(ih, 1), :])).astype(BF)
            r.dkv[i, :, cols] = mm(dst, r.qm[ih]).astype(BF)
            r.dkv[i, :, vcols] = mm(pt.astype(BF), dam).astype(BF)
            dq = merged(mm_tn(dst, r.kv[i, :, cols])).astype(BF)
            for k in range(4):
                r.dq_send[k // 2, k % 2, pl.ds(i * 16, 16), cols] = dq[k * 16 : k * 16 + 16]

    def kv_gradient(n, col, width):
        d_rows = r.dkv[:, :, pl.ds(pl.multiple_of(col, 256), width)].reshape(2 * ROWS, width)
        return mm(r.xt[n * 256 : n * 256 + 256, :], d_rows)

    g_pair = []
    for m in range(2):
        for n in range(4):
            part = kv_gradient(n, oc * INNER + m * 256, 256)
            r.g_send[m, n * 256 : n * 256 + 256, :] = part.astype(BF)
        g_pair.append(send(r.g_send.at[m], r.g_recv.at[m], partner))
    dq_copies = []
    for k in (1, 2, 3):
        target, s2 = sub(k)
        dq_copies.append(send(r.dq_send.at[s2 // 2, s2 % 2], r.dq_all.at[s], target))
    dqp_copies = []
    for k in range(1, 8):
        target, g2 = grp(k)
        src = r.dq_send.at[:, g2 % 2, :, pl.ds(pl.multiple_of(g2 // 2 * 128, 128), 128)]
        dqp_copies.append(send(src, r.dq_part.at[xh, s], target))
    for n in range(4):
        r.g_own[n * 256 : n * 256 + 256, :] = kv_gradient(n, c * INNER, INNER)
    r.dq_all[s] = r.dq_send[xl, c]
    r.dq_part[xh, s] = r.dq_send[:, c, :, pl.ds(pl.multiple_of(x * 128, 128), 128)]

    def index(axes, axis, at):
        return tuple(at if a == axis else slice(None) for a in axes)

    def added(own, got):
        part = own.astype(F32)
        for k in range(3):
            part += got[k].astype(F32)
        return part

    w_1 = []
    for i, (start, width, order) in enumerate(CHAINS):
        if i < 2:
            g_pair[i].wait_recv()
        half = r.g_recv.at[start // 256]
        cols = slice(start % 256, start % 256 + width)
        w = r[f"w_{i}"]
        for n in range(4):
            at = pl.ds(n * 256, 256)
            both = r.g_own[at, start : start + width] + half[at, cols].astype(F32)
            w[n] = both.astype(BF).reshape(4, 4, 16, width)
        axis = order[0]
        for d in (1, 2, 3):
            src = w.at[index("yzx", axis, (me[axis] + d) % 4)]
            w_1.append(send(src, r[f"r1_{i}"].at[d - 1], along(axis, d)))

    def stage_two(before):
        for copy in before:
            copy.wait_recv()
        copies = []
        for i, (start, width, order) in enumerate(CHAINS):
            axis = order[0]
            out = r[f"s1_{i}"]
            out[...] = added(r[f"w_{i}"][index("yzx", axis, me[axis])], r[f"r1_{i}"]).astype(BF)
            left = [a for a in "yzx" if a != axis]
            axis = order[1]
            for d in (1, 2, 3):
                src = out.at[index(left, axis, (me[axis] + d) % 4)]
                copies.append(send(src, r[f"r2_{i}"].at[d - 1], along(axis, d)))
        return copies

    def stage_three(before):
        for copy in before:
            copy.wait_recv()
        copies = []
        for i, (start, width, order) in enumerate(CHAINS):
            left = [a for a in "yzx" if a != order[0]]
            out = r[f"s2_{i}"]
            own = r[f"s1_{i}"][index(left, order[1], me[order[1]])]
            out[...] = added(own, r[f"r2_{i}"]).astype(BF)
            axis = order[2]
            for d in (1, 2, 3):
                src = out.at[(me[axis] + d) % 4]
                copies.append(send(src, r[f"r3_{i}"].at[d - 1], along(axis, d)))
        return copies

    for copy in gd_1 + gu_1:
        copy.wait_recv()
    r.gd_s[...] = added(r.gd[:, z], r.gd_r1).astype(BF)
    gd_2 = [send(r.gd_s.at[(y + d) % 4], r.gd_r2.at[d - 1], along("y", d)) for d in (1, 2, 3)]
    r.gu_s[...] = added(r.gu[y], r.gu_r1).astype(BF)
    gu_2 = [send(r.gu_s.at[(z + d) % 4], r.gu_r2.at[d - 1], along("z", d)) for d in (1, 2, 3)]

    for i in range(2):
        for n in range(0, D, 256):
            r.dj[i, :, n : n + 256] = mm_nt(r.dkv[i, :, :INNER], r.wk[n : n + 256, :]) + mm_nt(
                r.dkv[i, :, INNER:], r.wv[n : n + 256, :]
            )
    zero = jnp.zeros((8, D), F32)
    sums_of = (zero, zero)
    for i in range(2):

        def back_rows(t, carry, i=i):
            gain_sum, shift_sum = carry
            at = pl.ds(pl.multiple_of(t * 48, 48), 48)
            xh_ = r.mxhat[i, at, :]
            dn_ = r.dj[i, at, :]
            r.gm[i, at, :] = ln_back(dn_, xh_, r.mrstd[i, at, :1], mg[...])
            prod_ = dn_ * xh_
            return gain_sum + jnp.sum(prod_.reshape(6, 8, D), axis=0), shift_sum + jnp.sum(
                dn_.reshape(6, 8, D), axis=0
            )

        sums_of = lax.fori_loop(0, MED // 48, back_rows, sums_of)
    gm_out = fetch(r.gm, gmedia_o)
    r.vec[pl.ds(0, 1), :] = jnp.sum(sums_of[0], axis=0, keepdims=True)
    r.vec[pl.ds(1, 1), :] = jnp.sum(sums_of[1], axis=0, keepdims=True)
    for copy in dq_copies:
        copy.wait_recv()
    dq = r.dq_all[0].astype(F32)
    for k in range(1, 4):
        dq += r.dq_all[k].astype(F32)
    dq = dq.astype(BF)
    dj_lat = jnp.concatenate([r.dj[0, pl.ds(MED, LATD), :], r.dj[1, pl.ds(MED, LATD), :]], axis=0)
    dnl = mm_nt(dq, r.wq[...]) * SCALE + dj_lat
    xhat, rstd = normalised(r.lc[c, x, pl.ds(0, 2)].astype(F32).reshape(32, D))
    r.vec[pl.ds(2, 1), :] = jnp.sum(dnl * xhat, axis=0, keepdims=True)
    r.vec[pl.ds(3, 1), :] = jnp.sum(dnl, axis=0, keepdims=True)
    vec_1 = send(r.vec, r.vec_r, partner)
    glat_o[...] = (r.dhid[...] + ln_back(dnl, xhat, rstd, lg[...])).reshape(2, 16, D)

    for copy in db_copies + dqp_copies:
        copy.wait_recv()
    slice_x = pl.ds(pl.multiple_of(x * 128, 128), 128)
    att_x = r.attg[c, :, :, slice_x].reshape(128, 128)
    r.qo[1] = mm_tn(r.dbg[...].reshape(128, D), att_x).astype(BF)
    dq_x = r.dq_part[:, 0].astype(F32)
    for k in range(1, 4):
        dq_x += r.dq_part[:, k].astype(F32)
    r.qo[0] = (mm_tn(r.nl[...], dq_x.astype(BF).reshape(128, 128)) * SCALE).astype(BF)
    qo_pair = send(r.qo.at[oc], r.qo_r, partner)

    vec_1.wait_recv()
    for n in range(4):
        lanes = slice(n * 256, n * 256 + 256)
        r.vec_a[n] = r.vec[:, lanes] + r.vec_r[:, lanes]
    vec_2 = [send(r.vec_a.at[(y + d) % 4], r.vec_y.at[d - 1], along("y", d)) for d in (1, 2, 3)]
    qo_pair.wait_recv()
    r.qo_w[...] = (r.qo[c].astype(F32) + r.qo_r[...].astype(F32)).astype(BF).reshape(4, 4, 64, 128)
    qo_1 = [send(r.qo_w.at[(y + d) % 4], r.qo_r1.at[d - 1], along("y", d)) for d in (1, 2, 3)]

    w_2 = stage_two(w_1)
    for copy in gd_2 + gu_2:
        copy.wait_recv()
    r.gff[:, 0] = added(r.gu_s[z], r.gu_r2).reshape(8, 8, SLICE)
    r.gff[:, 1] = added(r.gd_s[y], r.gd_r2).reshape(8, 8, SLICE)
    cols = pl.ds(pl.multiple_of(g * SLICE, SLICE), SLICE)
    gff_copies = []
    for k in range(1, 8):
        target, g2 = grp(k)
        gff_copies.append(send(r.gff.at[g2], r.ffo.at[:, :, cols], target))
    r.ffo[:, :, cols] = r.gff[g]
    for copy in vec_2:
        copy.wait_recv()
    r.vec_b[...] = added(r.vec_a[y], r.vec_y)
    vec_3 = [send(r.vec_b, r.vec_z.at[d - 1], along("z", d)) for d in (1, 2, 3)]
    for copy in mx_copies:
        copy.wait_recv()
    mixed_o[...] = (r.hid[c, x] + added(r.mx_f[x], r.mx_xr)).astype(BF).reshape(2, 16, D)
    w_3 = stage_three(w_2)
    for copy in qo_1:
        copy.wait_recv()
    r.qo_s[...] = added(r.qo_w[y], r.qo_r1).astype(BF)
    qo_2 = [send(r.qo_s.at[(z + d) % 4], r.qo_r2.at[d - 1], along("z", d)) for d in (1, 2, 3)]
    for copy in vec_3:
        copy.wait_recv()
    r.vec_c[...] = added(r.vec_b[...], r.vec_z)
    vec_4 = [send(r.vec_c, r.vec_x.at[d - 1], along("x", d)) for d in (1, 2, 3)]
    for copy in w_3:
        copy.wait_recv()
    for i, (start, width, order) in enumerate(CHAINS):
        part = added(r[f"s2_{i}"][me[order[2]]], r[f"r3_{i}"])
        r.fin[:, :, start : start + width] = part.reshape(2, 8, width)
    w_4 = send(r.fin.at[oc], r.fin_r, partner)
    for copy in qo_2:
        copy.wait_recv()
    r.qo_f[...] = added(r.qo_s[z], r.qo_r2).reshape(8, 8, 128)
    qo_3 = []
    for k in range(1, 8):
        target, g2 = grp(k)
        qo_3.append(send(r.qo_f.at[g2], r.qoo.at[c, :, slice_x], target))
    r.qoo[c, :, slice_x] = r.qo_f[g]
    w_4.wait_recv()
    first = c == 0
    gk_o[...] = jnp.where(first, r.fin[c], r.fin_r[...])
    gv_o[...] = jnp.where(first, r.fin_r[...], r.fin[c])
    for copy in gff_copies:
        copy.wait_recv()
    gup_o[...] = r.ffo[0]
    gdown_o[...] = r.ffo[1]
    for copy in vec_4:
        copy.wait_recv()
    vec_o[...] = added(r.vec_c[...], r.vec_x)
    for copy in qo_3:
        copy.wait_recv()
    gqo_o[...] = r.qoo[...]
    for copy in pending:
        copy.wait_send()
    gm_out.wait()


def hand_over(mixed, gmedia, glat, vec, gk, gv, gqo, gup, gdown, *refs):
    outs, held, sem_in, sem_out = refs[:15], refs[15:24], refs[24], refs[25]
    plain = (gmedia, glat, gup, gdown, mixed, gqo.at[0], gk, gv, gqo.at[1])
    target = (outs[1], outs[2], outs[13], outs[14], outs[0], outs[9], outs[10], outs[11], outs[12])
    taken = [pltpu.make_async_copy(src, buf, sem_in.at[i]) for i, (src, buf) in enumerate(zip(plain, held))]
    given = [pltpu.make_async_copy(buf, dst, sem_out.at[i]) for i, (buf, dst) in enumerate(zip(held, target))]
    for copy in taken:
        copy.start()
    place = lax.rem(lax.axis_index("dp") * 4 + lax.axis_index("pb"), 32) * 8
    turned = pltpu.roll(vec[...], lax.rem(256 - place, 256), 1)
    for i in range(6):
        outs[3 + i][...] = turned[i : i + 1, :8]
    for copy, on in zip(taken, given):
        copy.wait()
        on.start()
    for on in given:
        on.wait()


def per_device(*args):
    args = list(args)
    for i in range(3, 9):
        args[i] = args[i].reshape(1, D)
    hbm = pl.BlockSpec(memory_space=pl.ANY)
    vmem = pl.BlockSpec(memory_space=pltpu.VMEM)
    smem = pl.BlockSpec(memory_space=pltpu.SMEM)
    far = pl.BlockSpec(memory_space=pltpu.HBM)
    order = [0, 1, 15, 2, 3, 4, 5, 6, 7, 8, 9, 10, 11, 12, 13, 14]
    outs = pl.pallas_call(
        layer_kernel,
        out_shape=(
            jax.ShapeDtypeStruct((2, 16, D), BF),
            jax.ShapeDtypeStruct((2, MED, D), F32),
            jax.ShapeDtypeStruct((2, 16, D), F32),
            jax.ShapeDtypeStruct((8, 256), F32),
            jax.ShapeDtypeStruct((8, INNER), F32),
            jax.ShapeDtypeStruct((8, INNER), F32),
            jax.ShapeDtypeStruct((2, 8, INNER), F32),
            jax.ShapeDtypeStruct((8, FF), F32),
            jax.ShapeDtypeStruct((8, FF), F32),
        ),
        in_specs=[hbm, hbm, hbm, smem] + [vmem] * 6 + [hbm] * 6,
        out_specs=(vmem, hbm) + (vmem,) * 7,
        scratch_shapes=[pltpu.VMEM(shape, dtype) for shape, dtype in SCRATCH.values()]
        + [
            pltpu.SemaphoreType.DMA((N_SEMS,)),
            pltpu.SemaphoreType.DMA((N_SEMS,)),
            pltpu.SemaphoreType.DMA((16,)),
        ],
        compiler_params=pltpu.CompilerParams(
            collective_id=0, has_side_effects=True, vmem_limit_bytes=56 * 2**20
        ),
    )(*[args[i] for i in order])
    shapes = [jax.ShapeDtypeStruct(o.shape, o.dtype) for o in outs]
    mixed, gmedia, glat, _, gk, _, _, gup, _ = shapes
    one = jax.ShapeDtypeStruct((1, 8), F32)
    done = pl.pallas_call(
        hand_over,
        out_shape=(mixed, gmedia, glat) + (one,) * 6 + (gk,) * 4 + (gup,) * 2,
        in_specs=[far] * 3 + [vmem] + [far] * 5,
        out_specs=(far,) * 3 + (vmem,) * 6 + (far,) * 6,
        scratch_shapes=[pltpu.VMEM(o.shape, o.dtype) for o in (gmedia, glat, gup, gup, mixed, gk, gk, gk, gk)]
        + [pltpu.SemaphoreType.DMA((9,))] * 2,
        compiler_params=pltpu.CompilerParams(vmem_limit_bytes=60 * 2**20),
    )(*outs)
    vectors = tuple(v.reshape(8) for v in done[3:9])
    gq, gk, gv, go, gup, gdown = done[9:]
    return tuple(done[:3]) + vectors + (gq, gk, gv, go.T, gup, gdown.T)


def solution(mesh):
    tokens = P("dp", "pb", None)
    return jax.shard_map(
        per_device,
        mesh=mesh,
        in_specs=(tokens, tokens, P("dp")) + (P(),) * 12 + (tokens,),
        out_specs=(tokens, tokens, tokens)
        + (P(("dp", "pb")),) * 6
        + (P(("dp", "pb"), None),) * 3
        + (P(None, ("dp", "pb")), P(("dp", "pb"), None), P(None, ("dp", "pb"))),
        check_vma=False,
    )
```

```python
import functools
import itertools

import jax
import jax.numpy as jnp
from jax import lax
from jax.experimental import pallas as pl
from jax.experimental.pallas import tpu as pltpu
from jax.sharding import PartitionSpec as P

MESH = pl.DeviceIdType.MESH
BF = jnp.bfloat16
F32 = jnp.float32
D = 1024
INNER = 512
FF = 4096
MED = 144
LATD = 16
ROWS = MED + LATD
SLICE = FF // 8
EPSILON = 1e-05
NEG_FILL = -1e30
SCALE = 0.125
N_SEMS = 160


def mm(a, b):
    return jnp.dot(a, b, preferred_element_type=F32)


def mm_nt(a, b):
    return lax.dot_general(a, b, (((1,), (1,)), ((), ())), preferred_element_type=F32)


def mm_tn(a, b):
    return lax.dot_general(a, b, (((0,), (0,)), ((), ())), preferred_element_type=F32)


def normalised(v):
    cen = v - jnp.mean(v, axis=-1, keepdims=True)
    rstd = lax.rsqrt(jnp.mean(cen * cen, axis=-1, keepdims=True) + EPSILON)
    return cen * rstd, rstd


def ln_back(dn, xhat, rstd, gain):
    dx = dn * gain
    return rstd * (
        dx - jnp.mean(dx, axis=-1, keepdims=True) - xhat * jnp.mean(dx * xhat, axis=-1, keepdims=True)
    )


SCRATCH = dict(
    media=((2, MED, D), BF),
    norms=((6, 1, D), F32),
    mxhat=((2, MED, D), F32),
    mrstd=((2, MED, 128), F32),
    lc=((2, 4, 4, LATD, D), BF),
    wq=((D, INNER), BF),
    wk=((D, INNER), BF),
    wv=((D, INNER), BF),
    wo=((INNER, D), BF),
    ups=((D, SLICE), BF),
    downs=((SLICE, D), BF),
    xj=((2, ROWS, D), BF),
    xt=((D, 2 * ROWS), BF),
    kv=((2, ROWS, 2 * INNER), BF),
    qg=((4, 32, INNER), BF),
    qm=((8, 128, 128), BF),
    st=((8, ROWS, 128), F32),
    o_send=((4, 32, INNER), BF),
    o_all=((4, 32, INNER), BF),
    stats=((4, 16, 128), F32),
    sct=((128, 128), F32),
    lt=((8, 128), F32),
    attg=((2, 4, 32, INNER), BF),
    hid=((2, 4, 32, D), F32),
    nf=((2, 128, D), BF),
    cott=((D, 256), BF),
    dact=((2, 128, SLICE), F32),
    act=((2, 128, SLICE), BF),
    dup=((2, 128, SLICE), BF),
    nl=((128, D), BF),
    dn_s=((128, D), BF),
    dn_r=((128, D), BF),
    dn_f=((4, 32, D), F32),
    dn_x=((4, 32, D), BF),
    dn_xr=((3, 32, D), BF),
    mx_s=((128, D), BF),
    mx_r=((128, D), BF),
    mx_f=((4, 32, D), F32),
    mx_x=((4, 32, D), BF),
    mx_xr=((3, 32, D), BF),
    hxhat=((32, D), F32),
    hrstd=((32, 128), F32),
    dhid=((32, D), F32),
    dbg=((4, 32, D), BF),
    dag=((4, 32, INNER), BF),
    dkv=((2, ROWS, 2 * INNER), BF),
    dq_send=((2, 2, 32, INNER), BF),
    dq_all=((4, 32, INNER), BF),
    dq_part=((2, 4, 2, 32, 128), BF),
    dj=((2, ROWS, D), F32),
    vec=((8, D), F32),
    vec_r=((8, D), F32),
    vec_a=((4, 8, 256), F32),
    vec_y=((3, 8, 256), F32),
    vec_b=((8, 256), F32),
    vec_z=((3, 8, 256), F32),
    vec_c=((8, 256), F32),
    vec_x=((3, 8, 256), F32),
    gu=((4, 4, 64, SLICE), BF),
    gu_r1=((3, 4, 64, SLICE), BF),
    gu_s=((4, 64, SLICE), BF),
    gu_r2=((3, 64, SLICE), BF),
    gd=((4, 4, 64, SLICE), BF),
    gd_r1=((3, 4, 64, SLICE), BF),
    gd_s=((4, 64, SLICE), BF),
    gd_r2=((3, 64, SLICE), BF),
    gff=((8, 2, 8, SLICE), F32),
    ffo=((2, 8, FF), F32),
    g_send=((2, D, 256), BF),
    g_recv=((2, D, 256), BF),
    g_own=((D, INNER), F32),
    fin=((2, 8, INNER), F32),
    fin_r=((8, INNER), F32),
    qo=((2, D, 128), BF),
    qo_r=((D, 128), BF),
    qo_w=((4, 4, 64, 128), BF),
    qo_r1=((3, 4, 64, 128), BF),
    qo_s=((4, 64, 128), BF),
    qo_r2=((3, 64, 128), BF),
    qo_f=((8, 8, 128), F32),
    qoo=((2, 8, INNER), F32),
)
CHAINS = ((0, 256, ("x", "y", "z")), (256, 128, ("y", "z", "x")), (384, 128, ("z", "x", "y")))
for _i, (_, _n, _) in enumerate(CHAINS):
    SCRATCH[f"w_{_i}"] = ((4, 4, 4, 16, _n), BF)
    SCRATCH[f"r1_{_i}"] = ((3, 4, 4, 16, _n), BF)
    SCRATCH[f"s1_{_i}"] = ((4, 4, 16, _n), BF)
    SCRATCH[f"r2_{_i}"] = ((3, 4, 16, _n), BF)
    SCRATCH[f"s2_{_i}"] = ((4, 16, _n), BF)
    SCRATCH[f"r3_{_i}"] = ((3, 16, _n), BF)
N_IN = 16
N_OUT = 9


class Refs:
    def __init__(self, names, refs):
        self.__dict__.update(zip(names, refs))

    def __getitem__(self, name):
        return self.__dict__[name]


def layer_kernel(*refs):
    (media_h, lat_h, cot_h, counts_h, mg_h, ms_h, lg_h, ls_h, fg_h, fs_h, wq_h, wk_h, wv_h, wo_h, up_h, down_h) = refs[:N_IN]
    (mixed_o, gmedia_o, glat_o, vec_o, gk_o, gv_o, gqo_o, gup_o, gdown_o) = refs[N_IN : N_IN + N_OUT]
    r = Refs(SCRATCH, refs[N_IN + N_OUT : N_IN + N_OUT + len(SCRATCH)])
    ssem, rsem, lsem, counts = refs[N_IN + N_OUT + len(SCRATCH) :]
    mg, ms, lg, ls, fg, fs = (r.norms.at[k] for k in range(6))

    dp = lax.axis_index("dp")
    pb = lax.axis_index("pb")
    y = dp // 8
    z = (dp // 2) % 4
    xh = dp % 2
    xl = pb // 2
    c = pb % 2
    x = xh * 2 + xl
    g = x * 2 + c
    s = pb
    oc = 1 - c
    me = {"x": x, "y": y, "z": z}

    def dev(yy, zz, xx, cc):
        return ((yy * 4 + zz) * 2 + xx // 2, (xx % 2) * 2 + cc)

    def along(axis, d):
        at = dict(me)
        at[axis] = (me[axis] + d) % 4
        return dev(at["y"], at["z"], at["x"], c)

    def sub(k):
        xl2 = (xl + (k >> 1)) % 2
        c2 = (c + (k & 1)) % 2
        return dev(y, z, xh * 2 + xl2, c2), xl2 * 2 + c2

    def grp(k):
        x2 = (x + (k >> 1)) % 4
        c2 = (c + (k & 1)) % 2
        return dev(y, z, x2, c2), x2 * 2 + c2

    partner = dev(y, z, x, oc)
    counter = itertools.count()
    pending = []

    def send(src, dst, target):
        i = next(counter)
        copy = pltpu.make_async_remote_copy(
            src_ref=src,
            dst_ref=dst,
            send_sem=ssem.at[i],
            recv_sem=rsem.at[i],
            device_id=target,
            device_id_type=MESH,
        )
        copy.start()
        pending.append(copy)
        return copy

    local_counter = itertools.count()

    def fetch(src, dst):
        copy = pltpu.make_async_copy(src, dst, lsem.at[next(local_counter)])
        copy.start()
        return copy

    barrier = pltpu.get_barrier_semaphore()
    greeted = [grp(k)[0] for k in range(1, 8)]
    greeted += [along(a, d) for a in ("y", "z") for d in (1, 2, 3)]
    for target in greeted:
        pl.semaphore_signal(barrier, inc=1, device_id=target, device_id_type=MESH)

    f_lat = fetch(lat_h, r.lc.at[c, x, pl.ds(0, 2)])
    f_lg, f_ls = fetch(lg_h, lg), fetch(ls_h, ls)
    f_wq = fetch(wq_h, r.wq)
    f_cot = fetch(cot_h, r.lc.at[c, x, pl.ds(2, 2)])
    f_mg, f_ms = fetch(mg_h, mg), fetch(ms_h, ms)
    f_media = fetch(media_h, r.media)
    f_wk = fetch(wk_h, r.wk)
    f_wv = fetch(wv_h, r.wv)
    f_counts = fetch(counts_h, counts)
    f_fg, f_fs = fetch(fg_h, fg), fetch(fs_h, fs)
    f_wo = fetch(wo_h, r.wo)
    f_down = fetch(down_h.at[pl.ds(g * SLICE, SLICE), :], r.downs)
    f_up = fetch(up_h.at[:, pl.ds(g * SLICE, SLICE)], r.ups)

    f_lat.wait()
    f_lg.wait()
    f_ls.wait()
    lat_own = r.lc[c, x, pl.ds(0, 2)].astype(F32).reshape(32, D)
    xhat, _ = normalised(lat_own)
    nl = (xhat * lg[...] + ls[...]).astype(BF)
    r.xj[0, pl.ds(MED, LATD), :] = nl[:16]
    r.xj[1, pl.ds(MED, LATD), :] = nl[16:]
    f_wq.wait()
    r.qg[s] = (mm(nl, r.wq[...]) * SCALE).astype(BF)

    f_cot.wait()
    pl.semaphore_wait(barrier, len(greeted))
    q_copies = [send(r.qg.at[s], r.qg.at[s], sub(k)[0]) for k in (1, 2, 3)]
    lc_copies = [send(r.lc.at[c, x], r.lc.at[c, x], along("x", d)) for d in (1, 2, 3)]

    f_media.wait()
    f_mg.wait()
    f_ms.wait()
    for i in range(2):

        def norm_rows(t, carry, i=i):
            at = pl.ds(pl.multiple_of(t * 48, 48), 48)
            xh_, rs_ = normalised(r.media[i, at, :].astype(F32))
            r.mxhat[i, at, :] = xh_
            r.mrstd[i, at, :] = jnp.broadcast_to(rs_, (48, 128))
            r.xj[i, at, :] = (xh_ * mg[...] + ms[...]).astype(BF)
            return carry

        lax.fori_loop(0, MED // 48, norm_rows, 0)
    f_wk.wait()
    f_wv.wait()
    xj = r.xj[...].reshape(2 * ROWS, D)
    for n in range(0, INNER, 256):
        r.kv[:, :, n : n + 256] = mm(xj, r.wk[:, n : n + 256]).astype(BF).reshape(2, ROWS, 256)
        r.kv[:, :, INNER + n : INNER + n + 256] = (
            mm(xj, r.wv[:, n : n + 256]).astype(BF).reshape(2, ROWS, 256)
        )
    r.xt[...] = jnp.transpose(xj)

    for copy in q_copies:
        copy.wait_recv()
    low = lax.broadcasted_iota(jnp.int32, (64, 128), 1) < 64
    row = lax.broadcasted_iota(jnp.int32, (ROWS, 128), 0)

    def by_head(v):
        v = v.astype(F32)
        return jnp.concatenate([jnp.where(low, v, 0.0), jnp.where(low, 0.0, v)], axis=0).astype(BF)

    def merged(v):
        return jnp.where(low, v[:64], v[64:])

    f_counts.wait()
    tops, sums = [], []
    for i in range(2):
        q_i = jnp.concatenate([r.qg[k, pl.ds(i * 16, 16), :] for k in range(4)], axis=0)
        valid = (row >= MED) | (row + pb * MED < counts[i])
        for hp in range(4):
            ih = i * 4 + hp
            cols = slice(hp * 128, hp * 128 + 128)
            qm = by_head(q_i[:, cols])
            r.qm[ih] = qm
            st = jnp.where(valid, mm_nt(r.kv[i, :, cols], qm), NEG_FILL)
            r.st[ih] = st
            top = jnp.max(st, axis=0, keepdims=True)
            p = jnp.exp(st - top)
            tops.append(top)
            sums.append(jnp.sum(p, axis=0, keepdims=True))
            o = merged(mm_tn(p.astype(BF), r.kv[i, :, INNER + hp * 128 : INNER + hp * 128 + 128])).astype(BF)
            for k in range(4):
                r.o_send[k, pl.ds(i * 16, 16), cols] = o[k * 16 : k * 16 + 16]
    r.stats[s] = jnp.concatenate(tops + sums, axis=0)
    st_copies = [send(r.stats.at[s], r.stats.at[s], sub(k)[0]) for k in (1, 2, 3)]
    o_copies = []
    for k in (1, 2, 3):
        target, s2 = sub(k)
        o_copies.append(send(r.o_send.at[s2], r.o_all.at[s], target))
    r.o_all[s] = r.o_send[s]

    for copy in lc_copies:
        copy.wait_recv()
    lc_half = send(r.lc.at[c], r.lc.at[c], partner)
    lc_half.wait_recv()
    f_down.wait()
    cot_all = r.lc[:, :, pl.ds(2, 2)].reshape(256, D)
    r.dact[...] = mm_nt(cot_all, r.downs[...]).reshape(2, 128, SLICE)
    r.cott[...] = jnp.transpose(cot_all)
    xhat, _ = normalised(r.lc[c, :, pl.ds(0, 2)].astype(F32).reshape(128, D))
    r.nl[...] = (xhat * lg[...] + ls[...]).astype(BF)

    for copy in st_copies + o_copies:
        copy.wait_recv()
    stats = r.stats[...]
    peak = jnp.max(stats[:, :8], axis=0)
    weight = jnp.exp(stats[:, :8] - peak[None])
    total = jnp.sum(weight * stats[:, 8:], axis=0)
    r.lt[...] = peak + jnp.log(total)
    share = (weight / total[None]).reshape(32, 128)
    r.sct[...] = jnp.transpose(jnp.concatenate([share, jnp.zeros((96, 128), F32)], axis=0))
    low16 = low[:16]
    sc0 = r.sct[pl.ds(pl.multiple_of(s * 16, 16), 16), :]
    sc1 = r.sct[pl.ds(pl.multiple_of(64 + s * 16, 16), 16), :]
    att_rows = []
    for i in range(2):
        pairs = []
        for hp in range(4):
            ih = i * 4 + hp
            acc = jnp.zeros((16, 128), F32)
            for k in range(4):
                col = k * 8 + ih
                factor = jnp.where(low16, sc0[:, col : col + 1], sc1[:, col : col + 1])
                acc += r.o_all[k, pl.ds(i * 16, 16), hp * 128 : hp * 128 + 128].astype(F32) * factor
            pairs.append(acc)
        att_rows.append(jnp.concatenate(pairs, axis=1))
    att_own = jnp.concatenate(att_rows, axis=0).astype(BF)
    r.attg[c, x] = att_own
    mine = r.attg.at[c, x]
    att_copies = [send(mine, mine, along("x", d)) for d in (1, 2, 3)]
    arrivals = [send(mine, mine, partner)]
    for d, copy in zip((1, 2, 3), att_copies):
        copy.wait_recv()
        part = r.attg.at[c, (x + 4 - d) % 4]
        arrivals.append(send(part, part, partner))

    f_wo.wait()
    f_up.wait()
    f_fg.wait()
    f_fs.wait()

    def feed_forward(h):
        lat_h_ = r.lc[h, :, pl.ds(0, 2)].astype(F32).reshape(128, D)
        hidden = lat_h_ + mm(r.attg[h].reshape(128, INNER), r.wo[...])
        r.hid[h] = hidden.reshape(4, 32, D)
        xh_, _ = normalised(hidden)
        nf = (xh_ * fg[...] + fs[...]).astype(BF)
        r.nf[h] = nf
        u = mm(nf, r.ups[...])
        cdf = 0.5 * (1.0 + lax.erf(u * 0.7071067811865476))
        slope = cdf + u * (jnp.exp(-0.5 * u * u) * 0.3989422804014327)
        r.act[h] = (u * cdf).astype(BF)
        dup = (r.dact[h] * slope).astype(BF)
        r.dup[h] = dup
        return mm_nt(dup, r.ups[...])

    r.dn_f[...] = feed_forward(c).reshape(4, 32, D)
    for copy in arrivals:
        copy.wait_recv()
    r.dn_s[...] = feed_forward(oc).astype(BF)
    dn_pair = send(r.dn_s, r.dn_r, partner)
    act_all = r.act[...].reshape(256, SLICE)
    for n in range(4):
        r.gd[n] = mm(r.cott[n * 256 : n * 256 + 256, :], act_all).astype(BF).reshape(4, 64, SLICE)
    xhat, rstd = normalised(r.hid[c, x])
    r.hxhat[...] = xhat
    r.hrstd[...] = jnp.broadcast_to(rstd, (32, 128))
    dn_pair.wait_recv()
    dn_sum = r.dn_f[...] + r.dn_r[...].astype(F32).reshape(4, 32, D)
    r.dn_f[...] = dn_sum
    r.dn_x[...] = dn_sum.astype(BF)
    dn_copies = [send(r.dn_x.at[(x + d) % 4], r.dn_xr.at[d - 1], along("x", d)) for d in (1, 2, 3)]
    gd_1 = [send(r.gd.at[:, (z + d) % 4], r.gd_r1.at[d - 1], along("z", d)) for d in (1, 2, 3)]
    nf_all = r.nf[...].reshape(256, D)
    dup_all = r.dup[...].reshape(256, SLICE)
    for n in range(4):
        r.gu[n] = mm_tn(nf_all[:, n * 256 : n * 256 + 256], dup_all).astype(BF).reshape(4, 64, SLICE)
    gu_1 = [send(r.gu.at[(y + d) % 4], r.gu_r1.at[d - 1], along("y", d)) for d in (1, 2, 3)]
    r.mx_s[...] = mm(r.act[oc], r.downs[...]).astype(BF)
    mx_pair = send(r.mx_s, r.mx_r, partner)
    r.mx_f[...] = mm(r.act[c], r.downs[...]).reshape(4, 32, D)

    for copy in dn_copies:
        copy.wait_recv()
    dn = r.dn_f[x]
    for k in range(3):
        dn += r.dn_xr[k].astype(F32)
    xhat = r.hxhat[...]
    cot_own = r.lc[c, x, pl.ds(2, 2)].astype(F32).reshape(32, D)
    d_hidden = cot_own + ln_back(dn, xhat, r.hrstd[:, :1], fg[...])
    branch = d_hidden.astype(BF)
    r.dag[s] = mm_nt(branch, r.wo[...]).astype(BF)
    da_copies = [send(r.dag.at[s], r.dag.at[s], sub(k)[0]) for k in (1, 2, 3)]
    r.dbg[x] = branch
    db_copies = [send(r.dbg.at[x], r.dbg.at[x], along("x", d)) for d in (1, 2, 3)]
    r.dhid[...] = d_hidden
    r.vec[pl.ds(4, 1), :] = jnp.sum(dn * xhat, axis=0, keepdims=True)
    r.vec[pl.ds(5, 1), :] = jnp.sum(dn, axis=0, keepdims=True)
    r.vec[pl.ds(6, 2), :] = jnp.zeros((2, D), F32)

    for copy in da_copies:
        copy.wait_recv()
    deltas = []
    for i in range(2):
        da_i = jnp.concatenate([r.dag[k, pl.ds(i * 16, 16), :] for k in range(4)], axis=0)
        at_i = jnp.concatenate(
            [r.attg[k % 2, xh * 2 + k // 2, pl.ds(i * 16, 16), :] for k in range(4)], axis=0
        )
        prod = da_i.astype(F32) * at_i.astype(F32)
        for hp in range(4):
            both = prod[:, hp * 128 : hp * 128 + 128]
            first = jnp.sum(jnp.where(low, both, 0.0), axis=1, keepdims=True)
            second = jnp.sum(jnp.where(low, 0.0, both), axis=1, keepdims=True)
            deltas.append(jnp.concatenate([first, second], axis=0))
    lane = lax.broadcasted_iota(jnp.int32, (128, 128), 1)
    spread = jnp.zeros((128, 128), F32)
    for ih in range(8):
        spread = jnp.where(lane == ih, deltas[ih], spread)
    r.sct[...] = jnp.transpose(spread)
    for i in range(2):
        da_i = jnp.concatenate([r.dag[k, pl.ds(i * 16, 16), :] for k in range(4)], axis=0)
        for hp in range(4):
            ih = i * 4 + hp
            cols = slice(hp * 128, hp * 128 + 128)
            vcols = slice(INNER + hp * 128, INNER + hp * 128 + 128)
            dam = by_head(da_i[:, cols])
            dpt = mm_nt(r.kv[i, :, vcols], dam)
            pt = jnp.exp(r.st[ih] - r.lt[pl.ds(ih, 1), :])
            dst = (pt * (dpt - r.sct[pl.ds(ih, 1), :])).astype(BF)
            r.dkv[i, :, cols] = mm(dst, r.qm[ih]).astype(BF)
            r.dkv[i, :, vcols] = mm(pt.astype(BF), dam).astype(BF)
            dq = merged(mm_tn(dst, r.kv[i, :, cols])).astype(BF)
            for k in range(4):
                r.dq_send[k // 2, k % 2, pl.ds(i * 16, 16), cols] = dq[k * 16 : k * 16 + 16]

    dqp_copies = []
    for k in range(1, 8):
        target, g2 = grp(k)
        src = r.dq_send.at[:, g2 % 2, :, pl.ds(pl.multiple_of(g2 // 2 * 128, 128), 128)]
        dqp_copies.append(send(src, r.dq_part.at[xh, s], target))

    def kv_gradient(n, col, width):
        d_rows = r.dkv[:, :, pl.ds(pl.multiple_of(col, 256), width)].reshape(2 * ROWS, width)
        return mm(r.xt[n * 256 : n * 256 + 256, :], d_rows)

    g_pair = []
    for m in range(2):
        for n in range(4):
            part = kv_gradient(n, oc * INNER + m * 256, 256)
            r.g_send[m, n * 256 : n * 256 + 256, :] = part.astype(BF)
        g_pair.append(send(r.g_send.at[m], r.g_recv.at[m], partner))
    for n in range(4):
        r.g_own[n * 256 : n * 256 + 256, :] = kv_gradient(n, c * INNER, INNER)
    dq_copies = []
    for k in (1, 2, 3):
        target, s2 = sub(k)
        dq_copies.append(send(r.dq_send.at[s2 // 2, s2 % 2], r.dq_all.at[s], target))
    r.dq_all[s] = r.dq_send[xl, c]
    r.dq_part[xh, s] = r.dq_send[:, c, :, pl.ds(pl.multiple_of(x * 128, 128), 128)]

    def index(axes, axis, at):
        return tuple(at if a == axis else slice(None) for a in axes)

    def added(own, got):
        part = own.astype(F32)
        for k in range(3):
            part += got[k].astype(F32)
        return part

    w_1 = []
    for i, (start, width, order) in enumerate(CHAINS):
        if i < 2:
            g_pair[i].wait_recv()
        half = r.g_recv.at[start // 256]
        cols = slice(start % 256, start % 256 + width)
        w = r[f"w_{i}"]
        for n in range(4):
            at = pl.ds(n * 256, 256)
            both = r.g_own[at, start : start + width] + half[at, cols].astype(F32)
            w[n] = both.astype(BF).reshape(4, 4, 16, width)
        axis = order[0]
        for d in (1, 2, 3):
            src = w.at[index("yzx", axis, (me[axis] + d) % 4)]
            w_1.append(send(src, r[f"r1_{i}"].at[d - 1], along(axis, d)))

    def stage_two(before):
        for copy in before:
            copy.wait_recv()
        copies = []
        for i, (start, width, order) in enumerate(CHAINS):
            axis = order[0]
            out = r[f"s1_{i}"]
            out[...] = added(r[f"w_{i}"][index("yzx", axis, me[axis])], r[f"r1_{i}"]).astype(BF)
            left = [a for a in "yzx" if a != axis]
            axis = order[1]
            for d in (1, 2, 3):
                src = out.at[index(left, axis, (me[axis] + d) % 4)]
                copies.append(send(src, r[f"r2_{i}"].at[d - 1], along(axis, d)))
        return copies

    def stage_three(before):
        for copy in before:
            copy.wait_recv()
        copies = []
        for i, (start, width, order) in enumerate(CHAINS):
            left = [a for a in "yzx" if a != order[0]]
            out = r[f"s2_{i}"]
            own = r[f"s1_{i}"][index(left, order[1], me[order[1]])]
            out[...] = added(own, r[f"r2_{i}"]).astype(BF)
            axis = order[2]
            for d in (1, 2, 3):
                src = out.at[(me[axis] + d) % 4]
                copies.append(send(src, r[f"r3_{i}"].at[d - 1], along(axis, d)))
        return copies

    mx_pair.wait_recv()
    mx_sum = r.mx_f[...] + r.mx_r[...].astype(F32).reshape(4, 32, D)
    r.mx_f[...] = mx_sum
    r.mx_x[...] = mx_sum.astype(BF)
    mx_copies = [send(r.mx_x.at[(x + d) % 4], r.mx_xr.at[d - 1], along("x", d)) for d in (1, 2, 3)]


    for copy in db_copies:
        copy.wait_recv()
    slice_x = pl.ds(pl.multiple_of(x * 128, 128), 128)
    att_x = r.attg[c, :, :, slice_x].reshape(128, 128)
    r.qo[1] = mm_tn(r.dbg[...].reshape(128, D), att_x).astype(BF)

    for i in range(2):
        for n in range(0, D, 256):
            r.dj[i, :, n : n + 256] = mm_nt(r.dkv[i, :, :INNER], r.wk[n : n + 256, :]) + mm_nt(
                r.dkv[i, :, INNER:], r.wv[n : n + 256, :]
            )

    for copy in dqp_copies:
        copy.wait_recv()
    dq_x = r.dq_part[:, 0].astype(F32)
    for k in range(1, 4):
        dq_x += r.dq_part[:, k].astype(F32)
    r.qo[0] = (mm_tn(r.nl[...], dq_x.astype(BF).reshape(128, 128)) * SCALE).astype(BF)
    qo_pair = send(r.qo.at[oc], r.qo_r, partner)


    zero = jnp.zeros((8, D), F32)
    sums_of = (zero, zero)
    for i in range(2):

        def back_rows(t, carry, i=i):
            gain_sum, shift_sum = carry
            at = pl.ds(pl.multiple_of(t * 48, 48), 48)
            xh_ = r.mxhat[i, at, :]
            dn_ = r.dj[i, at, :]
            gmedia_o[i, at, :] = ln_back(dn_, xh_, r.mrstd[i, at, :1], mg[...])
            prod_ = dn_ * xh_
            return gain_sum + jnp.sum(prod_.reshape(6, 8, D), axis=0), shift_sum + jnp.sum(
                dn_.reshape(6, 8, D), axis=0
            )

        sums_of = lax.fori_loop(0, MED // 48, back_rows, sums_of)
    r.vec[pl.ds(0, 1), :] = jnp.sum(sums_of[0], axis=0, keepdims=True)
    r.vec[pl.ds(1, 1), :] = jnp.sum(sums_of[1], axis=0, keepdims=True)
    for copy in dq_copies:
        copy.wait_recv()
    dq = r.dq_all[0].astype(F32)
    for k in range(1, 4):
        dq += r.dq_all[k].astype(F32)
    dq = dq.astype(BF)
    dj_lat = jnp.concatenate([r.dj[0, pl.ds(MED, LATD), :], r.dj[1, pl.ds(MED, LATD), :]], axis=0)
    dnl = mm_nt(dq, r.wq[...]) * SCALE + dj_lat
    xhat, rstd = normalised(r.lc[c, x, pl.ds(0, 2)].astype(F32).reshape(32, D))
    r.vec[pl.ds(2, 1), :] = jnp.sum(dnl * xhat, axis=0, keepdims=True)
    r.vec[pl.ds(3, 1), :] = jnp.sum(dnl, axis=0, keepdims=True)
    vec_1 = send(r.vec, r.vec_r, partner)
    glat_o[...] = (r.dhid[...] + ln_back(dnl, xhat, rstd, lg[...])).reshape(2, 16, D)

    qo_pair.wait_recv()
    r.qo_w[...] = (r.qo[c].astype(F32) + r.qo_r[...].astype(F32)).astype(BF).reshape(4, 4, 64, 128)
    qo_1 = [send(r.qo_w.at[(y + d) % 4], r.qo_r1.at[d - 1], along("y", d)) for d in (1, 2, 3)]

    for copy in gd_1 + gu_1:
        copy.wait_recv()
    r.gd_s[...] = added(r.gd[:, z], r.gd_r1).astype(BF)
    gd_2 = [send(r.gd_s.at[(y + d) % 4], r.gd_r2.at[d - 1], along("y", d)) for d in (1, 2, 3)]
    r.gu_s[...] = added(r.gu[y], r.gu_r1).astype(BF)
    gu_2 = [send(r.gu_s.at[(z + d) % 4], r.gu_r2.at[d - 1], along("z", d)) for d in (1, 2, 3)]

    vec_1.wait_recv()
    for n in range(4):
        lanes = slice(n * 256, n * 256 + 256)
        r.vec_a[n] = r.vec[:, lanes] + r.vec_r[:, lanes]
    vec_2 = [send(r.vec_a.at[(y + d) % 4], r.vec_y.at[d - 1], along("y", d)) for d in (1, 2, 3)]

    w_2 = stage_two(w_1)
    for copy in vec_2:
        copy.wait_recv()
    r.vec_b[...] = added(r.vec_a[y], r.vec_y)
    vec_3 = [send(r.vec_b, r.vec_z.at[d - 1], along("z", d)) for d in (1, 2, 3)]
    for copy in qo_1:
        copy.wait_recv()
    r.qo_s[...] = added(r.qo_w[y], r.qo_r1).astype(BF)
    qo_2 = [send(r.qo_s.at[(z + d) % 4], r.qo_r2.at[d - 1], along("z", d)) for d in (1, 2, 3)]
    w_3 = stage_three(w_2)
    for copy in gd_2 + gu_2:
        copy.wait_recv()
    r.gff[:, 0] = added(r.gu_s[z], r.gu_r2).reshape(8, 8, SLICE)
    r.gff[:, 1] = added(r.gd_s[y], r.gd_r2).reshape(8, 8, SLICE)
    cols = pl.ds(pl.multiple_of(g * SLICE, SLICE), SLICE)
    gff_copies = []
    for k in range(1, 8):
        target, g2 = grp(k)
        gff_copies.append(send(r.gff.at[g2], r.ffo.at[:, :, cols], target))
    r.ffo[:, :, cols] = r.gff[g]
    for copy in vec_3:
        copy.wait_recv()
    r.vec_c[...] = added(r.vec_b[...], r.vec_z)
    vec_4 = [send(r.vec_c, r.vec_x.at[d - 1], along("x", d)) for d in (1, 2, 3)]
    for copy in qo_2:
        copy.wait_recv()
    r.qo_f[...] = added(r.qo_s[z], r.qo_r2).reshape(8, 8, 128)
    qo_3 = []
    for k in range(1, 8):
        target, g2 = grp(k)
        qo_3.append(send(r.qo_f.at[g2], r.qoo.at[c, :, slice_x], target))
    r.qoo[c, :, slice_x] = r.qo_f[g]
    for copy in mx_copies:
        copy.wait_recv()
    mixed_o[...] = (r.hid[c, x] + added(r.mx_f[x], r.mx_xr)).astype(BF).reshape(2, 16, D)
    for copy in w_3:
        copy.wait_recv()
    for i, (start, width, order) in enumerate(CHAINS):
        part = added(r[f"s2_{i}"][me[order[2]]], r[f"r3_{i}"])
        r.fin[:, :, start : start + width] = part.reshape(2, 8, width)
    w_4 = send(r.fin.at[oc], r.fin_r, partner)
    for copy in gff_copies:
        copy.wait_recv()
    gup_o[...] = r.ffo[0]
    gdown_o[...] = r.ffo[1]
    for copy in vec_4:
        copy.wait_recv()
    vec_o[...] = added(r.vec_c[...], r.vec_x)
    w_4.wait_recv()
    first = c == 0
    gk_o[...] = jnp.where(first, r.fin[c], r.fin_r[...])
    gv_o[...] = jnp.where(first, r.fin_r[...], r.fin[c])
    for copy in qo_3:
        copy.wait_recv()
    gqo_o[...] = r.qoo[...]
    for copy in pending:
        copy.wait_send()


def hand_over(mixed, gmedia, glat, vec, gk, gv, gqo, gup, gdown, *refs):
    outs, lines, sem = refs[:15], refs[15], refs[16]
    pairs = [(gmedia, outs[1]), (glat, outs[2]), (gup, outs[13]), (gdown, outs[14]), (mixed, outs[0])]
    pairs += [(gqo.at[0], outs[9]), (gk, outs[10]), (gv, outs[11]), (gqo.at[1], outs[12])]
    pairs += [(lines.at[i], outs[3 + i]) for i in range(6)]
    copies = [pltpu.make_async_copy(src, dst, sem.at[i]) for i, (src, dst) in enumerate(pairs)]
    for copy in copies[:9]:
        copy.start()
    place = lax.rem(lax.axis_index("dp") * 4 + lax.axis_index("pb"), 32) * 8
    turned = pltpu.roll(vec[...], lax.rem(256 - place, 256), 1)
    for i in range(6):
        lines[i] = turned[i : i + 1, :8]
    for copy in copies[9:]:
        copy.start()
    for copy in copies:
        copy.wait()


def per_device(*args):
    args = list(args)
    for i in range(3, 9):
        args[i] = args[i].reshape(1, D)
    hbm = pl.BlockSpec(memory_space=pl.ANY)
    vmem = pl.BlockSpec(memory_space=pltpu.VMEM)
    far = pl.BlockSpec(memory_space=pltpu.HBM)
    order = [0, 1, 15, 2, 3, 4, 5, 6, 7, 8, 9, 10, 11, 12, 13, 14]
    outs = pl.pallas_call(
        layer_kernel,
        out_shape=(
            pltpu.VMEM((2, 16, D), BF),
            pltpu.VMEM((2, MED, D), F32),
            pltpu.VMEM((2, 16, D), F32),
            pltpu.VMEM((8, 256), F32),
            pltpu.VMEM((8, INNER), F32),
            pltpu.VMEM((8, INNER), F32),
            pltpu.VMEM((2, 8, INNER), F32),
            pltpu.VMEM((8, FF), F32),
            pltpu.VMEM((8, FF), F32),
        ),
        in_specs=[hbm] * 16,
        out_specs=(vmem,) * 9,
        scratch_shapes=[pltpu.VMEM(shape, dtype) for shape, dtype in SCRATCH.values()]
        + [
            pltpu.SemaphoreType.DMA((N_SEMS,)),
            pltpu.SemaphoreType.DMA((N_SEMS,)),
            pltpu.SemaphoreType.DMA((24,)),
            pltpu.SMEM((2,), jnp.int32),
        ],
        compiler_params=pltpu.CompilerParams(
            collective_id=0, has_side_effects=True, vmem_limit_bytes=52 * 2**20
        ),
    )(*[pltpu.with_memory_space_constraint(args[i], pltpu.HBM) for i in order])
    shapes = [jax.ShapeDtypeStruct(o.shape, o.dtype) for o in outs]
    mixed, gmedia, glat, _, gk, _, _, gup, _ = shapes
    one = jax.ShapeDtypeStruct((1, 8), F32)
    done = pl.pallas_call(
        hand_over,
        out_shape=(mixed, gmedia, glat) + (one,) * 6 + (gk,) * 4 + (gup,) * 2,
        in_specs=[vmem] * 9,
        out_specs=(far,) * 15,
        scratch_shapes=[pltpu.VMEM((6, 1, 8), F32), pltpu.SemaphoreType.DMA((15,))],
        compiler_params=pltpu.CompilerParams(vmem_limit_bytes=52 * 2**20),
    )(*outs)
    vectors = tuple(v.reshape(8) for v in done[3:9])
    gq, gk, gv, go, gup, gdown = done[9:]
    return tuple(done[:3]) + vectors + (gq, gk, gv, go.T, gup, gdown.T)


def solution(mesh):
    tokens = P("dp", "pb", None)
    return jax.shard_map(
        per_device,
        mesh=mesh,
        in_specs=(tokens, tokens, P("dp")) + (P(),) * 12 + (tokens,),
        out_specs=(tokens, tokens, tokens)
        + (P(("dp", "pb")),) * 6
        + (P(("dp", "pb"), None),) * 3
        + (P(None, ("dp", "pb")), P(("dp", "pb"), None), P(None, ("dp", "pb"))),
        check_vma=False,
    )
```

```python
import functools
import itertools

import jax
import jax.numpy as jnp
from jax import lax
from jax.experimental import pallas as pl
from jax.experimental.pallas import tpu as pltpu
from jax.sharding import PartitionSpec as P

MESH = pl.DeviceIdType.MESH
BF = jnp.bfloat16
F32 = jnp.float32
D = 1024
INNER = 512
FF = 4096
MED = 144
LATD = 16
ROWS = MED + LATD
SLICE = FF // 8
EPSILON = 1e-05
NEG_FILL = -1e30
SCALE = 0.125
N_SEMS = 160


def mm(a, b):
    return jnp.dot(a, b, preferred_element_type=F32)


def mm_nt(a, b):
    return lax.dot_general(a, b, (((1,), (1,)), ((), ())), preferred_element_type=F32)


def mm_tn(a, b):
    return lax.dot_general(a, b, (((0,), (0,)), ((), ())), preferred_element_type=F32)


def normalised(v):
    cen = v - jnp.mean(v, axis=-1, keepdims=True)
    rstd = lax.rsqrt(jnp.mean(cen * cen, axis=-1, keepdims=True) + EPSILON)
    return cen * rstd, rstd


def ln_back(dn, xhat, rstd, gain):
    dx = dn * gain
    return rstd * (
        dx - jnp.mean(dx, axis=-1, keepdims=True) - xhat * jnp.mean(dx * xhat, axis=-1, keepdims=True)
    )


SCRATCH = dict(
    media=((2, MED, D), BF),
    norms=((6, 1, D), F32),
    mxhat=((2, MED, D), F32),
    mrstd=((2, MED, 128), F32),
    lc=((2, 4, 4, LATD, D), BF),
    wq=((D, INNER), BF),
    wk=((D, INNER), BF),
    wv=((D, INNER), BF),
    wo=((INNER, D), BF),
    ups=((D, SLICE), BF),
    downs=((SLICE, D), BF),
    xj=((2, ROWS, D), BF),
    xt=((2, D, 2 * ROWS), BF),
    kv=((2, ROWS, 2 * INNER), BF),
    qg=((4, 32, INNER), BF),
    qm=((8, 128, 128), BF),
    st=((8, ROWS, 128), F32),
    o_send=((4, 32, INNER), BF),
    o_all=((4, 32, INNER), BF),
    stats=((4, 16, 128), F32),
    sct=((128, 128), F32),
    lt=((8, 128), F32),
    attg=((2, 4, 32, INNER), BF),
    hid=((2, 4, 32, D), F32),
    nf=((2, 128, D), BF),
    cott=((D, 256), BF),
    dact=((2, 128, SLICE), F32),
    act=((2, 128, SLICE), BF),
    dup=((2, 128, SLICE), BF),
    nls=((2, 2, 32, D), BF),
    dnv=((2, 128, D), F32),
    xhv=((2, 128, D), F32),
    coto=((2, 32, INNER), F32),
    p_s=((128, INNER), BF),
    p_r=((128, INNER), BF),
    p_f=((4, 32, INNER), F32),
    p_x=((4, 32, INNER), BF),
    p_xr=((3, 2, 32, INNER), BF),
    dx_s=((128, D), BF),
    dx_r=((128, D), BF),
    dx_f=((4, 32, D), F32),
    dxa=((2, 4, 32, D), BF),
    dx_xr=((3, 32, D), BF),
    mx_s=((128, D), BF),
    mx_r=((128, D), BF),
    mx_f=((4, 32, D), F32),
    mx_x=((4, 32, D), BF),
    mx_xr=((3, 32, D), BF),
    dhid=((32, D), F32),
    dag=((2, 2, 32, INNER), BF),
    dkv=((2, ROWS, 2 * INNER), BF),
    dq_send=((2, 2, 32, INNER), BF),
    dq_all=((4, 32, INNER), BF),
    dq_r=((2, 2, 32, 256), BF),
    dj=((2, ROWS, D), F32),
    vec=((8, D), F32),
    vec_r=((8, D), F32),
    vec_a=((4, 8, 256), F32),
    vec_y=((3, 8, 256), F32),
    vec_b=((8, 256), F32),
    vec_z=((3, 8, 256), F32),
    vec_c=((8, 256), F32),
    vec_x=((3, 8, 256), F32),
    gu=((4, 4, 64, SLICE), BF),
    gu_r1=((3, 4, 64, SLICE), BF),
    gu_s=((4, 64, SLICE), BF),
    gu_r2=((3, 64, SLICE), BF),
    gd=((4, 4, 64, SLICE), BF),
    gd_r1=((3, 4, 64, SLICE), BF),
    gd_s=((4, 64, SLICE), BF),
    gd_r2=((3, 64, SLICE), BF),
    gff=((8, 2, 8, SLICE), F32),
    ffo=((2, 8, FF), F32),
    dkv_r=((2, ROWS, INNER), BF),
    g_own=((D, INNER), F32),
    fin=((2, 8, 768), F32),
    fin_r=((8, 768), F32),
    fin_o=((2, 8, 256), F32),
    fin_or=((8, 256), F32),
)
CHAINS = (("k0", "xyz"), ("k1", "yzx"), ("k2", "zxy"), ("og", "xyz"))
for _n, _ in CHAINS:
    SCRATCH[f"{_n}_w"] = ((4, 4, 4, 16, 256), BF)
    SCRATCH[f"{_n}_r1"] = ((3, 4, 4, 16, 256), BF)
    SCRATCH[f"{_n}_s1"] = ((4, 4, 16, 256), BF)
    SCRATCH[f"{_n}_r2"] = ((3, 4, 16, 256), BF)
    SCRATCH[f"{_n}_s2"] = ((4, 16, 256), BF)
    SCRATCH[f"{_n}_r3"] = ((3, 16, 256), BF)
N_IN = 16
N_OUT = 10


class Refs:
    def __init__(self, names, refs):
        self.__dict__.update(zip(names, refs))

    def __getitem__(self, name):
        return self.__dict__[name]


def layer_kernel(*refs):
    (media_h, lat_h, cot_h, counts_h, mg_h, ms_h, lg_h, ls_h, fg_h, fs_h, wq_h, wk_h, wv_h, wo_h, up_h, down_h) = refs[:N_IN]
    (mixed_o, gmedia_o, glat_o, vec_o, gq_o, gk_o, gv_o, go_o, gup_o, gdown_o) = refs[N_IN : N_IN + N_OUT]
    r = Refs(SCRATCH, refs[N_IN + N_OUT : N_IN + N_OUT + len(SCRATCH)])
    ssem, rsem, lsem, counts = refs[N_IN + N_OUT + len(SCRATCH) :]
    mg, ms, lg, ls, fg, fs = (r.norms.at[k] for k in range(6))

    dp = lax.axis_index("dp")
    pb = lax.axis_index("pb")
    y = dp // 8
    z = (dp // 2) % 4
    xh = dp % 2
    xl = pb // 2
    c = pb % 2
    x = xh * 2 + xl
    g = x * 2 + c
    s = pb
    oc = 1 - c
    me = {"x": x, "y": y, "z": z}

    def dev(yy, zz, xx, cc):
        return ((yy * 4 + zz) * 2 + xx // 2, (xx % 2) * 2 + cc)

    def along(axis, d):
        at = dict(me)
        at[axis] = (me[axis] + d) % 4
        return dev(at["y"], at["z"], at["x"], c)

    def sub(k):
        xl2 = (xl + (k >> 1)) % 2
        c2 = (c + (k & 1)) % 2
        return dev(y, z, xh * 2 + xl2, c2), xl2 * 2 + c2

    def grp(k):
        x2 = (x + (k >> 1)) % 4
        c2 = (c + (k & 1)) % 2
        return dev(y, z, x2, c2), x2 * 2 + c2

    partner = dev(y, z, x, oc)
    counter = itertools.count()
    pending = []

    def send(src, dst, target):
        i = next(counter)
        copy = pltpu.make_async_remote_copy(
            src_ref=src,
            dst_ref=dst,
            send_sem=ssem.at[i],
            recv_sem=rsem.at[i],
            device_id=target,
            device_id_type=MESH,
        )
        copy.start()
        pending.append(copy)
        return copy

    local_counter = itertools.count()

    def fetch(src, dst):
        copy = pltpu.make_async_copy(src, dst, lsem.at[next(local_counter)])
        copy.start()
        return copy

    def index(axes, axis, at):
        return tuple(at if a == axis else slice(None) for a in axes)

    def added(own, got):
        part = own.astype(F32)
        for k in range(3):
            part += got[k].astype(F32)
        return part

    orders = dict(CHAINS)

    def first_step(n):
        axis, w, got = orders[n][0], r[f"{n}_w"], r[f"{n}_r1"]
        return [
            send(w.at[index("yzx", axis, (me[axis] + d) % 4)], got.at[d - 1], along(axis, d))
            for d in (1, 2, 3)
        ]

    def second_step(n, before):
        for copy in before:
            copy.wait_recv()
        axis, out, got = orders[n][0], r[f"{n}_s1"], r[f"{n}_r2"]
        out[...] = added(r[f"{n}_w"][index("yzx", axis, me[axis])], r[f"{n}_r1"]).astype(BF)
        left = [a for a in "yzx" if a != axis]
        axis = orders[n][1]
        return [
            send(out.at[index(left, axis, (me[axis] + d) % 4)], got.at[d - 1], along(axis, d))
            for d in (1, 2, 3)
        ]

    def third_step(n, before):
        for copy in before:
            copy.wait_recv()
        axis, out, got = orders[n][1], r[f"{n}_s2"], r[f"{n}_r3"]
        left = [a for a in "yzx" if a != orders[n][0]]
        out[...] = added(r[f"{n}_s1"][index(left, axis, me[axis])], r[f"{n}_r2"]).astype(BF)
        axis = orders[n][2]
        return [send(out.at[(me[axis] + d) % 4], got.at[d - 1], along(axis, d)) for d in (1, 2, 3)]

    def summed(n, before):
        for copy in before:
            copy.wait_recv()
        return added(r[f"{n}_s2"][me[orders[n][2]]], r[f"{n}_r3"]).reshape(2, 8, 256)

    barrier = pltpu.get_barrier_semaphore()
    greeted = [grp(k)[0] for k in range(1, 8)]
    greeted += [along(a, d) for a in ("y", "z") for d in (1, 2, 3)]
    for target in greeted:
        pl.semaphore_signal(barrier, inc=1, device_id=target, device_id_type=MESH)

    f_lat = fetch(lat_h, r.lc.at[c, x, pl.ds(0, 2)])
    f_lg, f_ls = fetch(lg_h, lg), fetch(ls_h, ls)
    f_wq = fetch(wq_h, r.wq)
    f_cot = fetch(cot_h, r.lc.at[c, x, pl.ds(2, 2)])
    f_mg, f_ms = fetch(mg_h, mg), fetch(ms_h, ms)
    f_media = fetch(media_h, r.media)
    f_wk = fetch(wk_h, r.wk)
    f_wv = fetch(wv_h, r.wv)
    f_counts = fetch(counts_h, counts)
    f_fg, f_fs = fetch(fg_h, fg), fetch(fs_h, fs)
    f_wo = fetch(wo_h, r.wo)
    f_down = fetch(down_h.at[pl.ds(g * SLICE, SLICE), :], r.downs)
    f_up = fetch(up_h.at[:, pl.ds(g * SLICE, SLICE)], r.ups)

    f_lat.wait()
    f_lg.wait()
    f_ls.wait()
    lat_own = r.lc[c, x, pl.ds(0, 2)].astype(F32).reshape(32, D)
    xhat, _ = normalised(lat_own)
    nl = (xhat * lg[...] + ls[...]).astype(BF)
    r.xj[0, pl.ds(MED, LATD), :] = nl[:16]
    r.xj[1, pl.ds(MED, LATD), :] = nl[16:]
    f_wq.wait()
    r.qg[s] = (mm(nl, r.wq[...]) * SCALE).astype(BF)

    pl.semaphore_wait(barrier, len(greeted))
    q_copies = [send(r.qg.at[s], r.qg.at[s], sub(k)[0]) for k in (1, 2, 3)]
    own_lat, own_cot = r.lc.at[c, x, pl.ds(0, 2)], r.lc.at[c, x, pl.ds(2, 2)]
    lat_copies = [send(own_lat, own_lat, along("x", d)) for d in (1, 2, 3)]

    f_media.wait()
    f_mg.wait()
    f_ms.wait()
    for i in range(2):

        def norm_rows(t, carry, i=i):
            at = pl.ds(pl.multiple_of(t * 48, 48), 48)
            xh_, rs_ = normalised(r.media[i, at, :].astype(F32))
            r.mxhat[i, at, :] = xh_
            r.mrstd[i, at, :] = jnp.broadcast_to(rs_, (48, 128))
            r.xj[i, at, :] = (xh_ * mg[...] + ms[...]).astype(BF)
            return carry

        lax.fori_loop(0, MED // 48, norm_rows, 0)
    f_wk.wait()
    f_wv.wait()
    xj = r.xj[...].reshape(2 * ROWS, D)
    for n in range(0, INNER, 256):
        r.kv[:, :, n : n + 256] = mm(xj, r.wk[:, n : n + 256]).astype(BF).reshape(2, ROWS, 256)
        r.kv[:, :, INNER + n : INNER + n + 256] = (
            mm(xj, r.wv[:, n : n + 256]).astype(BF).reshape(2, ROWS, 256)
        )
    r.xt[c] = jnp.transpose(xj)
    xt_pair = send(r.xt.at[c], r.xt.at[c], partner)

    for copy in q_copies:
        copy.wait_recv()
    low = lax.broadcasted_iota(jnp.int32, (64, 128), 1) < 64
    row = lax.broadcasted_iota(jnp.int32, (ROWS, 128), 0)

    def by_head(v):
        v = v.astype(F32)
        return jnp.concatenate([jnp.where(low, v, 0.0), jnp.where(low, 0.0, v)], axis=0).astype(BF)

    def merged(v):
        return jnp.where(low, v[:64], v[64:])

    f_counts.wait()
    tops, sums = [], []
    for i in range(2):
        q_i = jnp.concatenate([r.qg[k, pl.ds(i * 16, 16), :] for k in range(4)], axis=0)
        valid = (row >= MED) | (row + pb * MED < counts[i])
        for hp in range(4):
            ih = i * 4 + hp
            cols = slice(hp * 128, hp * 128 + 128)
            qm = by_head(q_i[:, cols])
            r.qm[ih] = qm
            st = jnp.where(valid, mm_nt(r.kv[i, :, cols], qm), NEG_FILL)
            r.st[ih] = st
            top = jnp.max(st, axis=0, keepdims=True)
            p = jnp.exp(st - top)
            tops.append(top)
            sums.append(jnp.sum(p, axis=0, keepdims=True))
            o = merged(mm_tn(p.astype(BF), r.kv[i, :, INNER + hp * 128 : INNER + hp * 128 + 128])).astype(BF)
            for k in range(4):
                r.o_send[k, pl.ds(i * 16, 16), cols] = o[k * 16 : k * 16 + 16]
    r.stats[s] = jnp.concatenate(tops + sums, axis=0)
    st_copies = [send(r.stats.at[s], r.stats.at[s], sub(k)[0]) for k in (1, 2, 3)]
    o_copies = []
    for k in (1, 2, 3):
        target, s2 = sub(k)
        o_copies.append(send(r.o_send.at[s2], r.o_all.at[s], target))
    f_cot.wait()
    cot_copies = [send(own_cot, own_cot, along("x", d)) for d in (1, 2, 3)]
    r.o_all[s] = r.o_send[s]

    for copy in lat_copies:
        copy.wait_recv()
    half = r.lc.at[c, :, pl.ds(0, 2)]
    lat_half = send(half, half, partner)

    for copy in st_copies + o_copies:
        copy.wait_recv()
    stats = r.stats[...]
    peak = jnp.max(stats[:, :8], axis=0)
    weight = jnp.exp(stats[:, :8] - peak[None])
    total = jnp.sum(weight * stats[:, 8:], axis=0)
    r.lt[...] = peak + jnp.log(total)
    share = (weight / total[None]).reshape(32, 128)
    r.sct[...] = jnp.transpose(jnp.concatenate([share, jnp.zeros((96, 128), F32)], axis=0))
    low16 = low[:16]
    sc0 = r.sct[pl.ds(pl.multiple_of(s * 16, 16), 16), :]
    sc1 = r.sct[pl.ds(pl.multiple_of(64 + s * 16, 16), 16), :]
    att_rows = []
    for i in range(2):
        pairs = []
        for hp in range(4):
            ih = i * 4 + hp
            acc = jnp.zeros((16, 128), F32)
            for k in range(4):
                col = k * 8 + ih
                factor = jnp.where(low16, sc0[:, col : col + 1], sc1[:, col : col + 1])
                acc += r.o_all[k, pl.ds(i * 16, 16), hp * 128 : hp * 128 + 128].astype(F32) * factor
            pairs.append(acc)
        att_rows.append(jnp.concatenate(pairs, axis=1))
    att_own = jnp.concatenate(att_rows, axis=0).astype(BF)
    r.attg[c, x] = att_own
    mine = r.attg.at[c, x]
    att_copies = [send(mine, mine, along("x", d)) for d in (1, 2, 3)]
    arrivals = [send(mine, mine, partner)]
    for copy in cot_copies:
        copy.wait_recv()
    half = r.lc.at[c, :, pl.ds(2, 2)]
    cot_half = send(half, half, partner)
    f_down.wait()
    f_wo.wait()
    r.dact[c] = mm_nt(r.lc[c, :, pl.ds(2, 2)].reshape(128, D), r.downs[...])
    cot_s = r.lc[c, pl.ds(xh * 2, 2), pl.ds(2, 2)].reshape(64, D)
    r.coto[...] = mm_nt(cot_s, r.wo[...]).reshape(2, 32, INNER)
    cot_half.wait_recv()
    r.dact[oc] = mm_nt(r.lc[oc, :, pl.ds(2, 2)].reshape(128, D), r.downs[...])
    lat_half.wait_recv()
    for h in range(2):
        xhat, _ = normalised(r.lc[h, pl.ds(xh * 2, 2), pl.ds(0, 2)].astype(F32).reshape(64, D))
        r.nls[h] = (xhat * lg[...] + ls[...]).astype(BF).reshape(2, 32, D)
    for d, copy in zip((1, 2, 3), att_copies):
        copy.wait_recv()
        part = r.attg.at[c, (x + 4 - d) % 4]
        arrivals.append(send(part, part, partner))

    f_up.wait()
    f_fg.wait()
    f_fs.wait()

    def feed_forward(h):
        lat_h_ = r.lc[h, :, pl.ds(0, 2)].astype(F32).reshape(128, D)
        hidden = lat_h_ + mm(r.attg[h].reshape(128, INNER), r.wo[...])
        r.hid[h] = hidden.reshape(4, 32, D)
        xh_, rs_ = normalised(hidden)
        r.xhv[h] = xh_
        nf = (xh_ * fg[...] + fs[...]).astype(BF)
        r.nf[h] = nf
        u = mm(nf, r.ups[...])
        cdf = 0.5 * (1.0 + lax.erf(u * 0.7071067811865476))
        slope = cdf + u * (jnp.exp(-0.5 * u * u) * 0.3989422804014327)
        r.act[h] = (u * cdf).astype(BF)
        dup = (r.dact[h] * slope).astype(BF)
        r.dup[h] = dup
        dn = mm_nt(dup, r.ups[...])
        r.dnv[h] = dn
        dx = ln_back(dn, xh_, rs_, fg[...])
        return dx, mm_nt(dx.astype(BF), r.wo[...])

    dx, p = feed_forward(c)
    r.dx_f[...] = dx.reshape(4, 32, D)
    r.p_f[...] = p.reshape(4, 32, INNER)
    for copy in arrivals:
        copy.wait_recv()
    dx, p = feed_forward(oc)
    r.p_s[...] = p.astype(BF)
    p_pair = send(r.p_s, r.p_r, partner)
    r.dx_s[...] = dx.astype(BF)
    dx_pair = send(r.dx_s, r.dx_r, partner)
    r.cott[...] = jnp.transpose(r.lc[:, :, pl.ds(2, 2)].reshape(256, D))
    p_pair.wait_recv()
    p_sum = r.p_f[...] + r.p_r[...].astype(F32).reshape(4, 32, INNER)
    r.p_f[...] = p_sum
    r.p_x[...] = p_sum.astype(BF)
    p_copies = []
    for d in (1, 2, 3):
        src = r.p_x.at[pl.ds((x + d) % 4 // 2 * 2, 2)]
        p_copies.append(send(src, r.p_xr.at[d - 1], along("x", d)))
    act_all = r.act[...].reshape(256, SLICE)
    for n in range(4):
        r.gd[n] = mm(r.cott[n * 256 : n * 256 + 256, :], act_all).astype(BF).reshape(4, 64, SLICE)
    gd_1 = [send(r.gd.at[:, (z + d) % 4], r.gd_r1.at[d - 1], along("z", d)) for d in (1, 2, 3)]
    dx_pair.wait_recv()
    dx_sum = r.dx_f[...] + r.dx_r[...].astype(F32).reshape(4, 32, D)
    r.dx_f[...] = dx_sum
    r.dx_f[x] += r.lc[c, x, pl.ds(2, 2)].astype(F32).reshape(32, D)
    r.dxa[c] = r.dx_f[...].astype(BF)
    dx_copies = [send(r.dxa.at[c, (x + d) % 4], r.dx_xr.at[d - 1], along("x", d)) for d in (1, 2, 3)]
    dxa_pair = send(r.dxa.at[c], r.dxa.at[c], partner)
    nf_all = r.nf[...].reshape(256, D)
    dup_all = r.dup[...].reshape(256, SLICE)
    for n in range(4):
        r.gu[n] = mm_tn(nf_all[:, n * 256 : n * 256 + 256], dup_all).astype(BF).reshape(4, 64, SLICE)
    gu_1 = [send(r.gu.at[(y + d) % 4], r.gu_r1.at[d - 1], along("y", d)) for d in (1, 2, 3)]
    dxa_pair.wait_recv()
    dxa = r.dxa[...].reshape(256, D)
    att_half = r.attg[:, :, :, pl.ds(pl.multiple_of(c * 256, 256), 256)].reshape(256, 256)
    for n in range(4):
        r.og_w[n] = mm_tn(dxa[:, n * 256 : n * 256 + 256], att_half).astype(BF).reshape(4, 4, 16, 256)
    og_1 = first_step("og")
    r.mx_s[...] = mm(r.act[oc], r.downs[...]).astype(BF)
    mx_pair = send(r.mx_s, r.mx_r, partner)
    r.mx_f[...] = mm(r.act[c], r.downs[...]).reshape(4, 32, D)

    for copy in p_copies:
        copy.wait_recv()
    da = r.coto[...] + r.p_f[pl.ds(xh * 2, 2)]
    for k in range(3):
        da += r.p_xr[k].astype(F32)
    r.dag[c] = da.astype(BF)
    da_pair = send(r.dag.at[c], r.dag.at[c], partner)
    gain_sum, shift_sum = jnp.zeros((8, D), F32), jnp.zeros((8, D), F32)
    for h in range(2):
        for t in range(0, 128, 32):
            dn = r.dnv[h, t : t + 32, :]
            gain_sum += jnp.sum((dn * r.xhv[h, t : t + 32, :]).reshape(4, 8, D), axis=0)
            shift_sum += jnp.sum(dn.reshape(4, 8, D), axis=0)
    r.vec[pl.ds(4, 1), :] = jnp.sum(gain_sum, axis=0, keepdims=True)
    r.vec[pl.ds(5, 1), :] = jnp.sum(shift_sum, axis=0, keepdims=True)
    r.vec[pl.ds(6, 2), :] = jnp.zeros((2, D), F32)

    da_pair.wait_recv()
    deltas = []
    for i in range(2):
        da_i = jnp.concatenate([r.dag[k % 2, k // 2, pl.ds(i * 16, 16), :] for k in range(4)], axis=0)
        at_i = jnp.concatenate(
            [r.attg[k % 2, xh * 2 + k // 2, pl.ds(i * 16, 16), :] for k in range(4)], axis=0
        )
        prod = da_i.astype(F32) * at_i.astype(F32)
        for hp in range(4):
            both = prod[:, hp * 128 : hp * 128 + 128]
            first = jnp.sum(jnp.where(low, both, 0.0), axis=1, keepdims=True)
            second = jnp.sum(jnp.where(low, 0.0, both), axis=1, keepdims=True)
            deltas.append(jnp.concatenate([first, second], axis=0))
    lane = lax.broadcasted_iota(jnp.int32, (128, 128), 1)
    spread = jnp.zeros((128, 128), F32)
    for ih in range(8):
        spread = jnp.where(lane == ih, deltas[ih], spread)
    r.sct[...] = jnp.transpose(spread)
    for i in range(2):
        da_i = jnp.concatenate([r.dag[k % 2, k // 2, pl.ds(i * 16, 16), :] for k in range(4)], axis=0)
        for hp in range(4):
            ih = i * 4 + hp
            cols = slice(hp * 128, hp * 128 + 128)
            vcols = slice(INNER + hp * 128, INNER + hp * 128 + 128)
            dam = by_head(da_i[:, cols])
            dpt = mm_nt(r.kv[i, :, vcols], dam)
            pt = jnp.exp(r.st[ih] - r.lt[pl.ds(ih, 1), :])
            dst = (pt * (dpt - r.sct[pl.ds(ih, 1), :])).astype(BF)
            r.dkv[i, :, cols] = mm(dst, r.qm[ih]).astype(BF)
            r.dkv[i, :, vcols] = mm(pt.astype(BF), dam).astype(BF)
            dq = merged(mm_tn(dst, r.kv[i, :, cols])).astype(BF)
            for k in range(4):
                r.dq_send[k % 2, k // 2, pl.ds(i * 16, 16), cols] = dq[k * 16 : k * 16 + 16]

    own_cols = pl.ds(pl.multiple_of(c * INNER, INNER), INNER)
    other_cols = pl.ds(pl.multiple_of(oc * INNER, INNER), INNER)
    kv_pair = send(r.dkv.at[:, :, other_cols], r.dkv_r, partner)
    own_half = pl.ds(pl.multiple_of(c * 256, 256), 256)
    other_half = pl.ds(pl.multiple_of(oc * 256, 256), 256)
    dq_pair = send(r.dq_send.at[:, :, :, other_half], r.dq_r, partner)
    dq_copies = []
    for k in (1, 2, 3):
        target, s2 = sub(k)
        dq_copies.append(send(r.dq_send.at[s2 % 2, s2 // 2], r.dq_all.at[s], target))
    r.dq_all[s] = r.dq_send[c, xl]
    d_rows = r.dkv[:, :, own_cols].reshape(2 * ROWS, INNER)
    for n in range(4):
        r.g_own[n * 256 : n * 256 + 256, :] = mm(r.xt[c, n * 256 : n * 256 + 256, :], d_rows)
    xt_pair.wait_recv()
    kv_pair.wait_recv()

    def kv_block(n, cols):
        d_rows = r.dkv_r[:, :, cols].reshape(2 * ROWS, -1)
        at = slice(n * 256, n * 256 + 256)
        part = r.g_own[at, cols] + mm(r.xt[oc, at, :], d_rows)
        return part.astype(BF).reshape(4, 4, 16, -1)

    for n in range(4):
        r.k0_w[n] = kv_block(n, slice(0, 256))
    k0 = first_step("k0")
    dq_pair.wait_recv()
    dq_chip = r.dq_send[:, :, :, own_half].astype(F32) + r.dq_r[...].astype(F32)
    dq_chip = dq_chip.astype(BF).reshape(128, 256)
    nls = r.nls[...].reshape(128, D)
    for n in range(4):
        gq = (mm_tn(nls[:, n * 256 : n * 256 + 256], dq_chip) * SCALE).astype(BF)
        gq = gq.reshape(4, 4, 16, 256)
        r.k1_w[n, :, :, :, 128:] = gq[..., :128]
        r.k2_w[n, :, :, :, 128:] = gq[..., 128:]
        r.k1_w[n, :, :, :, :128] = kv_block(n, slice(256, 384))
        r.k2_w[n, :, :, :, :128] = kv_block(n, slice(384, 512))
    k1 = first_step("k1")
    k2 = first_step("k2")

    mx_pair.wait_recv()
    mx_sum = r.mx_f[...] + r.mx_r[...].astype(F32).reshape(4, 32, D)
    r.mx_f[...] = mx_sum
    r.mx_x[...] = mx_sum.astype(BF)
    mx_copies = [send(r.mx_x.at[(x + d) % 4], r.mx_xr.at[d - 1], along("x", d)) for d in (1, 2, 3)]
    for copy in dx_copies:
        copy.wait_recv()
    r.dhid[...] = added(r.dx_f[x], r.dx_xr)

    for i in range(2):
        for n in range(0, D, 256):
            r.dj[i, :, n : n + 256] = mm_nt(r.dkv[i, :, :INNER], r.wk[n : n + 256, :]) + mm_nt(
                r.dkv[i, :, INNER:], r.wv[n : n + 256, :]
            )
    zero = jnp.zeros((8, D), F32)
    sums_of = (zero, zero)
    for i in range(2):

        def back_rows(t, carry, i=i):
            gain_sum, shift_sum = carry
            at = pl.ds(pl.multiple_of(t * 48, 48), 48)
            xh_ = r.mxhat[i, at, :]
            dn_ = r.dj[i, at, :]
            gmedia_o[i, at, :] = ln_back(dn_, xh_, r.mrstd[i, at, :1], mg[...])
            prod_ = dn_ * xh_
            return gain_sum + jnp.sum(prod_.reshape(6, 8, D), axis=0), shift_sum + jnp.sum(
                dn_.reshape(6, 8, D), axis=0
            )

        sums_of = lax.fori_loop(0, MED // 48, back_rows, sums_of)
    r.vec[pl.ds(0, 1), :] = jnp.sum(sums_of[0], axis=0, keepdims=True)
    r.vec[pl.ds(1, 1), :] = jnp.sum(sums_of[1], axis=0, keepdims=True)
    for copy in dq_copies:
        copy.wait_recv()
    dq = r.dq_all[0].astype(F32)
    for k in range(1, 4):
        dq += r.dq_all[k].astype(F32)
    dq = dq.astype(BF)
    dj_lat = jnp.concatenate([r.dj[0, pl.ds(MED, LATD), :], r.dj[1, pl.ds(MED, LATD), :]], axis=0)
    dnl = mm_nt(dq, r.wq[...]) * SCALE + dj_lat
    xhat, rstd = normalised(r.lc[c, x, pl.ds(0, 2)].astype(F32).reshape(32, D))
    r.vec[pl.ds(2, 1), :] = jnp.sum(dnl * xhat, axis=0, keepdims=True)
    r.vec[pl.ds(3, 1), :] = jnp.sum(dnl, axis=0, keepdims=True)
    vec_1 = send(r.vec, r.vec_r, partner)
    glat_o[...] = (r.dhid[...] + ln_back(dnl, xhat, rstd, lg[...])).reshape(2, 16, D)

    og_2 = second_step("og", og_1)
    for copy in gd_1 + gu_1:
        copy.wait_recv()
    r.gd_s[...] = added(r.gd[:, z], r.gd_r1).astype(BF)
    gd_2 = [send(r.gd_s.at[(y + d) % 4], r.gd_r2.at[d - 1], along("y", d)) for d in (1, 2, 3)]
    r.gu_s[...] = added(r.gu[y], r.gu_r1).astype(BF)
    gu_2 = [send(r.gu_s.at[(z + d) % 4], r.gu_r2.at[d - 1], along("z", d)) for d in (1, 2, 3)]
    vec_1.wait_recv()
    for n in range(4):
        lanes = slice(n * 256, n * 256 + 256)
        r.vec_a[n] = r.vec[:, lanes] + r.vec_r[:, lanes]
    vec_2 = [send(r.vec_a.at[(y + d) % 4], r.vec_y.at[d - 1], along("y", d)) for d in (1, 2, 3)]

    k0 = second_step("k0", k0)
    k1 = second_step("k1", k1)
    k2 = second_step("k2", k2)
    for copy in vec_2:
        copy.wait_recv()
    r.vec_b[...] = added(r.vec_a[y], r.vec_y)
    vec_3 = [send(r.vec_b, r.vec_z.at[d - 1], along("z", d)) for d in (1, 2, 3)]
    og_3 = third_step("og", og_2)
    for copy in gd_2 + gu_2:
        copy.wait_recv()
    r.gff[:, 0] = added(r.gu_s[z], r.gu_r2).reshape(8, 8, SLICE)
    r.gff[:, 1] = added(r.gd_s[y], r.gd_r2).reshape(8, 8, SLICE)
    cols = pl.ds(pl.multiple_of(g * SLICE, SLICE), SLICE)
    gff_copies = []
    for k in range(1, 8):
        target, g2 = grp(k)
        gff_copies.append(send(r.gff.at[g2], r.ffo.at[:, :, cols], target))
    r.ffo[:, :, cols] = r.gff[g]
    k0 = third_step("k0", k0)
    k1 = third_step("k1", k1)
    k2 = third_step("k2", k2)
    for copy in vec_3:
        copy.wait_recv()
    r.vec_c[...] = added(r.vec_b[...], r.vec_z)
    vec_4 = [send(r.vec_c, r.vec_x.at[d - 1], along("x", d)) for d in (1, 2, 3)]
    for copy in mx_copies:
        copy.wait_recv()
    mixed_o[...] = (r.hid[c, x] + added(r.mx_f[x], r.mx_xr)).astype(BF).reshape(2, 16, D)
    r.fin_o[...] = summed("og", og_3)
    og_4 = send(r.fin_o.at[oc], r.fin_or, partner)
    for copy in gff_copies:
        copy.wait_recv()
    gup_o[...] = r.ffo[0]
    gdown_o[...] = r.ffo[1]
    r.fin[:, :, :256] = summed("k0", k0)
    part = summed("k1", k1)
    r.fin[:, :, 256:384] = part[..., :128]
    r.fin[:, :, 512:640] = part[..., 128:]
    part = summed("k2", k2)
    r.fin[:, :, 384:512] = part[..., :128]
    r.fin[:, :, 640:] = part[..., 128:]
    fin_pair = send(r.fin.at[oc], r.fin_r, partner)
    for copy in vec_4:
        copy.wait_recv()
    vec_o[...] = added(r.vec_c[...], r.vec_x)
    og_4.wait_recv()
    go_o[:, own_half] = r.fin_o[c]
    go_o[:, other_half] = r.fin_or[...]
    fin_pair.wait_recv()
    first = c == 0
    mine, other = r.fin[c], r.fin_r[...]
    gk_o[...] = jnp.where(first, mine[:, :INNER], other[:, :INNER])
    gv_o[...] = jnp.where(first, other[:, :INNER], mine[:, :INNER])
    gq_o[:, own_half] = mine[:, INNER:]
    gq_o[:, other_half] = other[:, INNER:]
    for copy in pending:
        copy.wait_send()


def hand_over(mixed, gmedia, glat, vec, gq, gk, gv, go, gup, gdown, *refs):
    outs, lines, sem = refs[:15], refs[15], refs[16]
    pairs = [(gmedia, outs[1]), (glat, outs[2]), (gup, outs[13]), (gdown, outs[14]), (mixed, outs[0])]
    pairs += [(gq, outs[9]), (gk, outs[10]), (gv, outs[11]), (go, outs[12])]
    pairs += [(lines.at[i], outs[3 + i]) for i in range(6)]
    copies = [pltpu.make_async_copy(src, dst, sem.at[i]) for i, (src, dst) in enumerate(pairs)]
    for copy in copies[:9]:
        copy.start()
    place = lax.rem(lax.axis_index("dp") * 4 + lax.axis_index("pb"), 32) * 8
    turned = pltpu.roll(vec[...], lax.rem(256 - place, 256), 1)
    for i in range(6):
        lines[i] = turned[i : i + 1, :8]
    for copy in copies[9:]:
        copy.start()
    for copy in copies:
        copy.wait()


def per_device(*args):
    args = list(args)
    for i in range(3, 9):
        args[i] = args[i].reshape(1, D)
    hbm = pl.BlockSpec(memory_space=pl.ANY)
    vmem = pl.BlockSpec(memory_space=pltpu.VMEM)
    far = pl.BlockSpec(memory_space=pltpu.HBM)
    order = [0, 1, 15, 2, 3, 4, 5, 6, 7, 8, 9, 10, 11, 12, 13, 14]
    outs = pl.pallas_call(
        layer_kernel,
        out_shape=(
            pltpu.VMEM((2, 16, D), BF),
            pltpu.VMEM((2, MED, D), F32),
            pltpu.VMEM((2, 16, D), F32),
            pltpu.VMEM((8, 256), F32),
            pltpu.VMEM((8, INNER), F32),
            pltpu.VMEM((8, INNER), F32),
            pltpu.VMEM((8, INNER), F32),
            pltpu.VMEM((8, INNER), F32),
            pltpu.VMEM((8, FF), F32),
            pltpu.VMEM((8, FF), F32),
        ),
        in_specs=[hbm] * 16,
        out_specs=(vmem,) * N_OUT,
        scratch_shapes=[pltpu.VMEM(shape, dtype) for shape, dtype in SCRATCH.values()]
        + [
            pltpu.SemaphoreType.DMA((N_SEMS,)),
            pltpu.SemaphoreType.DMA((N_SEMS,)),
            pltpu.SemaphoreType.DMA((24,)),
            pltpu.SMEM((2,), jnp.int32),
        ],
        compiler_params=pltpu.CompilerParams(
            collective_id=0, has_side_effects=True, vmem_limit_bytes=52 * 2**20
        ),
    )(*[pltpu.with_memory_space_constraint(args[i], pltpu.HBM) for i in order])
    shapes = [jax.ShapeDtypeStruct(o.shape, o.dtype) for o in outs]
    mixed, gmedia, glat, _, gk, _, _, _, gup, _ = shapes
    one = jax.ShapeDtypeStruct((1, 8), F32)
    done = pl.pallas_call(
        hand_over,
        out_shape=(mixed, gmedia, glat) + (one,) * 6 + (gk,) * 4 + (gup,) * 2,
        in_specs=[vmem] * N_OUT,
        out_specs=(far,) * 15,
        scratch_shapes=[pltpu.VMEM((6, 1, 8), F32), pltpu.SemaphoreType.DMA((15,))],
        compiler_params=pltpu.CompilerParams(vmem_limit_bytes=52 * 2**20),
    )(*outs)
    vectors = tuple(v.reshape(8) for v in done[3:9])
    gq, gk, gv, go, gup, gdown = done[9:]
    return tuple(done[:3]) + vectors + (gq, gk, gv, go.T, gup, gdown.T)


def solution(mesh):
    tokens = P("dp", "pb", None)
    return jax.shard_map(
        per_device,
        mesh=mesh,
        in_specs=(tokens, tokens, P("dp")) + (P(),) * 12 + (tokens,),
        out_specs=(tokens, tokens, tokens)
        + (P(("dp", "pb")),) * 6
        + (P(("dp", "pb"), None),) * 3
        + (P(None, ("dp", "pb")), P(("dp", "pb"), None), P(None, ("dp", "pb"))),
        check_vma=False,
    )
```

```python
import functools
import itertools

import jax
import jax.numpy as jnp
from jax import lax
from jax.experimental import pallas as pl
from jax.experimental.pallas import tpu as pltpu
from jax.sharding import PartitionSpec as P

MESH = pl.DeviceIdType.MESH
BF = jnp.bfloat16
F32 = jnp.float32
D = 1024
INNER = 512
FF = 4096
MED = 144
LATD = 16
ROWS = MED + LATD
SLICE = FF // 8
EPSILON = 1e-05
NEG_FILL = -1e30
SCALE = 0.125
N_SEMS = 200


def mm(a, b):
    return jnp.dot(a, b, preferred_element_type=F32)


def mm_nt(a, b):
    return lax.dot_general(a, b, (((1,), (1,)), ((), ())), preferred_element_type=F32)


def mm_tn(a, b):
    return lax.dot_general(a, b, (((0,), (0,)), ((), ())), preferred_element_type=F32)


def normalised(v):
    cen = v - jnp.mean(v, axis=-1, keepdims=True)
    rstd = lax.rsqrt(jnp.mean(cen * cen, axis=-1, keepdims=True) + EPSILON)
    return cen * rstd, rstd


def ln_back(dn, xhat, rstd, gain):
    dx = dn * gain
    return rstd * (
        dx - jnp.mean(dx, axis=-1, keepdims=True) - xhat * jnp.mean(dx * xhat, axis=-1, keepdims=True)
    )


SCRATCH = dict(
    media=((2, MED, D), BF),
    norms=((6, 1, D), F32),
    mxhat=((2, MED, D), F32),
    mrstd=((2, MED, 128), F32),
    lc=((2, 4, 4, LATD, D), BF),
    wq=((D, INNER), BF),
    wk=((D, INNER), BF),
    wv=((D, INNER), BF),
    wo=((INNER, D), BF),
    ups=((D, SLICE), BF),
    downs=((SLICE, D), BF),
    xj=((2, ROWS, D), BF),
    xt=((2, D, 2 * ROWS), BF),
    kv=((2, ROWS, 2 * INNER), BF),
    qg=((4, 32, INNER), BF),
    qm=((8, 128, 128), BF),
    st=((8, ROWS, 128), F32),
    o_send=((4, 32, INNER), BF),
    o_all=((4, 32, INNER), BF),
    stats=((4, 16, 128), F32),
    sct=((128, 128), F32),
    lt=((8, 128), F32),
    attg=((2, 4, 32, INNER), BF),
    hid=((2, 4, 32, D), F32),
    nf=((2, 128, D), BF),
    cott=((D, 256), BF),
    dact=((2, 128, SLICE), F32),
    act=((2, 128, SLICE), BF),
    dup=((2, 128, SLICE), BF),
    nls=((2, 2, 32, D), BF),
    dnv=((2, 128, D), F32),
    xhv=((2, 128, D), F32),
    coto=((2, 32, INNER), F32),
    p_s=((128, INNER), BF),
    p_r=((128, INNER), BF),
    p_f=((4, 32, INNER), F32),
    p_x=((4, 32, INNER), BF),
    p_xr=((3, 2, 32, INNER), BF),
    dx_s=((128, D), BF),
    dx_r=((128, D), BF),
    dx_f=((4, 32, D), F32),
    dxa=((2, 4, 32, D), BF),
    dx_xr=((3, 32, D), BF),
    mx_s=((128, D), BF),
    mx_r=((128, D), BF),
    mx_f=((4, 32, D), F32),
    mx_x=((4, 32, D), BF),
    mx_xr=((3, 32, D), BF),
    dhid=((32, D), F32),
    dag=((2, 2, 32, INNER), BF),
    dkv=((2, ROWS, 2 * INNER), BF),
    dq_send=((2, 2, 32, INNER), BF),
    dq_all=((4, 32, INNER), BF),
    dq_r=((2, 2, 32, 256), BF),
    dj=((2, ROWS, D), F32),
    vec=((8, D), F32),
    vec_r=((8, D), F32),
    vec_a=((4, 8, 256), F32),
    vec_y=((3, 8, 256), F32),
    vec_b=((8, 256), F32),
    vec_p=((15, 8, 256), F32),
    gu=((4, 4, 64, SLICE), BF),
    gu_r1=((3, 4, 64, SLICE), BF),
    gu_s=((4, 64, SLICE), BF),
    gu_r2=((3, 64, SLICE), BF),
    gd=((4, 4, 64, SLICE), BF),
    gd_r1=((3, 4, 64, SLICE), BF),
    gd_s=((4, 64, SLICE), BF),
    gd_r2=((3, 64, SLICE), BF),
    gff=((8, 16, SLICE), BF),
    ffo=((16, FF), BF),
    dkv_r=((2, ROWS, INNER), BF),
    g_own=((D, INNER), F32),
    fin=((2, 8, 768), F32),
    fin_r=((8, 768), F32),
    fin_o=((2, 8, 256), F32),
    fin_or=((8, 256), F32),
)
FIRST = {"k0": "x", "k1": "y", "k2": "z", "og": "x"}
PLANE = sorted(itertools.product(range(4), range(4)), key=lambda d: -sum(min(a, 4 - a) for a in d))[:15]
for _n in FIRST:
    SCRATCH[f"{_n}_w"] = ((4, 4, 4, 16, 256), BF)
    SCRATCH[f"{_n}_r1"] = ((3, 4, 4, 16, 256), BF)
    SCRATCH[f"{_n}_s1"] = ((4, 4, 16, 256), BF)
    SCRATCH[f"{_n}_r2"] = ((15, 16, 256), BF)
N_IN = 16
N_OUT = 10


class Refs:
    def __init__(self, names, refs):
        self.__dict__.update(zip(names, refs))

    def __getitem__(self, name):
        return self.__dict__[name]


def layer_kernel(*refs):
    (media_h, lat_h, cot_h, counts_h, mg_h, ms_h, lg_h, ls_h, fg_h, fs_h, wq_h, wk_h, wv_h, wo_h, up_h, down_h) = refs[:N_IN]
    (mixed_o, gmedia_o, glat_o, vec_o, gq_o, gk_o, gv_o, go_o, gup_o, gdown_o) = refs[N_IN : N_IN + N_OUT]
    r = Refs(SCRATCH, refs[N_IN + N_OUT : N_IN + N_OUT + len(SCRATCH)])
    ssem, rsem, lsem, counts = refs[N_IN + N_OUT + len(SCRATCH) :]
    mg, ms, lg, ls, fg, fs = (r.norms.at[k] for k in range(6))

    dp = lax.axis_index("dp")
    pb = lax.axis_index("pb")
    y = dp // 8
    z = (dp // 2) % 4
    xh = dp % 2
    xl = pb // 2
    c = pb % 2
    x = xh * 2 + xl
    g = x * 2 + c
    s = pb
    oc = 1 - c
    me = {"x": x, "y": y, "z": z}

    def dev(yy, zz, xx, cc):
        return ((yy * 4 + zz) * 2 + xx // 2, (xx % 2) * 2 + cc)

    def along(axis, d):
        at = dict(me)
        at[axis] = (me[axis] + d) % 4
        return dev(at["y"], at["z"], at["x"], c)

    def sub(k):
        xl2 = (xl + (k >> 1)) % 2
        c2 = (c + (k & 1)) % 2
        return dev(y, z, xh * 2 + xl2, c2), xl2 * 2 + c2

    def grp(k):
        x2 = (x + (k >> 1)) % 4
        c2 = (c + (k & 1)) % 2
        return dev(y, z, x2, c2), x2 * 2 + c2

    partner = dev(y, z, x, oc)
    counter = itertools.count()
    pending = []

    def send(src, dst, target):
        i = next(counter)
        copy = pltpu.make_async_remote_copy(
            src_ref=src,
            dst_ref=dst,
            send_sem=ssem.at[i],
            recv_sem=rsem.at[i],
            device_id=target,
            device_id_type=MESH,
        )
        copy.start()
        pending.append(copy)
        return copy

    local_counter = itertools.count()

    def fetch(src, dst):
        copy = pltpu.make_async_copy(src, dst, lsem.at[next(local_counter)])
        copy.start()
        return copy

    def index(axes, axis, at):
        return tuple(at if a == axis else slice(None) for a in axes)

    def added(own, got):
        part = own.astype(F32)
        for k in range(3):
            part += got[k].astype(F32)
        return part

    def first_step(n):
        axis, w, got = FIRST[n], r[f"{n}_w"], r[f"{n}_r1"]
        return [
            send(w.at[index("yzx", axis, (me[axis] + d) % 4)], got.at[d - 1], along(axis, d))
            for d in (2, 1, 3)
        ]

    def second_step(n, before):
        for copy in before:
            copy.wait_recv()
        axis, out, got = FIRST[n], r[f"{n}_s1"], r[f"{n}_r2"]
        out[...] = added(r[f"{n}_w"][index("yzx", axis, me[axis])], r[f"{n}_r1"]).astype(BF)
        one, two = [a for a in "yzx" if a != axis]
        copies = []
        for k, (d, e) in enumerate(PLANE):
            at = dict(me)
            at[one], at[two] = (me[one] + d) % 4, (me[two] + e) % 4
            target = dev(at["y"], at["z"], at["x"], c)
            copies.append(send(out.at[at[one], at[two]], got.at[k], target))
        return copies

    def summed(n, before):
        for copy in before:
            copy.wait_recv()
        one, two = [a for a in "yzx" if a != FIRST[n]]
        part = r[f"{n}_s1"][me[one], me[two]].astype(F32)
        for k in range(15):
            part += r[f"{n}_r2"][k].astype(F32)
        return part.reshape(2, 8, 256)

    barrier = pltpu.get_barrier_semaphore()
    greeted = [grp(k)[0] for k in range(1, 8)]
    greeted += [along(a, d) for a in ("y", "z") for d in (2, 1, 3)]
    for target in greeted:
        pl.semaphore_signal(barrier, inc=1, device_id=target, device_id_type=MESH)

    f_lat = fetch(lat_h, r.lc.at[c, x, pl.ds(0, 2)])
    f_lg, f_ls = fetch(lg_h, lg), fetch(ls_h, ls)
    f_wq = fetch(wq_h, r.wq)
    f_cot = fetch(cot_h, r.lc.at[c, x, pl.ds(2, 2)])
    f_mg, f_ms = fetch(mg_h, mg), fetch(ms_h, ms)
    f_media = fetch(media_h, r.media)
    f_wk = fetch(wk_h, r.wk)
    f_wv = fetch(wv_h, r.wv)
    f_counts = fetch(counts_h, counts)
    f_fg, f_fs = fetch(fg_h, fg), fetch(fs_h, fs)
    f_wo = fetch(wo_h, r.wo)
    f_down = fetch(down_h.at[pl.ds(g * SLICE, SLICE), :], r.downs)
    f_up = fetch(up_h.at[:, pl.ds(g * SLICE, SLICE)], r.ups)

    f_lat.wait()
    f_lg.wait()
    f_ls.wait()
    lat_own = r.lc[c, x, pl.ds(0, 2)].astype(F32).reshape(32, D)
    xhat, _ = normalised(lat_own)
    nl = (xhat * lg[...] + ls[...]).astype(BF)
    r.xj[0, pl.ds(MED, LATD), :] = nl[:16]
    r.xj[1, pl.ds(MED, LATD), :] = nl[16:]
    f_wq.wait()
    r.qg[s] = (mm(nl, r.wq[...]) * SCALE).astype(BF)

    pl.semaphore_wait(barrier, len(greeted))
    q_copies = [send(r.qg.at[s], r.qg.at[s], sub(k)[0]) for k in (1, 2, 3)]
    own_lat, own_cot = r.lc.at[c, x, pl.ds(0, 2)], r.lc.at[c, x, pl.ds(2, 2)]
    lat_copies = [send(own_lat, own_lat, along("x", d)) for d in (2, 1, 3)]

    f_media.wait()
    f_mg.wait()
    f_ms.wait()
    for i in range(2):

        def norm_rows(t, carry, i=i):
            at = pl.ds(pl.multiple_of(t * 48, 48), 48)
            xh_, rs_ = normalised(r.media[i, at, :].astype(F32))
            r.mxhat[i, at, :] = xh_
            r.mrstd[i, at, :] = jnp.broadcast_to(rs_, (48, 128))
            r.xj[i, at, :] = (xh_ * mg[...] + ms[...]).astype(BF)
            return carry

        lax.fori_loop(0, MED // 48, norm_rows, 0)
    f_wk.wait()
    f_wv.wait()
    xj = r.xj[...].reshape(2 * ROWS, D)
    for n in range(0, INNER, 256):
        r.kv[:, :, n : n + 256] = mm(xj, r.wk[:, n : n + 256]).astype(BF).reshape(2, ROWS, 256)
        r.kv[:, :, INNER + n : INNER + n + 256] = (
            mm(xj, r.wv[:, n : n + 256]).astype(BF).reshape(2, ROWS, 256)
        )
    r.xt[c] = jnp.transpose(xj)
    xt_pair = send(r.xt.at[c], r.xt.at[c], partner)

    for copy in q_copies:
        copy.wait_recv()
    low = lax.broadcasted_iota(jnp.int32, (64, 128), 1) < 64
    row = lax.broadcasted_iota(jnp.int32, (ROWS, 128), 0)

    def by_head(v):
        v = v.astype(F32)
        return jnp.concatenate([jnp.where(low, v, 0.0), jnp.where(low, 0.0, v)], axis=0).astype(BF)

    def merged(v):
        return jnp.where(low, v[:64], v[64:])

    f_counts.wait()
    tops, sums = [], []
    for i in range(2):
        q_i = jnp.concatenate([r.qg[k, pl.ds(i * 16, 16), :] for k in range(4)], axis=0)
        valid = (row >= MED) | (row + pb * MED < counts[i])
        for hp in range(4):
            ih = i * 4 + hp
            cols = slice(hp * 128, hp * 128 + 128)
            qm = by_head(q_i[:, cols])
            r.qm[ih] = qm
            st = jnp.where(valid, mm_nt(r.kv[i, :, cols], qm), NEG_FILL)
            r.st[ih] = st
            top = jnp.max(st, axis=0, keepdims=True)
            p = jnp.exp(st - top)
            tops.append(top)
            sums.append(jnp.sum(p, axis=0, keepdims=True))
            o = merged(mm_tn(p.astype(BF), r.kv[i, :, INNER + hp * 128 : INNER + hp * 128 + 128])).astype(BF)
            for k in range(4):
                r.o_send[k, pl.ds(i * 16, 16), cols] = o[k * 16 : k * 16 + 16]
    r.stats[s] = jnp.concatenate(tops + sums, axis=0)
    st_copies = [send(r.stats.at[s], r.stats.at[s], sub(k)[0]) for k in (1, 2, 3)]
    o_copies = []
    for k in (1, 2, 3):
        target, s2 = sub(k)
        o_copies.append(send(r.o_send.at[s2], r.o_all.at[s], target))
    f_cot.wait()
    cot_copies = [send(own_cot, own_cot, along("x", d)) for d in (2, 1, 3)]
    r.o_all[s] = r.o_send[s]

    for copy in lat_copies:
        copy.wait_recv()
    half = r.lc.at[c, :, pl.ds(0, 2)]
    lat_half = send(half, half, partner)

    for copy in st_copies + o_copies:
        copy.wait_recv()
    stats = r.stats[...]
    peak = jnp.max(stats[:, :8], axis=0)
    weight = jnp.exp(stats[:, :8] - peak[None])
    total = jnp.sum(weight * stats[:, 8:], axis=0)
    r.lt[...] = peak + jnp.log(total)
    share = (weight / total[None]).reshape(32, 128)
    r.sct[...] = jnp.transpose(jnp.concatenate([share, jnp.zeros((96, 128), F32)], axis=0))
    low16 = low[:16]
    sc0 = r.sct[pl.ds(pl.multiple_of(s * 16, 16), 16), :]
    sc1 = r.sct[pl.ds(pl.multiple_of(64 + s * 16, 16), 16), :]
    att_rows = []
    for i in range(2):
        pairs = []
        for hp in range(4):
            ih = i * 4 + hp
            acc = jnp.zeros((16, 128), F32)
            for k in range(4):
                col = k * 8 + ih
                factor = jnp.where(low16, sc0[:, col : col + 1], sc1[:, col : col + 1])
                acc += r.o_all[k, pl.ds(i * 16, 16), hp * 128 : hp * 128 + 128].astype(F32) * factor
            pairs.append(acc)
        att_rows.append(jnp.concatenate(pairs, axis=1))
    att_own = jnp.concatenate(att_rows, axis=0).astype(BF)
    r.attg[c, x] = att_own
    mine = r.attg.at[c, x]
    att_copies = [send(mine, mine, along("x", d)) for d in (2, 1, 3)]
    arrivals = [send(mine, mine, partner)]
    for copy in cot_copies:
        copy.wait_recv()
    half = r.lc.at[c, :, pl.ds(2, 2)]
    cot_half = send(half, half, partner)
    f_down.wait()
    f_wo.wait()
    r.dact[c] = mm_nt(r.lc[c, :, pl.ds(2, 2)].reshape(128, D), r.downs[...])
    cot_s = r.lc[c, pl.ds(xh * 2, 2), pl.ds(2, 2)].reshape(64, D)
    r.coto[...] = mm_nt(cot_s, r.wo[...]).reshape(2, 32, INNER)
    cot_half.wait_recv()
    r.cott[...] = jnp.transpose(r.lc[:, :, pl.ds(2, 2)].reshape(256, D))
    r.dact[oc] = mm_nt(r.lc[oc, :, pl.ds(2, 2)].reshape(128, D), r.downs[...])
    lat_half.wait_recv()
    for h in range(2):
        xhat, _ = normalised(r.lc[h, pl.ds(xh * 2, 2), pl.ds(0, 2)].astype(F32).reshape(64, D))
        r.nls[h] = (xhat * lg[...] + ls[...]).astype(BF).reshape(2, 32, D)
    for d, copy in zip((2, 1, 3), att_copies):
        copy.wait_recv()
        part = r.attg.at[c, (x + 4 - d) % 4]
        arrivals.append(send(part, part, partner))

    f_up.wait()
    f_fg.wait()
    f_fs.wait()

    def feed_forward(h):
        lat_h_ = r.lc[h, :, pl.ds(0, 2)].astype(F32).reshape(128, D)
        hidden = lat_h_ + mm(r.attg[h].reshape(128, INNER), r.wo[...])
        r.hid[h] = hidden.reshape(4, 32, D)
        xh_, rs_ = normalised(hidden)
        r.xhv[h] = xh_
        nf = (xh_ * fg[...] + fs[...]).astype(BF)
        r.nf[h] = nf
        u = mm(nf, r.ups[...])
        cdf = 0.5 * (1.0 + lax.erf(u * 0.7071067811865476))
        slope = cdf + u * (jnp.exp(-0.5 * u * u) * 0.3989422804014327)
        r.act[h] = (u * cdf).astype(BF)
        dup = (r.dact[h] * slope).astype(BF)
        r.dup[h] = dup
        dn = mm_nt(dup, r.ups[...])
        r.dnv[h] = dn
        dx = ln_back(dn, xh_, rs_, fg[...])
        return dx, mm_nt(dx.astype(BF), r.wo[...])

    dx, p = feed_forward(c)
    r.dx_f[...] = dx.reshape(4, 32, D)
    r.p_f[...] = p.reshape(4, 32, INNER)
    for copy in arrivals:
        copy.wait_recv()
    dx, p = feed_forward(oc)
    r.p_s[...] = p.astype(BF)
    p_pair = send(r.p_s, r.p_r, partner)
    r.dx_s[...] = dx.astype(BF)
    dx_pair = send(r.dx_s, r.dx_r, partner)
    act_all = r.act[...].reshape(256, SLICE)
    for n in range(4):
        r.gd[n] = mm(r.cott[n * 256 : n * 256 + 256, :], act_all).astype(BF).reshape(4, 64, SLICE)
    gd_1 = [send(r.gd.at[:, (z + d) % 4], r.gd_r1.at[d - 1], along("z", d)) for d in (2, 1, 3)]
    p_pair.wait_recv()
    p_sum = r.p_f[...] + r.p_r[...].astype(F32).reshape(4, 32, INNER)
    r.p_f[...] = p_sum
    r.p_x[...] = p_sum.astype(BF)
    p_copies = []
    for d in (2, 1, 3):
        src = r.p_x.at[pl.ds((x + d) % 4 // 2 * 2, 2)]
        p_copies.append(send(src, r.p_xr.at[d - 1], along("x", d)))
    nf_all = r.nf[...].reshape(256, D)
    dup_all = r.dup[...].reshape(256, SLICE)
    for n in range(4):
        r.gu[n] = mm_tn(nf_all[:, n * 256 : n * 256 + 256], dup_all).astype(BF).reshape(4, 64, SLICE)
    gu_1 = [send(r.gu.at[(y + d) % 4], r.gu_r1.at[d - 1], along("y", d)) for d in (2, 1, 3)]
    dx_pair.wait_recv()
    dx_sum = r.dx_f[...] + r.dx_r[...].astype(F32).reshape(4, 32, D)
    r.dx_f[...] = dx_sum
    r.dx_f[x] += r.lc[c, x, pl.ds(2, 2)].astype(F32).reshape(32, D)
    r.dxa[c] = r.dx_f[...].astype(BF)
    dx_copies = [send(r.dxa.at[c, (x + d) % 4], r.dx_xr.at[d - 1], along("x", d)) for d in (2, 1, 3)]
    dxa_pair = send(r.dxa.at[c], r.dxa.at[c], partner)
    dxa_pair.wait_recv()
    dxa = r.dxa[...].reshape(256, D)
    att_half = r.attg[:, :, :, pl.ds(pl.multiple_of(c * 256, 256), 256)].reshape(256, 256)
    for n in range(4):
        r.og_w[n] = mm_tn(dxa[:, n * 256 : n * 256 + 256], att_half).astype(BF).reshape(4, 4, 16, 256)
    og_1 = first_step("og")
    r.mx_s[...] = mm(r.act[oc], r.downs[...]).astype(BF)
    mx_pair = send(r.mx_s, r.mx_r, partner)
    r.mx_f[...] = mm(r.act[c], r.downs[...]).reshape(4, 32, D)

    for copy in p_copies:
        copy.wait_recv()
    da = r.coto[...] + r.p_f[pl.ds(xh * 2, 2)]
    for k in range(3):
        da += r.p_xr[k].astype(F32)
    r.dag[c] = da.astype(BF)
    da_pair = send(r.dag.at[c], r.dag.at[c], partner)
    gain_sum, shift_sum = jnp.zeros((8, D), F32), jnp.zeros((8, D), F32)
    for h in range(2):
        for t in range(0, 128, 32):
            dn = r.dnv[h, t : t + 32, :]
            gain_sum += jnp.sum((dn * r.xhv[h, t : t + 32, :]).reshape(4, 8, D), axis=0)
            shift_sum += jnp.sum(dn.reshape(4, 8, D), axis=0)
    r.vec[pl.ds(4, 1), :] = jnp.sum(gain_sum, axis=0, keepdims=True)
    r.vec[pl.ds(5, 1), :] = jnp.sum(shift_sum, axis=0, keepdims=True)
    r.vec[pl.ds(6, 2), :] = jnp.zeros((2, D), F32)

    da_pair.wait_recv()
    deltas = []
    for i in range(2):
        da_i = jnp.concatenate([r.dag[k % 2, k // 2, pl.ds(i * 16, 16), :] for k in range(4)], axis=0)
        at_i = jnp.concatenate(
            [r.attg[k % 2, xh * 2 + k // 2, pl.ds(i * 16, 16), :] for k in range(4)], axis=0
        )
        prod = da_i.astype(F32) * at_i.astype(F32)
        for hp in range(4):
            both = prod[:, hp * 128 : hp * 128 + 128]
            first = jnp.sum(jnp.where(low, both, 0.0), axis=1, keepdims=True)
            second = jnp.sum(jnp.where(low, 0.0, both), axis=1, keepdims=True)
            deltas.append(jnp.concatenate([first, second], axis=0))
    lane = lax.broadcasted_iota(jnp.int32, (128, 128), 1)
    spread = jnp.zeros((128, 128), F32)
    for ih in range(8):
        spread = jnp.where(lane == ih, deltas[ih], spread)
    r.sct[...] = jnp.transpose(spread)
    for i in range(2):
        da_i = jnp.concatenate([r.dag[k % 2, k // 2, pl.ds(i * 16, 16), :] for k in range(4)], axis=0)
        for hp in range(4):
            ih = i * 4 + hp
            cols = slice(hp * 128, hp * 128 + 128)
            vcols = slice(INNER + hp * 128, INNER + hp * 128 + 128)
            dam = by_head(da_i[:, cols])
            dpt = mm_nt(r.kv[i, :, vcols], dam)
            pt = jnp.exp(r.st[ih] - r.lt[pl.ds(ih, 1), :])
            dst = (pt * (dpt - r.sct[pl.ds(ih, 1), :])).astype(BF)
            r.dkv[i, :, cols] = mm(dst, r.qm[ih]).astype(BF)
            r.dkv[i, :, vcols] = mm(pt.astype(BF), dam).astype(BF)
            dq = merged(mm_tn(dst, r.kv[i, :, cols])).astype(BF)
            for k in range(4):
                r.dq_send[k % 2, k // 2, pl.ds(i * 16, 16), cols] = dq[k * 16 : k * 16 + 16]

    own_cols = pl.ds(pl.multiple_of(c * INNER, INNER), INNER)
    other_cols = pl.ds(pl.multiple_of(oc * INNER, INNER), INNER)
    kv_pair = send(r.dkv.at[:, :, other_cols], r.dkv_r, partner)
    own_half = pl.ds(pl.multiple_of(c * 256, 256), 256)
    other_half = pl.ds(pl.multiple_of(oc * 256, 256), 256)
    dq_pair = send(r.dq_send.at[:, :, :, other_half], r.dq_r, partner)
    dq_copies = []
    for k in (1, 2, 3):
        target, s2 = sub(k)
        dq_copies.append(send(r.dq_send.at[s2 % 2, s2 // 2], r.dq_all.at[s], target))
    r.dq_all[s] = r.dq_send[c, xl]
    d_rows = r.dkv[:, :, own_cols].reshape(2 * ROWS, INNER)
    for n in range(4):
        r.g_own[n * 256 : n * 256 + 256, :] = mm(r.xt[c, n * 256 : n * 256 + 256, :], d_rows)
    xt_pair.wait_recv()
    kv_pair.wait_recv()

    def kv_block(n, cols):
        d_rows = r.dkv_r[:, :, cols].reshape(2 * ROWS, -1)
        at = slice(n * 256, n * 256 + 256)
        part = r.g_own[at, cols] + mm(r.xt[oc, at, :], d_rows)
        return part.astype(BF).reshape(4, 4, 16, -1)

    for n in range(4):
        r.k0_w[n] = kv_block(n, slice(0, 256))
    k0 = first_step("k0")
    dq_pair.wait_recv()
    dq_chip = r.dq_send[:, :, :, own_half].astype(F32) + r.dq_r[...].astype(F32)
    dq_chip = dq_chip.astype(BF).reshape(128, 256)
    nls = r.nls[...].reshape(128, D)
    for n in range(4):
        gq = (mm_tn(nls[:, n * 256 : n * 256 + 256], dq_chip) * SCALE).astype(BF)
        gq = gq.reshape(4, 4, 16, 256)
        r.k1_w[n, :, :, :, 128:] = gq[..., :128]
        r.k2_w[n, :, :, :, 128:] = gq[..., 128:]
        r.k1_w[n, :, :, :, :128] = kv_block(n, slice(256, 384))
        r.k2_w[n, :, :, :, :128] = kv_block(n, slice(384, 512))
    k1 = first_step("k1")
    k2 = first_step("k2")

    mx_pair.wait_recv()
    mx_sum = r.mx_f[...] + r.mx_r[...].astype(F32).reshape(4, 32, D)
    r.mx_f[...] = mx_sum
    r.mx_x[...] = mx_sum.astype(BF)
    mx_copies = [send(r.mx_x.at[(x + d) % 4], r.mx_xr.at[d - 1], along("x", d)) for d in (2, 1, 3)]
    for copy in dx_copies:
        copy.wait_recv()
    r.dhid[...] = added(r.dx_f[x], r.dx_xr)

    for i in range(2):
        for n in range(0, D, 256):
            r.dj[i, :, n : n + 256] = mm_nt(r.dkv[i, :, :INNER], r.wk[n : n + 256, :]) + mm_nt(
                r.dkv[i, :, INNER:], r.wv[n : n + 256, :]
            )
    zero = jnp.zeros((8, D), F32)
    sums_of = (zero, zero)
    for i in range(2):

        def back_rows(t, carry, i=i):
            gain_sum, shift_sum = carry
            at = pl.ds(pl.multiple_of(t * 48, 48), 48)
            xh_ = r.mxhat[i, at, :]
            dn_ = r.dj[i, at, :]
            gmedia_o[i, at, :] = ln_back(dn_, xh_, r.mrstd[i, at, :1], mg[...])
            prod_ = dn_ * xh_
            return gain_sum + jnp.sum(prod_.reshape(6, 8, D), axis=0), shift_sum + jnp.sum(
                dn_.reshape(6, 8, D), axis=0
            )

        sums_of = lax.fori_loop(0, MED // 48, back_rows, sums_of)
    r.vec[pl.ds(0, 1), :] = jnp.sum(sums_of[0], axis=0, keepdims=True)
    r.vec[pl.ds(1, 1), :] = jnp.sum(sums_of[1], axis=0, keepdims=True)
    for copy in dq_copies:
        copy.wait_recv()
    dq = r.dq_all[0].astype(F32)
    for k in range(1, 4):
        dq += r.dq_all[k].astype(F32)
    dq = dq.astype(BF)
    dj_lat = jnp.concatenate([r.dj[0, pl.ds(MED, LATD), :], r.dj[1, pl.ds(MED, LATD), :]], axis=0)
    dnl = mm_nt(dq, r.wq[...]) * SCALE + dj_lat
    xhat, rstd = normalised(r.lc[c, x, pl.ds(0, 2)].astype(F32).reshape(32, D))
    r.vec[pl.ds(2, 1), :] = jnp.sum(dnl * xhat, axis=0, keepdims=True)
    r.vec[pl.ds(3, 1), :] = jnp.sum(dnl, axis=0, keepdims=True)
    vec_1 = send(r.vec, r.vec_r, partner)
    glat_o[...] = (r.dhid[...] + ln_back(dnl, xhat, rstd, lg[...])).reshape(2, 16, D)

    for copy in gd_1 + gu_1:
        copy.wait_recv()
    r.gd_s[...] = added(r.gd[:, z], r.gd_r1).astype(BF)
    gd_2 = [send(r.gd_s.at[(y + d) % 4], r.gd_r2.at[d - 1], along("y", d)) for d in (2, 1, 3)]
    r.gu_s[...] = added(r.gu[y], r.gu_r1).astype(BF)
    gu_2 = [send(r.gu_s.at[(z + d) % 4], r.gu_r2.at[d - 1], along("z", d)) for d in (2, 1, 3)]
    vec_1.wait_recv()
    for n in range(4):
        lanes = slice(n * 256, n * 256 + 256)
        r.vec_a[n] = r.vec[:, lanes] + r.vec_r[:, lanes]
    vec_2 = [send(r.vec_a.at[(y + d) % 4], r.vec_y.at[d - 1], along("y", d)) for d in (2, 1, 3)]

    og_2 = second_step("og", og_1)

    k0 = second_step("k0", k0)
    k1 = second_step("k1", k1)
    k2 = second_step("k2", k2)
    for copy in vec_2:
        copy.wait_recv()
    r.vec_b[...] = added(r.vec_a[y], r.vec_y)
    vec_3 = []
    for k, (d, e) in enumerate(PLANE):
        vec_3.append(send(r.vec_b, r.vec_p.at[k], dev(y, (z + d) % 4, (x + e) % 4, c)))
    for copy in gd_2 + gu_2:
        copy.wait_recv()
    up = added(r.gu_s[z], r.gu_r2).reshape(8, 8, SLICE)
    down = added(r.gd_s[y], r.gd_r2).reshape(8, 8, SLICE)
    r.gff[...] = jnp.concatenate([up, down], axis=1).astype(BF)
    cols = pl.ds(pl.multiple_of(g * SLICE, SLICE), SLICE)
    gff_copies = []
    for k in range(1, 8):
        target, g2 = grp(k)
        gff_copies.append(send(r.gff.at[g2], r.ffo.at[:, cols], target))
    r.ffo[:, cols] = r.gff[g]
    for copy in mx_copies:
        copy.wait_recv()
    mixed_o[...] = (r.hid[c, x] + added(r.mx_f[x], r.mx_xr)).astype(BF).reshape(2, 16, D)
    r.fin_o[...] = summed("og", og_2)
    og_4 = send(r.fin_o.at[oc], r.fin_or, partner)
    for copy in gff_copies:
        copy.wait_recv()
    gup_o[...] = r.ffo[pl.ds(0, 16), :].astype(F32)[:8]
    gdown_o[...] = r.ffo[pl.ds(0, 16), :].astype(F32)[8:]
    r.fin[:, :, :256] = summed("k0", k0)
    part = summed("k1", k1)
    r.fin[:, :, 256:384] = part[..., :128]
    r.fin[:, :, 512:640] = part[..., 128:]
    part = summed("k2", k2)
    r.fin[:, :, 384:512] = part[..., :128]
    r.fin[:, :, 640:] = part[..., 128:]
    fin_pair = send(r.fin.at[oc], r.fin_r, partner)
    for copy in vec_3:
        copy.wait_recv()
    vec_o[...] = r.vec_b[...] + jnp.sum(r.vec_p[...], axis=0)
    og_4.wait_recv()
    go_o[:, own_half] = r.fin_o[c]
    go_o[:, other_half] = r.fin_or[...]
    fin_pair.wait_recv()
    first = c == 0
    mine, other = r.fin[c], r.fin_r[...]
    gk_o[...] = jnp.where(first, mine[:, :INNER], other[:, :INNER])
    gv_o[...] = jnp.where(first, other[:, :INNER], mine[:, :INNER])
    gq_o[:, own_half] = mine[:, INNER:]
    gq_o[:, other_half] = other[:, INNER:]
    for copy in pending:
        copy.wait_send()


def hand_over(mixed, gmedia, glat, vec, gq, gk, gv, go, gup, gdown, *refs):
    outs, lines, sem = refs[:15], refs[15], refs[16]
    pairs = [(gmedia, outs[1]), (glat, outs[2]), (gup, outs[13]), (gdown, outs[14]), (mixed, outs[0])]
    pairs += [(gq, outs[9]), (gk, outs[10]), (gv, outs[11]), (go, outs[12])]
    pairs += [(lines.at[i], outs[3 + i]) for i in range(6)]
    copies = [pltpu.make_async_copy(src, dst, sem.at[i]) for i, (src, dst) in enumerate(pairs)]
    for copy in copies[:9]:
        copy.start()
    place = lax.rem(lax.axis_index("dp") * 4 + lax.axis_index("pb"), 32) * 8
    turned = pltpu.roll(vec[...], lax.rem(256 - place, 256), 1)
    for i in range(6):
        lines[i] = turned[i : i + 1, :8]
    for copy in copies[9:]:
        copy.start()
    for copy in copies:
        copy.wait()


def per_device(*args):
    args = list(args)
    for i in range(3, 9):
        args[i] = args[i].reshape(1, D)
    hbm = pl.BlockSpec(memory_space=pl.ANY)
    vmem = pl.BlockSpec(memory_space=pltpu.VMEM)
    far = pl.BlockSpec(memory_space=pltpu.HBM)
    order = [0, 1, 15, 2, 3, 4, 5, 6, 7, 8, 9, 10, 11, 12, 13, 14]
    outs = pl.pallas_call(
        layer_kernel,
        out_shape=(
            pltpu.VMEM((2, 16, D), BF),
            pltpu.VMEM((2, MED, D), F32),
            pltpu.VMEM((2, 16, D), F32),
            pltpu.VMEM((8, 256), F32),
            pltpu.VMEM((8, INNER), F32),
            pltpu.VMEM((8, INNER), F32),
            pltpu.VMEM((8, INNER), F32),
            pltpu.VMEM((8, INNER), F32),
            pltpu.VMEM((8, FF), F32),
            pltpu.VMEM((8, FF), F32),
        ),
        in_specs=[hbm] * 16,
        out_specs=(vmem,) * N_OUT,
        scratch_shapes=[pltpu.VMEM(shape, dtype) for shape, dtype in SCRATCH.values()]
        + [
            pltpu.SemaphoreType.DMA((N_SEMS,)),
            pltpu.SemaphoreType.DMA((N_SEMS,)),
            pltpu.SemaphoreType.DMA((24,)),
            pltpu.SMEM((2,), jnp.int32),
        ],
        compiler_params=pltpu.CompilerParams(
            collective_id=0, has_side_effects=True, vmem_limit_bytes=52 * 2**20
        ),
    )(*[pltpu.with_memory_space_constraint(args[i], pltpu.HBM) for i in order])
    shapes = [jax.ShapeDtypeStruct(o.shape, o.dtype) for o in outs]
    mixed, gmedia, glat, _, gk, _, _, _, gup, _ = shapes
    one = jax.ShapeDtypeStruct((1, 8), F32)
    done = pl.pallas_call(
        hand_over,
        out_shape=(mixed, gmedia, glat) + (one,) * 6 + (gk,) * 4 + (gup,) * 2,
        in_specs=[vmem] * N_OUT,
        out_specs=(far,) * 15,
        scratch_shapes=[pltpu.VMEM((6, 1, 8), F32), pltpu.SemaphoreType.DMA((15,))],
        compiler_params=pltpu.CompilerParams(vmem_limit_bytes=52 * 2**20),
    )(*outs)
    vectors = tuple(v.reshape(8) for v in done[3:9])
    gq, gk, gv, go, gup, gdown = done[9:]
    return tuple(done[:3]) + vectors + (gq, gk, gv, go.T, gup, gdown.T)


def solution(mesh):
    tokens = P("dp", "pb", None)
    return jax.shard_map(
        per_device,
        mesh=mesh,
        in_specs=(tokens, tokens, P("dp")) + (P(),) * 12 + (tokens,),
        out_specs=(tokens, tokens, tokens)
        + (P(("dp", "pb")),) * 6
        + (P(("dp", "pb"), None),) * 3
        + (P(None, ("dp", "pb")), P(("dp", "pb"), None), P(None, ("dp", "pb"))),
        check_vma=False,
    )
```

```python
import functools
import itertools

import jax
import jax.numpy as jnp
from jax import lax
from jax.experimental import pallas as pl
from jax.experimental.pallas import tpu as pltpu
from jax.sharding import PartitionSpec as P

MESH = pl.DeviceIdType.MESH
BF = jnp.bfloat16
F32 = jnp.float32
D = 1024
INNER = 512
FF = 4096
MED = 144
LATD = 16
ROWS = MED + LATD
SLICE = FF // 8
EPSILON = 1e-05
NEG_FILL = -1e30
SCALE = 0.125
RECV_SEMS = 41
SEND_SEMS = 16


def mm(a, b):
    return jnp.dot(a, b, preferred_element_type=F32)


def mm_nt(a, b):
    return lax.dot_general(a, b, (((1,), (1,)), ((), ())), preferred_element_type=F32)


def mm_tn(a, b):
    return lax.dot_general(a, b, (((0,), (0,)), ((), ())), preferred_element_type=F32)


def normalised(v):
    cen = v - jnp.mean(v, axis=-1, keepdims=True)
    rstd = lax.rsqrt(jnp.mean(cen * cen, axis=-1, keepdims=True) + EPSILON)
    return cen * rstd, rstd


def ln_back(dn, xhat, rstd, gain):
    dx = dn * gain
    return rstd * (
        dx - jnp.mean(dx, axis=-1, keepdims=True) - xhat * jnp.mean(dx * xhat, axis=-1, keepdims=True)
    )


SCRATCH = dict(
    media=((2, MED, D), BF),
    norms=((6, 1, D), F32),
    mxhat=((2, MED, D), F32),
    mrstd=((2, MED, 128), F32),
    lc=((2, 4, 4, LATD, D), BF),
    wq=((D, INNER), BF),
    wk=((D, INNER), BF),
    wv=((D, INNER), BF),
    wo=((INNER, D), BF),
    ups=((D, SLICE), BF),
    downs=((SLICE, D), BF),
    xj=((2, ROWS, D), BF),
    xt=((2, D, 2 * ROWS), BF),
    kv=((2, ROWS, 2 * INNER), BF),
    qg=((4, 32, INNER), BF),
    qm=((8, 128, 128), BF),
    st=((8, ROWS, 128), F32),
    o_send=((4, 32, INNER), BF),
    o_all=((4, 32, INNER), BF),
    stats=((4, 16, 128), F32),
    sct=((128, 128), F32),
    lt=((8, 128), F32),
    attg=((2, 4, 32, INNER), BF),
    hid=((2, 4, 32, D), F32),
    nf=((2, 128, D), BF),
    cott=((D, 256), BF),
    dact=((2, 128, SLICE), F32),
    act=((2, 128, SLICE), BF),
    dup=((2, 128, SLICE), BF),
    nls=((2, 2, 32, D), BF),
    dnv=((2, 128, D), F32),
    xhv=((2, 128, D), F32),
    coto=((2, 32, INNER), F32),
    p_s=((128, INNER), BF),
    p_r=((128, INNER), BF),
    p_f=((4, 32, INNER), F32),
    p_x=((4, 32, INNER), BF),
    p_xr=((3, 2, 32, INNER), BF),
    dx_s=((128, D), BF),
    dx_r=((128, D), BF),
    dx_f=((4, 32, D), F32),
    dxa=((2, 4, 32, D), BF),
    dx_xr=((3, 32, D), BF),
    mx_s=((128, D), BF),
    mx_r=((128, D), BF),
    mx_f=((4, 32, D), F32),
    mx_x=((4, 32, D), BF),
    mx_xr=((3, 32, D), BF),
    dhid=((32, D), F32),
    dag=((2, 2, 32, INNER), BF),
    dkv=((2, ROWS, 2 * INNER), BF),
    dq_send=((2, 2, 32, INNER), BF),
    dq_all=((4, 32, INNER), BF),
    dq_r=((2, 2, 32, 256), BF),
    dj=((2, ROWS, D), F32),
    vec=((8, D), F32),
    vec_r=((8, D), F32),
    vec_a=((4, 8, 256), F32),
    vec_y=((3, 8, 256), F32),
    vec_b=((8, 256), F32),
    vec_p=((15, 8, 256), F32),
    gu=((4, 4, 64, SLICE), BF),
    gu_r1=((3, 4, 64, SLICE), BF),
    gu_s=((4, 64, SLICE), BF),
    gu_r2=((3, 64, SLICE), BF),
    gd=((4, 4, 64, SLICE), BF),
    gd_r1=((3, 4, 64, SLICE), BF),
    gd_s=((4, 64, SLICE), BF),
    gd_r2=((3, 64, SLICE), BF),
    gff=((8, 16, SLICE), BF),
    ffo=((16, FF), BF),
    dkv_r=((2, ROWS, INNER), BF),
    g_own=((D, INNER), F32),
    fin=((2, 8, 768), F32),
    fin_r=((8, 768), F32),
    fin_o=((2, 8, 256), F32),
    fin_or=((8, 256), F32),
)
FIRST = {"k0": "x", "k1": "y", "k2": "z", "og": "x"}
PLANE = sorted(itertools.product(range(4), range(4)), key=lambda d: -sum(min(a, 4 - a) for a in d))[:15]
for _n in FIRST:
    SCRATCH[f"{_n}_w"] = ((4, 4, 4, 16, 256), BF)
    SCRATCH[f"{_n}_r1"] = ((3, 4, 4, 16, 256), BF)
    SCRATCH[f"{_n}_s1"] = ((4, 4, 16, 256), BF)
    SCRATCH[f"{_n}_r2"] = ((15, 16, 256), BF)
N_IN = 16
N_OUT = 10


class Refs:
    def __init__(self, names, refs):
        self.__dict__.update(zip(names, refs))

    def __getitem__(self, name):
        return self.__dict__[name]


def layer_kernel(*refs):
    (media_h, lat_h, cot_h, counts_h, mg_h, ms_h, lg_h, ls_h, fg_h, fs_h, wq_h, wk_h, wv_h, wo_h, up_h, down_h) = refs[:N_IN]
    (mixed_o, gmedia_o, glat_o, vec_o, gq_o, gk_o, gv_o, go_o, gup_o, gdown_o) = refs[N_IN : N_IN + N_OUT]
    r = Refs(SCRATCH, refs[N_IN + N_OUT : N_IN + N_OUT + len(SCRATCH)])
    ssem, rsem, lsem, counts = refs[N_IN + N_OUT + len(SCRATCH) :]
    mg, ms, lg, ls, fg, fs = (r.norms.at[k] for k in range(6))

    dp = lax.axis_index("dp")
    pb = lax.axis_index("pb")
    y = dp // 8
    z = (dp // 2) % 4
    xh = dp % 2
    xl = pb // 2
    c = pb % 2
    x = xh * 2 + xl
    g = x * 2 + c
    s = pb
    oc = 1 - c
    me = {"x": x, "y": y, "z": z}

    def dev(yy, zz, xx, cc):
        return ((yy * 4 + zz) * 2 + xx // 2, (xx % 2) * 2 + cc)

    def along(axis, d):
        at = dict(me)
        at[axis] = (me[axis] + d) % 4
        return dev(at["y"], at["z"], at["x"], c)

    def sub(k):
        xl2 = (xl + (k >> 1)) % 2
        c2 = (c + (k & 1)) % 2
        return dev(y, z, xh * 2 + xl2, c2), xl2 * 2 + c2

    def grp(k):
        x2 = (x + (k >> 1)) % 4
        c2 = (c + (k & 1)) % 2
        return dev(y, z, x2, c2), x2 * 2 + c2

    partner = dev(y, z, x, oc)
    counter = itertools.count()
    pending = {}

    class Sent:
        def __init__(self, whole):
            self.whole = whole
            self.index = next(counter)
            self.slot = self.index % SEND_SEMS
            if self.slot in pending:
                pending.pop(self.slot).wait_send()
            pending[self.slot] = self

        def copy(self, src, dst, target):
            return pltpu.make_async_remote_copy(
                src_ref=src,
                dst_ref=dst,
                send_sem=ssem.at[self.slot],
                recv_sem=rsem.at[self.index],
                device_id=target,
                device_id_type=MESH,
            )

        def add(self, src, dst, target):
            self.copy(src, dst, target).start()

        def wait_recv(self):
            self.copy(self.whole, self.whole, partner).wait_recv()

        def wait_send(self):
            self.copy(self.whole, self.whole, partner).wait_send()

    def send_all(whole, copies):
        sent = Sent(whole)
        for src, dst, target in copies:
            sent.add(src, dst, target)
        return sent

    def send(src, dst, target):
        return send_all(dst, [(src, dst, target)])

    local_counter = itertools.count()

    def fetch(src, dst):
        copy = pltpu.make_async_copy(src, dst, lsem.at[next(local_counter)])
        copy.start()
        return copy

    def index(axes, axis, at):
        return tuple(at if a == axis else slice(None) for a in axes)

    def added(own, got):
        part = own.astype(F32)
        for k in range(3):
            part += got[k].astype(F32)
        return part

    def first_step(n):
        axis, w, got = FIRST[n], r[f"{n}_w"], r[f"{n}_r1"]
        sent = Sent(got)
        for d in (2, 1, 3):
            sent.add(w.at[index("yzx", axis, (me[axis] + d) % 4)], got.at[d - 1], along(axis, d))
        return [sent]

    def second_step(n, before):
        for copy in before:
            copy.wait_recv()
        axis, out, got = FIRST[n], r[f"{n}_s1"], r[f"{n}_r2"]
        out[...] = added(r[f"{n}_w"][index("yzx", axis, me[axis])], r[f"{n}_r1"]).astype(BF)
        one, two = [a for a in "yzx" if a != axis]
        sent = Sent(got)
        for k, (d, e) in enumerate(PLANE):
            at = dict(me)
            at[one], at[two] = (me[one] + d) % 4, (me[two] + e) % 4
            target = dev(at["y"], at["z"], at["x"], c)
            sent.add(out.at[at[one], at[two]], got.at[k], target)
        return [sent]

    def summed(n, before):
        for copy in before:
            copy.wait_recv()
        one, two = [a for a in "yzx" if a != FIRST[n]]
        part = r[f"{n}_s1"][me[one], me[two]].astype(F32)
        for k in range(15):
            part += r[f"{n}_r2"][k].astype(F32)
        return part.reshape(2, 8, 256)

    barrier = pltpu.get_barrier_semaphore()
    greeted = [grp(k)[0] for k in range(1, 8)]
    greeted += [along(a, d) for a in ("y", "z") for d in (2, 1, 3)]
    for target in greeted:
        pl.semaphore_signal(barrier, inc=1, device_id=target, device_id_type=MESH)

    f_lat = fetch(lat_h, r.lc.at[c, x, pl.ds(0, 2)])
    f_lg, f_ls = fetch(lg_h, lg), fetch(ls_h, ls)
    f_wq = fetch(wq_h, r.wq)
    f_cot = fetch(cot_h, r.lc.at[c, x, pl.ds(2, 2)])
    f_mg, f_ms = fetch(mg_h, mg), fetch(ms_h, ms)
    f_media = fetch(media_h, r.media)
    f_wk = fetch(wk_h, r.wk)
    f_wv = fetch(wv_h, r.wv)
    f_counts = fetch(counts_h, counts)
    f_fg, f_fs = fetch(fg_h, fg), fetch(fs_h, fs)
    f_wo = fetch(wo_h, r.wo)
    f_down = fetch(down_h.at[pl.ds(g * SLICE, SLICE), :], r.downs)
    f_up = fetch(up_h.at[:, pl.ds(g * SLICE, SLICE)], r.ups)

    f_lat.wait()
    f_lg.wait()
    f_ls.wait()
    lat_own = r.lc[c, x, pl.ds(0, 2)].astype(F32).reshape(32, D)
    xhat, _ = normalised(lat_own)
    nl = (xhat * lg[...] + ls[...]).astype(BF)
    r.xj[0, pl.ds(MED, LATD), :] = nl[:16]
    r.xj[1, pl.ds(MED, LATD), :] = nl[16:]
    f_wq.wait()
    r.qg[s] = (mm(nl, r.wq[...]) * SCALE).astype(BF)

    pl.semaphore_wait(barrier, len(greeted))
    q_copies = [send_all(r.qg.at[pl.ds(0, 3)], [(r.qg.at[s], r.qg.at[s], sub(k)[0]) for k in (1, 2, 3)])]
    own_lat, own_cot = r.lc.at[c, x, pl.ds(0, 2)], r.lc.at[c, x, pl.ds(2, 2)]
    lat_copies = [send_all(r.lc.at[0, pl.ds(0, 3), pl.ds(0, 2)], [(own_lat, own_lat, along("x", d)) for d in (2, 1, 3)])]

    f_media.wait()
    f_mg.wait()
    f_ms.wait()
    for i in range(2):

        def norm_rows(t, carry, i=i):
            at = pl.ds(pl.multiple_of(t * 48, 48), 48)
            xh_, rs_ = normalised(r.media[i, at, :].astype(F32))
            r.mxhat[i, at, :] = xh_
            r.mrstd[i, at, :] = jnp.broadcast_to(rs_, (48, 128))
            r.xj[i, at, :] = (xh_ * mg[...] + ms[...]).astype(BF)
            return carry

        lax.fori_loop(0, MED // 48, norm_rows, 0)
    f_wk.wait()
    f_wv.wait()
    xj = r.xj[...].reshape(2 * ROWS, D)
    for n in range(0, INNER, 256):
        r.kv[:, :, n : n + 256] = mm(xj, r.wk[:, n : n + 256]).astype(BF).reshape(2, ROWS, 256)
        r.kv[:, :, INNER + n : INNER + n + 256] = (
            mm(xj, r.wv[:, n : n + 256]).astype(BF).reshape(2, ROWS, 256)
        )
    r.xt[c] = jnp.transpose(xj)
    xt_pair = send(r.xt.at[c], r.xt.at[c], partner)

    for copy in q_copies:
        copy.wait_recv()
    low = lax.broadcasted_iota(jnp.int32, (64, 128), 1) < 64
    row = lax.broadcasted_iota(jnp.int32, (ROWS, 128), 0)

    def by_head(v):
        v = v.astype(F32)
        return jnp.concatenate([jnp.where(low, v, 0.0), jnp.where(low, 0.0, v)], axis=0).astype(BF)

    def merged(v):
        return jnp.where(low, v[:64], v[64:])

    f_counts.wait()
    tops, sums = [], []
    for i in range(2):
        q_i = jnp.concatenate([r.qg[k, pl.ds(i * 16, 16), :] for k in range(4)], axis=0)
        valid = (row >= MED) | (row + pb * MED < counts[i])
        for hp in range(4):
            ih = i * 4 + hp
            cols = slice(hp * 128, hp * 128 + 128)
            qm = by_head(q_i[:, cols])
            r.qm[ih] = qm
            st = jnp.where(valid, mm_nt(r.kv[i, :, cols], qm), NEG_FILL)
            r.st[ih] = st
            top = jnp.max(st, axis=0, keepdims=True)
            p = jnp.exp(st - top)
            tops.append(top)
            sums.append(jnp.sum(p, axis=0, keepdims=True))
            o = merged(mm_tn(p.astype(BF), r.kv[i, :, INNER + hp * 128 : INNER + hp * 128 + 128])).astype(BF)
            for k in range(4):
                r.o_send[k, pl.ds(i * 16, 16), cols] = o[k * 16 : k * 16 + 16]
    r.stats[s] = jnp.concatenate(tops + sums, axis=0)
    st_copies = [send_all(r.stats.at[pl.ds(0, 3)], [(r.stats.at[s], r.stats.at[s], sub(k)[0]) for k in (1, 2, 3)])]
    o_sent = Sent(r.o_all.at[pl.ds(0, 3)])
    for k in (1, 2, 3):
        target, s2 = sub(k)
        o_sent.add(r.o_send.at[s2], r.o_all.at[s], target)
    o_copies = [o_sent]
    f_cot.wait()
    cot_copies = [send_all(r.lc.at[0, pl.ds(0, 3), pl.ds(2, 2)], [(own_cot, own_cot, along("x", d)) for d in (2, 1, 3)])]
    r.o_all[s] = r.o_send[s]

    for copy in lat_copies:
        copy.wait_recv()
    half = r.lc.at[c, :, pl.ds(0, 2)]
    lat_half = send(half, half, partner)

    lat_half.wait_recv()
    for h in range(2):
        xhat, _ = normalised(r.lc[h, pl.ds(xh * 2, 2), pl.ds(0, 2)].astype(F32).reshape(64, D))
        r.nls[h] = (xhat * lg[...] + ls[...]).astype(BF).reshape(2, 32, D)

    for copy in st_copies + o_copies:
        copy.wait_recv()
    stats = r.stats[...]
    peak = jnp.max(stats[:, :8], axis=0)
    weight = jnp.exp(stats[:, :8] - peak[None])
    total = jnp.sum(weight * stats[:, 8:], axis=0)
    r.lt[...] = peak + jnp.log(total)
    share = (weight / total[None]).reshape(32, 128)
    r.sct[...] = jnp.transpose(jnp.concatenate([share, jnp.zeros((96, 128), F32)], axis=0))
    low16 = low[:16]
    sc0 = r.sct[pl.ds(pl.multiple_of(s * 16, 16), 16), :]
    sc1 = r.sct[pl.ds(pl.multiple_of(64 + s * 16, 16), 16), :]
    att_rows = []
    for i in range(2):
        pairs = []
        for hp in range(4):
            ih = i * 4 + hp
            acc = jnp.zeros((16, 128), F32)
            for k in range(4):
                col = k * 8 + ih
                factor = jnp.where(low16, sc0[:, col : col + 1], sc1[:, col : col + 1])
                acc += r.o_all[k, pl.ds(i * 16, 16), hp * 128 : hp * 128 + 128].astype(F32) * factor
            pairs.append(acc)
        att_rows.append(jnp.concatenate(pairs, axis=1))
    att_own = jnp.concatenate(att_rows, axis=0).astype(BF)
    r.attg[c, x] = att_own
    mine = r.attg.at[c, x]
    att_copies = [send(mine, mine, along("x", d)) for d in (2, 1, 3)]
    halves = Sent(r.attg.at[0])
    halves.add(mine, mine, partner)
    arrivals = [halves]
    for copy in cot_copies:
        copy.wait_recv()
    half = r.lc.at[c, :, pl.ds(2, 2)]
    cot_half = send(half, half, partner)
    f_down.wait()
    f_wo.wait()
    r.dact[c] = mm_nt(r.lc[c, :, pl.ds(2, 2)].reshape(128, D), r.downs[...])
    cot_s = r.lc[c, pl.ds(xh * 2, 2), pl.ds(2, 2)].reshape(64, D)
    r.coto[...] = mm_nt(cot_s, r.wo[...]).reshape(2, 32, INNER)
    cot_half.wait_recv()
    r.cott[...] = jnp.transpose(r.lc[:, :, pl.ds(2, 2)].reshape(256, D))
    r.dact[oc] = mm_nt(r.lc[oc, :, pl.ds(2, 2)].reshape(128, D), r.downs[...])
    for d, copy in zip((2, 1, 3), att_copies):
        copy.wait_recv()
        part = r.attg.at[c, (x + 4 - d) % 4]
        halves.add(part, part, partner)

    f_up.wait()
    f_fg.wait()
    f_fs.wait()

    def feed_forward(h):
        lat_h_ = r.lc[h, :, pl.ds(0, 2)].astype(F32).reshape(128, D)
        hidden = lat_h_ + mm(r.attg[h].reshape(128, INNER), r.wo[...])
        r.hid[h] = hidden.reshape(4, 32, D)
        xh_, rs_ = normalised(hidden)
        r.xhv[h] = xh_
        nf = (xh_ * fg[...] + fs[...]).astype(BF)
        r.nf[h] = nf
        u = mm(nf, r.ups[...])
        cdf = 0.5 * (1.0 + lax.erf(u * 0.7071067811865476))
        slope = cdf + u * (jnp.exp(-0.5 * u * u) * 0.3989422804014327)
        r.act[h] = (u * cdf).astype(BF)
        dup = (r.dact[h] * slope).astype(BF)
        r.dup[h] = dup
        dn = mm_nt(dup, r.ups[...])
        r.dnv[h] = dn
        dx = ln_back(dn, xh_, rs_, fg[...])
        return dx, mm_nt(dx.astype(BF), r.wo[...])

    dx, p = feed_forward(c)
    r.dx_f[...] = dx.reshape(4, 32, D)
    r.p_f[...] = p.reshape(4, 32, INNER)
    for copy in arrivals:
        copy.wait_recv()
    dx, p = feed_forward(oc)
    r.p_s[...] = p.astype(BF)
    p_pair = send(r.p_s, r.p_r, partner)
    r.dx_s[...] = dx.astype(BF)
    dx_pair = send(r.dx_s, r.dx_r, partner)
    act_all = r.act[...].reshape(256, SLICE)
    for n in range(4):
        r.gd[n] = mm(r.cott[n * 256 : n * 256 + 256, :], act_all).astype(BF).reshape(4, 64, SLICE)
    gd_1 = [send_all(r.gd_r1, [(r.gd.at[:, (z + d) % 4], r.gd_r1.at[d - 1], along("z", d)) for d in (2, 1, 3)])]
    p_pair.wait_recv()
    p_sum = r.p_f[...] + r.p_r[...].astype(F32).reshape(4, 32, INNER)
    r.p_f[...] = p_sum
    r.p_x[...] = p_sum.astype(BF)
    p_sent = Sent(r.p_xr)
    for d in (2, 1, 3):
        src = r.p_x.at[pl.ds((x + d) % 4 // 2 * 2, 2)]
        p_sent.add(src, r.p_xr.at[d - 1], along("x", d))
    p_copies = [p_sent]
    nf_all = r.nf[...].reshape(256, D)
    dup_all = r.dup[...].reshape(256, SLICE)
    for n in range(4):
        r.gu[n] = mm_tn(nf_all[:, n * 256 : n * 256 + 256], dup_all).astype(BF).reshape(4, 64, SLICE)
    gu_1 = [send_all(r.gu_r1, [(r.gu.at[(y + d) % 4], r.gu_r1.at[d - 1], along("y", d)) for d in (2, 1, 3)])]
    dx_pair.wait_recv()
    dx_sum = r.dx_f[...] + r.dx_r[...].astype(F32).reshape(4, 32, D)
    r.dx_f[...] = dx_sum
    r.dx_f[x] += r.lc[c, x, pl.ds(2, 2)].astype(F32).reshape(32, D)
    r.dxa[c] = r.dx_f[...].astype(BF)
    dx_copies = [send_all(r.dx_xr, [(r.dxa.at[c, (x + d) % 4], r.dx_xr.at[d - 1], along("x", d)) for d in (2, 1, 3)])]
    dxa_pair = send(r.dxa.at[c], r.dxa.at[c], partner)
    dxa_pair.wait_recv()
    dxa = r.dxa[...].reshape(256, D)
    att_half = r.attg[:, :, :, pl.ds(pl.multiple_of(c * 256, 256), 256)].reshape(256, 256)
    for n in range(4):
        r.og_w[n] = mm_tn(dxa[:, n * 256 : n * 256 + 256], att_half).astype(BF).reshape(4, 4, 16, 256)
    og_1 = first_step("og")
    r.mx_s[...] = mm(r.act[oc], r.downs[...]).astype(BF)
    mx_pair = send(r.mx_s, r.mx_r, partner)
    r.mx_f[...] = mm(r.act[c], r.downs[...]).reshape(4, 32, D)

    for copy in p_copies:
        copy.wait_recv()
    da = r.coto[...] + r.p_f[pl.ds(xh * 2, 2)]
    for k in range(3):
        da += r.p_xr[k].astype(F32)
    r.dag[c] = da.astype(BF)
    da_pair = send(r.dag.at[c], r.dag.at[c], partner)
    gain_sum, shift_sum = jnp.zeros((8, D), F32), jnp.zeros((8, D), F32)
    for h in range(2):
        for t in range(0, 128, 32):
            dn = r.dnv[h, t : t + 32, :]
            gain_sum += jnp.sum((dn * r.xhv[h, t : t + 32, :]).reshape(4, 8, D), axis=0)
            shift_sum += jnp.sum(dn.reshape(4, 8, D), axis=0)
    r.vec[pl.ds(4, 1), :] = jnp.sum(gain_sum, axis=0, keepdims=True)
    r.vec[pl.ds(5, 1), :] = jnp.sum(shift_sum, axis=0, keepdims=True)
    r.vec[pl.ds(6, 2), :] = jnp.zeros((2, D), F32)

    da_pair.wait_recv()
    deltas = []
    for i in range(2):
        da_i = jnp.concatenate([r.dag[k % 2, k // 2, pl.ds(i * 16, 16), :] for k in range(4)], axis=0)
        at_i = jnp.concatenate(
            [r.attg[k % 2, xh * 2 + k // 2, pl.ds(i * 16, 16), :] for k in range(4)], axis=0
        )
        prod = da_i.astype(F32) * at_i.astype(F32)
        for hp in range(4):
            both = prod[:, hp * 128 : hp * 128 + 128]
            first = jnp.sum(jnp.where(low, both, 0.0), axis=1, keepdims=True)
            second = jnp.sum(jnp.where(low, 0.0, both), axis=1, keepdims=True)
            deltas.append(jnp.concatenate([first, second], axis=0))
    lane = lax.broadcasted_iota(jnp.int32, (128, 128), 1)
    spread = jnp.zeros((128, 128), F32)
    for ih in range(8):
        spread = jnp.where(lane == ih, deltas[ih], spread)
    r.sct[...] = jnp.transpose(spread)
    for i in range(2):
        da_i = jnp.concatenate([r.dag[k % 2, k // 2, pl.ds(i * 16, 16), :] for k in range(4)], axis=0)
        for hp in range(4):
            ih = i * 4 + hp
            cols = slice(hp * 128, hp * 128 + 128)
            vcols = slice(INNER + hp * 128, INNER + hp * 128 + 128)
            dam = by_head(da_i[:, cols])
            dpt = mm_nt(r.kv[i, :, vcols], dam)
            pt = jnp.exp(r.st[ih] - r.lt[pl.ds(ih, 1), :])
            dst = (pt * (dpt - r.sct[pl.ds(ih, 1), :])).astype(BF)
            r.dkv[i, :, cols] = mm(dst, r.qm[ih]).astype(BF)
            r.dkv[i, :, vcols] = mm(pt.astype(BF), dam).astype(BF)
            dq = merged(mm_tn(dst, r.kv[i, :, cols])).astype(BF)
            for k in range(4):
                r.dq_send[k % 2, k // 2, pl.ds(i * 16, 16), cols] = dq[k * 16 : k * 16 + 16]

    own_cols = pl.ds(pl.multiple_of(c * INNER, INNER), INNER)
    other_cols = pl.ds(pl.multiple_of(oc * INNER, INNER), INNER)
    kv_pair = send(r.dkv.at[:, :, other_cols], r.dkv_r, partner)
    own_half = pl.ds(pl.multiple_of(c * 256, 256), 256)
    other_half = pl.ds(pl.multiple_of(oc * 256, 256), 256)
    dq_pair = send(r.dq_send.at[:, :, :, other_half], r.dq_r, partner)
    dq_sent = Sent(r.dq_all.at[pl.ds(0, 3)])
    for k in (1, 2, 3):
        target, s2 = sub(k)
        dq_sent.add(r.dq_send.at[s2 % 2, s2 // 2], r.dq_all.at[s], target)
    dq_copies = [dq_sent]
    r.dq_all[s] = r.dq_send[c, xl]
    d_rows = r.dkv[:, :, own_cols].reshape(2 * ROWS, INNER)
    for n in range(4):
        r.g_own[n * 256 : n * 256 + 256, :] = mm(r.xt[c, n * 256 : n * 256 + 256, :], d_rows)
    xt_pair.wait_recv()
    kv_pair.wait_recv()

    def kv_block(n, cols):
        d_rows = r.dkv_r[:, :, cols].reshape(2 * ROWS, -1)
        at = slice(n * 256, n * 256 + 256)
        part = r.g_own[at, cols] + mm(r.xt[oc, at, :], d_rows)
        return part.astype(BF).reshape(4, 4, 16, -1)

    for n in range(4):
        r.k0_w[n] = kv_block(n, slice(0, 256))
    k0 = first_step("k0")
    dq_pair.wait_recv()
    dq_chip = r.dq_send[:, :, :, own_half].astype(F32) + r.dq_r[...].astype(F32)
    dq_chip = dq_chip.astype(BF).reshape(128, 256)
    nls = r.nls[...].reshape(128, D)
    for n in range(4):
        gq = (mm_tn(nls[:, n * 256 : n * 256 + 256], dq_chip) * SCALE).astype(BF)
        gq = gq.reshape(4, 4, 16, 256)
        r.k1_w[n, :, :, :, 128:] = gq[..., :128]
        r.k2_w[n, :, :, :, 128:] = gq[..., 128:]
        r.k1_w[n, :, :, :, :128] = kv_block(n, slice(256, 384))
        r.k2_w[n, :, :, :, :128] = kv_block(n, slice(384, 512))
    k1 = first_step("k1")
    k2 = first_step("k2")

    mx_pair.wait_recv()
    mx_sum = r.mx_f[...] + r.mx_r[...].astype(F32).reshape(4, 32, D)
    r.mx_f[...] = mx_sum
    r.mx_x[...] = mx_sum.astype(BF)
    mx_copies = [send_all(r.mx_xr, [(r.mx_x.at[(x + d) % 4], r.mx_xr.at[d - 1], along("x", d)) for d in (2, 1, 3)])]
    for copy in dx_copies:
        copy.wait_recv()
    r.dhid[...] = added(r.dx_f[x], r.dx_xr)

    for i in range(2):
        for n in range(0, D, 256):
            r.dj[i, :, n : n + 256] = mm_nt(r.dkv[i, :, :INNER], r.wk[n : n + 256, :]) + mm_nt(
                r.dkv[i, :, INNER:], r.wv[n : n + 256, :]
            )
    zero = jnp.zeros((8, D), F32)
    sums_of = (zero, zero)
    for i in range(2):

        def back_rows(t, carry, i=i):
            gain_sum, shift_sum = carry
            at = pl.ds(pl.multiple_of(t * 48, 48), 48)
            xh_ = r.mxhat[i, at, :]
            dn_ = r.dj[i, at, :]
            gmedia_o[i, at, :] = ln_back(dn_, xh_, r.mrstd[i, at, :1], mg[...])
            prod_ = dn_ * xh_
            return gain_sum + jnp.sum(prod_.reshape(6, 8, D), axis=0), shift_sum + jnp.sum(
                dn_.reshape(6, 8, D), axis=0
            )

        sums_of = lax.fori_loop(0, MED // 48, back_rows, sums_of)
    r.vec[pl.ds(0, 1), :] = jnp.sum(sums_of[0], axis=0, keepdims=True)
    r.vec[pl.ds(1, 1), :] = jnp.sum(sums_of[1], axis=0, keepdims=True)
    for copy in dq_copies:
        copy.wait_recv()
    dq = r.dq_all[0].astype(F32)
    for k in range(1, 4):
        dq += r.dq_all[k].astype(F32)
    dq = dq.astype(BF)
    dj_lat = jnp.concatenate([r.dj[0, pl.ds(MED, LATD), :], r.dj[1, pl.ds(MED, LATD), :]], axis=0)
    dnl = mm_nt(dq, r.wq[...]) * SCALE + dj_lat
    xhat, rstd = normalised(r.lc[c, x, pl.ds(0, 2)].astype(F32).reshape(32, D))
    r.vec[pl.ds(2, 1), :] = jnp.sum(dnl * xhat, axis=0, keepdims=True)
    r.vec[pl.ds(3, 1), :] = jnp.sum(dnl, axis=0, keepdims=True)
    vec_1 = send(r.vec, r.vec_r, partner)
    glat_o[...] = (r.dhid[...] + ln_back(dnl, xhat, rstd, lg[...])).reshape(2, 16, D)

    for copy in gd_1 + gu_1:
        copy.wait_recv()
    r.gd_s[...] = added(r.gd[:, z], r.gd_r1).astype(BF)
    gd_2 = [send_all(r.gd_r2, [(r.gd_s.at[(y + d) % 4], r.gd_r2.at[d - 1], along("y", d)) for d in (2, 1, 3)])]
    r.gu_s[...] = added(r.gu[y], r.gu_r1).astype(BF)
    gu_2 = [send_all(r.gu_r2, [(r.gu_s.at[(z + d) % 4], r.gu_r2.at[d - 1], along("z", d)) for d in (2, 1, 3)])]
    vec_1.wait_recv()
    for n in range(4):
        lanes = slice(n * 256, n * 256 + 256)
        r.vec_a[n] = r.vec[:, lanes] + r.vec_r[:, lanes]
    vec_2 = [send_all(r.vec_y, [(r.vec_a.at[(y + d) % 4], r.vec_y.at[d - 1], along("y", d)) for d in (2, 1, 3)])]

    og_2 = second_step("og", og_1)

    k0 = second_step("k0", k0)
    k1 = second_step("k1", k1)
    k2 = second_step("k2", k2)
    for copy in vec_2:
        copy.wait_recv()
    r.vec_b[...] = added(r.vec_a[y], r.vec_y)
    vec_sent = Sent(r.vec_p)
    for k, (d, e) in enumerate(PLANE):
        vec_sent.add(r.vec_b, r.vec_p.at[k], dev(y, (z + d) % 4, (x + e) % 4, c))
    vec_3 = [vec_sent]
    for copy in gd_2 + gu_2:
        copy.wait_recv()
    up = added(r.gu_s[z], r.gu_r2).reshape(8, 8, SLICE)
    down = added(r.gd_s[y], r.gd_r2).reshape(8, 8, SLICE)
    r.gff[...] = jnp.concatenate([up, down], axis=1).astype(BF)
    cols = pl.ds(pl.multiple_of(g * SLICE, SLICE), SLICE)
    gff_sent = Sent(r.ffo.at[:, pl.ds(0, 7 * SLICE)])
    for k in range(1, 8):
        target, g2 = grp(k)
        gff_sent.add(r.gff.at[g2], r.ffo.at[:, cols], target)
    gff_copies = [gff_sent]
    r.ffo[:, cols] = r.gff[g]
    for copy in mx_copies:
        copy.wait_recv()
    mixed_o[...] = (r.hid[c, x] + added(r.mx_f[x], r.mx_xr)).astype(BF).reshape(2, 16, D)
    r.fin_o[...] = summed("og", og_2)
    og_4 = send(r.fin_o.at[oc], r.fin_or, partner)
    for copy in gff_copies:
        copy.wait_recv()
    gup_o[...] = r.ffo[pl.ds(0, 16), :].astype(F32)[:8]
    gdown_o[...] = r.ffo[pl.ds(0, 16), :].astype(F32)[8:]
    r.fin[:, :, :256] = summed("k0", k0)
    part = summed("k1", k1)
    r.fin[:, :, 256:384] = part[..., :128]
    r.fin[:, :, 512:640] = part[..., 128:]
    part = summed("k2", k2)
    r.fin[:, :, 384:512] = part[..., :128]
    r.fin[:, :, 640:] = part[..., 128:]
    fin_pair = send(r.fin.at[oc], r.fin_r, partner)
    for copy in vec_3:
        copy.wait_recv()
    vec_o[...] = r.vec_b[...] + jnp.sum(r.vec_p[...], axis=0)
    og_4.wait_recv()
    go_o[:, own_half] = r.fin_o[c]
    go_o[:, other_half] = r.fin_or[...]
    fin_pair.wait_recv()
    first = c == 0
    mine, other = r.fin[c], r.fin_r[...]
    gk_o[...] = jnp.where(first, mine[:, :INNER], other[:, :INNER])
    gv_o[...] = jnp.where(first, other[:, :INNER], mine[:, :INNER])
    gq_o[:, own_half] = mine[:, INNER:]
    gq_o[:, other_half] = other[:, INNER:]
    for copy in pending.values():
        copy.wait_send()


def hand_over(mixed, gmedia, glat, vec, gq, gk, gv, go, gup, gdown, *refs):
    outs, lines, sem = refs[:15], refs[15], refs[16]
    pairs = [(gmedia, outs[1]), (glat, outs[2]), (gup, outs[13]), (gdown, outs[14]), (mixed, outs[0])]
    pairs += [(gq, outs[9]), (gk, outs[10]), (gv, outs[11]), (go, outs[12])]
    pairs += [(lines.at[i], outs[3 + i]) for i in range(6)]
    copies = [pltpu.make_async_copy(src, dst, sem.at[i]) for i, (src, dst) in enumerate(pairs)]
    for copy in copies[:9]:
        copy.start()
    place = lax.rem(lax.axis_index("dp") * 4 + lax.axis_index("pb"), 32) * 8
    turned = pltpu.roll(vec[...], lax.rem(256 - place, 256), 1)
    for i in range(6):
        lines[i] = turned[i : i + 1, :8]
    for copy in copies[9:]:
        copy.start()
    for copy in copies:
        copy.wait()


def per_device(*args):
    args = list(args)
    for i in range(3, 9):
        args[i] = args[i].reshape(1, D)
    hbm = pl.BlockSpec(memory_space=pl.ANY)
    vmem = pl.BlockSpec(memory_space=pltpu.VMEM)
    far = pl.BlockSpec(memory_space=pltpu.HBM)
    order = [0, 1, 15, 2, 3, 4, 5, 6, 7, 8, 9, 10, 11, 12, 13, 14]
    outs = pl.pallas_call(
        layer_kernel,
        out_shape=(
            pltpu.VMEM((2, 16, D), BF),
            pltpu.VMEM((2, MED, D), F32),
            pltpu.VMEM((2, 16, D), F32),
            pltpu.VMEM((8, 256), F32),
            pltpu.VMEM((8, INNER), F32),
            pltpu.VMEM((8, INNER), F32),
            pltpu.VMEM((8, INNER), F32),
            pltpu.VMEM((8, INNER), F32),
            pltpu.VMEM((8, FF), F32),
            pltpu.VMEM((8, FF), F32),
        ),
        in_specs=[hbm] * 16,
        out_specs=(vmem,) * N_OUT,
        scratch_shapes=[pltpu.VMEM(shape, dtype) for shape, dtype in SCRATCH.values()]
        + [
            pltpu.SemaphoreType.DMA((SEND_SEMS,)),
            pltpu.SemaphoreType.DMA((RECV_SEMS,)),
            pltpu.SemaphoreType.DMA((16,)),
            pltpu.SMEM((2,), jnp.int32),
        ],
        compiler_params=pltpu.CompilerParams(
            collective_id=0, has_side_effects=True, vmem_limit_bytes=52 * 2**20
        ),
    )(*[pltpu.with_memory_space_constraint(args[i], pltpu.HBM) for i in order])
    shapes = [jax.ShapeDtypeStruct(o.shape, o.dtype) for o in outs]
    mixed, gmedia, glat, _, gk, _, _, _, gup, _ = shapes
    one = jax.ShapeDtypeStruct((1, 8), F32)
    done = pl.pallas_call(
        hand_over,
        out_shape=(mixed, gmedia, glat) + (one,) * 6 + (gk,) * 4 + (gup,) * 2,
        in_specs=[vmem] * N_OUT,
        out_specs=(far,) * 15,
        scratch_shapes=[pltpu.VMEM((6, 1, 8), F32), pltpu.SemaphoreType.DMA((15,))],
        compiler_params=pltpu.CompilerParams(vmem_limit_bytes=52 * 2**20),
    )(*outs)
    vectors = tuple(v.reshape(8) for v in done[3:9])
    gq, gk, gv, go, gup, gdown = done[9:]
    return tuple(done[:3]) + vectors + (gq, gk, gv, go.T, gup, gdown.T)


def solution(mesh):
    tokens = P("dp", "pb", None)
    return jax.shard_map(
        per_device,
        mesh=mesh,
        in_specs=(tokens, tokens, P("dp")) + (P(),) * 12 + (tokens,),
        out_specs=(tokens, tokens, tokens)
        + (P(("dp", "pb")),) * 6
        + (P(("dp", "pb"), None),) * 3
        + (P(None, ("dp", "pb")), P(("dp", "pb"), None), P(None, ("dp", "pb"))),
        check_vma=False,
    )
```

```python
import functools
import itertools

import jax
import jax.numpy as jnp
from jax import lax
from jax.experimental import pallas as pl
from jax.experimental.pallas import tpu as pltpu
from jax.sharding import PartitionSpec as P

MESH = pl.DeviceIdType.MESH
BF = jnp.bfloat16
F32 = jnp.float32
D = 1024
INNER = 512
FF = 4096
MED = 144
LATD = 16
ROWS = MED + LATD
SLICE = FF // 8
EPSILON = 1e-05
NEG_FILL = -1e30
SCALE = 0.125
RECV_SEMS = 39
SEND_SEMS = 12


def mm(a, b):
    return jnp.dot(a, b, preferred_element_type=F32)


def mm_nt(a, b):
    return lax.dot_general(a, b, (((1,), (1,)), ((), ())), preferred_element_type=F32)


def mm_tn(a, b):
    return lax.dot_general(a, b, (((0,), (0,)), ((), ())), preferred_element_type=F32)


def normalised(v):
    cen = v - jnp.mean(v, axis=-1, keepdims=True)
    rstd = lax.rsqrt(jnp.mean(cen * cen, axis=-1, keepdims=True) + EPSILON)
    return cen * rstd, rstd


def ln_back(dn, xhat, rstd, gain):
    dx = dn * gain
    return rstd * (
        dx - jnp.mean(dx, axis=-1, keepdims=True) - xhat * jnp.mean(dx * xhat, axis=-1, keepdims=True)
    )


SCRATCH = dict(
    media=((2, MED, D), BF),
    norms=((6, 1, D), F32),
    mxhat=((2, MED, D), F32),
    mrstd=((2, MED, 128), F32),
    lc=((2, 4, 4, LATD, D), BF),
    wq=((D, INNER), BF),
    wk=((D, INNER), BF),
    wv=((D, INNER), BF),
    wo=((INNER, D), BF),
    ups=((D, SLICE), BF),
    downs=((SLICE, D), BF),
    xj=((2, ROWS, D), BF),
    xt=((2, D, 2 * ROWS), BF),
    kv=((2, ROWS, 2 * INNER), BF),
    qg=((4, 32, INNER), BF),
    qm=((8, 128, 128), BF),
    st=((8, ROWS, 128), F32),
    o_send=((4, 32, INNER), BF),
    o_all=((4, 32, INNER), BF),
    stats=((4, 16, 128), F32),
    sct=((128, 128), F32),
    lt=((8, 128), F32),
    attg=((2, 4, 32, INNER), BF),
    hid=((2, 4, 32, D), F32),
    nf=((2, 128, D), BF),
    cott=((D, 256), BF),
    dact=((2, 128, SLICE), F32),
    act=((2, 128, SLICE), BF),
    dup=((2, 128, SLICE), BF),
    nls=((2, 2, 32, D), BF),
    dnv=((2, 128, D), F32),
    xhv=((2, 128, D), F32),
    coto=((2, 32, INNER), F32),
    p_s=((128, INNER), BF),
    p_r=((128, INNER), BF),
    p_f=((4, 32, INNER), F32),
    p_x=((4, 32, INNER), BF),
    p_xr=((3, 2, 32, INNER), BF),
    dx_s=((128, D), BF),
    dx_r=((128, D), BF),
    dx_f=((4, 32, D), F32),
    dxa=((2, 4, 32, D), BF),
    dx_xr=((3, 32, D), BF),
    mx_s=((128, D), BF),
    mx_r=((128, D), BF),
    mx_f=((4, 32, D), F32),
    mx_x=((4, 32, D), BF),
    mx_xr=((3, 32, D), BF),
    dhid=((32, D), F32),
    dag=((2, 2, 32, INNER), BF),
    dkv=((2, ROWS, 2 * INNER), BF),
    dq_send=((2, 2, 32, INNER), BF),
    dq_all=((4, 32, INNER), BF),
    dq_r=((2, 2, 32, 256), BF),
    dj=((2, ROWS, D), F32),
    vec=((8, D), F32),
    vec_r=((8, D), F32),
    vec_a=((4, 8, 256), F32),
    vec_y=((3, 8, 256), F32),
    vec_b=((8, 256), F32),
    vec_p=((15, 8, 256), F32),
    gu=((4, 4, 64, SLICE), BF),
    gu_r1=((3, 4, 64, SLICE), BF),
    gu_s=((4, 64, SLICE), BF),
    gu_r2=((3, 64, SLICE), BF),
    gd=((4, 4, 64, SLICE), BF),
    gd_r1=((3, 4, 64, SLICE), BF),
    gd_s=((4, 64, SLICE), BF),
    gd_r2=((3, 64, SLICE), BF),
    gff=((8, 16, SLICE), BF),
    ffo=((16, FF), BF),
    dkv_r=((2, ROWS, INNER), BF),
    g_own=((D, INNER), F32),
)
FIRST = {"k0": "x", "k1": "y", "k2": "z", "og": "x"}
PLANE = sorted(itertools.product(range(4), range(4)), key=lambda d: -sum(min(a, 4 - a) for a in d))[:15]
for _n in FIRST:
    SCRATCH[f"{_n}_w"] = ((4, 4, 4, 16, 256), BF)
    SCRATCH[f"{_n}_r1"] = ((3, 4, 4, 16, 256), BF)
    SCRATCH[f"{_n}_s1"] = ((4, 4, 2, 16, 128), BF)
    SCRATCH[f"{_n}_r2"] = ((31, 16, 128), BF)
N_IN = 16
N_OUT = 10


class Refs:
    def __init__(self, names, refs):
        self.__dict__.update(zip(names, refs))

    def __getitem__(self, name):
        return self.__dict__[name]


def layer_kernel(*refs):
    (media_h, lat_h, cot_h, counts_h, mg_h, ms_h, lg_h, ls_h, fg_h, fs_h, wq_h, wk_h, wv_h, wo_h, up_h, down_h) = refs[:N_IN]
    (mixed_o, gmedia_o, glat_o, vec_o, gq_o, gk_o, gv_o, go_o, gup_o, gdown_o) = refs[N_IN : N_IN + N_OUT]
    r = Refs(SCRATCH, refs[N_IN + N_OUT : N_IN + N_OUT + len(SCRATCH)])
    ssem, rsem, lsem, counts = refs[N_IN + N_OUT + len(SCRATCH) :]
    mg, ms, lg, ls, fg, fs = (r.norms.at[k] for k in range(6))

    dp = lax.axis_index("dp")
    pb = lax.axis_index("pb")
    y = dp // 8
    z = (dp // 2) % 4
    xh = dp % 2
    xl = pb // 2
    c = pb % 2
    x = xh * 2 + xl
    g = x * 2 + c
    s = pb
    oc = 1 - c
    me = {"x": x, "y": y, "z": z}

    def dev(yy, zz, xx, cc):
        return ((yy * 4 + zz) * 2 + xx // 2, (xx % 2) * 2 + cc)

    def along(axis, d):
        at = dict(me)
        at[axis] = (me[axis] + d) % 4
        return dev(at["y"], at["z"], at["x"], c)

    def sub(k):
        xl2 = (xl + (k >> 1)) % 2
        c2 = (c + (k & 1)) % 2
        return dev(y, z, xh * 2 + xl2, c2), xl2 * 2 + c2

    def grp(k):
        x2 = (x + (k >> 1)) % 4
        c2 = (c + (k & 1)) % 2
        return dev(y, z, x2, c2), x2 * 2 + c2

    partner = dev(y, z, x, oc)
    counter = itertools.count()
    pending = {}

    class Sent:
        def __init__(self, whole):
            self.whole = whole
            self.index = next(counter)
            self.slot = self.index % SEND_SEMS
            if self.slot in pending:
                pending.pop(self.slot).wait_send()
            pending[self.slot] = self

        def copy(self, src, dst, target):
            return pltpu.make_async_remote_copy(
                src_ref=src,
                dst_ref=dst,
                send_sem=ssem.at[self.slot],
                recv_sem=rsem.at[self.index],
                device_id=target,
                device_id_type=MESH,
            )

        def add(self, src, dst, target):
            self.copy(src, dst, target).start()

        def wait_recv(self):
            self.copy(self.whole, self.whole, partner).wait_recv()

        def wait_send(self):
            self.copy(self.whole, self.whole, partner).wait_send()

    def send_all(whole, copies):
        sent = Sent(whole)
        for src, dst, target in copies:
            sent.add(src, dst, target)
        return sent

    def send(src, dst, target):
        return send_all(dst, [(src, dst, target)])

    local_counter = itertools.count()

    def fetch(src, dst):
        copy = pltpu.make_async_copy(src, dst, lsem.at[next(local_counter)])
        copy.start()
        return copy

    def index(axes, axis, at):
        return tuple(at if a == axis else slice(None) for a in axes)

    def added(own, got):
        part = own.astype(F32)
        for k in range(3):
            part += got[k].astype(F32)
        return part

    def first_step(n):
        axis, w, got = FIRST[n], r[f"{n}_w"], r[f"{n}_r1"]
        sent = Sent(got)
        for d in (2, 1, 3):
            sent.add(w.at[index("yzx", axis, (me[axis] + d) % 4)], got.at[d - 1], along(axis, d))
        return [sent]

    def second_step(n, before):
        for copy in before:
            copy.wait_recv()
        axis, out, got = FIRST[n], r[f"{n}_s1"], r[f"{n}_r2"]
        part = added(r[f"{n}_w"][index("yzx", axis, me[axis])], r[f"{n}_r1"])
        for h in range(2):
            rows = slice(h * 8, h * 8 + 8)
            both = jnp.concatenate([part[:, :, rows, :128], part[:, :, rows, 128:]], axis=2)
            out[:, :, h] = both.astype(BF)
        one, two = [a for a in "yzx" if a != axis]
        sent = Sent(got)
        for k, (d, e) in enumerate(PLANE):
            at = dict(me)
            at[one], at[two] = (me[one] + d) % 4, (me[two] + e) % 4
            block = out.at[at[one], at[two]]
            sent.add(block.at[c], got.at[k], dev(at["y"], at["z"], at["x"], c))
            sent.add(block.at[oc], got.at[15 + k], dev(at["y"], at["z"], at["x"], oc))
        sent.add(out.at[me[one], me[two], oc], got.at[30], partner)
        return [sent]

    def summed(n, before):
        for copy in before:
            copy.wait_recv()
        one, two = [a for a in "yzx" if a != FIRST[n]]
        got = r[f"{n}_r2"]
        mine = r[f"{n}_s1"][me[one], me[two], c].astype(F32)
        for k in range(15):
            mine += got[k].astype(F32)
        other = got[15].astype(F32)
        for k in range(16, 31):
            other += got[k].astype(F32)
        return [jnp.concatenate([v[:8], v[8:]], axis=1) for v in (mine, other)]

    barrier = pltpu.get_barrier_semaphore()
    greeted = [grp(k)[0] for k in range(1, 8)]
    greeted += [along(a, d) for a in ("y", "z") for d in (2, 1, 3)]
    for target in greeted:
        pl.semaphore_signal(barrier, inc=1, device_id=target, device_id_type=MESH)

    f_lat = fetch(lat_h, r.lc.at[c, x, pl.ds(0, 2)])
    f_lg, f_ls = fetch(lg_h, lg), fetch(ls_h, ls)
    f_wq = fetch(wq_h, r.wq)
    f_cot = fetch(cot_h, r.lc.at[c, x, pl.ds(2, 2)])
    f_mg, f_ms = fetch(mg_h, mg), fetch(ms_h, ms)
    f_media = fetch(media_h, r.media)
    f_wk = fetch(wk_h, r.wk)
    f_wv = fetch(wv_h, r.wv)
    f_counts = fetch(counts_h, counts)
    f_fg, f_fs = fetch(fg_h, fg), fetch(fs_h, fs)
    f_wo = fetch(wo_h, r.wo)
    f_down = fetch(down_h.at[pl.ds(g * SLICE, SLICE), :], r.downs)
    f_up = fetch(up_h.at[:, pl.ds(g * SLICE, SLICE)], r.ups)

    f_lat.wait()
    f_lg.wait()
    f_ls.wait()
    lat_own = r.lc[c, x, pl.ds(0, 2)].astype(F32).reshape(32, D)
    xhat, _ = normalised(lat_own)
    nl = (xhat * lg[...] + ls[...]).astype(BF)
    r.xj[0, pl.ds(MED, LATD), :] = nl[:16]
    r.xj[1, pl.ds(MED, LATD), :] = nl[16:]
    f_wq.wait()
    r.qg[s] = (mm(nl, r.wq[...]) * SCALE).astype(BF)

    pl.semaphore_wait(barrier, len(greeted))
    q_copies = [send_all(r.qg.at[pl.ds(0, 3)], [(r.qg.at[s], r.qg.at[s], sub(k)[0]) for k in (1, 2, 3)])]
    own_lat, own_cot = r.lc.at[c, x, pl.ds(0, 2)], r.lc.at[c, x, pl.ds(2, 2)]
    lat_copies = [send_all(r.lc.at[0, pl.ds(0, 3), pl.ds(0, 2)], [(own_lat, own_lat, along("x", d)) for d in (2, 1, 3)])]

    f_media.wait()
    f_mg.wait()
    f_ms.wait()
    for i in range(2):

        def norm_rows(t, carry, i=i):
            at = pl.ds(pl.multiple_of(t * 48, 48), 48)
            xh_, rs_ = normalised(r.media[i, at, :].astype(F32))
            r.mxhat[i, at, :] = xh_
            r.mrstd[i, at, :] = jnp.broadcast_to(rs_, (48, 128))
            r.xj[i, at, :] = (xh_ * mg[...] + ms[...]).astype(BF)
            return carry

        lax.fori_loop(0, MED // 48, norm_rows, 0)
    f_wk.wait()
    f_wv.wait()
    xj = r.xj[...].reshape(2 * ROWS, D)
    for n in range(0, INNER, 256):
        r.kv[:, :, n : n + 256] = mm(xj, r.wk[:, n : n + 256]).astype(BF).reshape(2, ROWS, 256)
        r.kv[:, :, INNER + n : INNER + n + 256] = (
            mm(xj, r.wv[:, n : n + 256]).astype(BF).reshape(2, ROWS, 256)
        )
    r.xt[c] = jnp.transpose(xj)
    xt_pair = send(r.xt.at[c], r.xt.at[c], partner)

    for copy in q_copies:
        copy.wait_recv()
    low = lax.broadcasted_iota(jnp.int32, (64, 128), 1) < 64
    row = lax.broadcasted_iota(jnp.int32, (ROWS, 128), 0)

    def by_head(v):
        v = v.astype(F32)
        return jnp.concatenate([jnp.where(low, v, 0.0), jnp.where(low, 0.0, v)], axis=0).astype(BF)

    def merged(v):
        return jnp.where(low, v[:64], v[64:])

    f_counts.wait()
    tops, sums = [], []
    for i in range(2):
        q_i = jnp.concatenate([r.qg[k, pl.ds(i * 16, 16), :] for k in range(4)], axis=0)
        valid = (row >= MED) | (row + pb * MED < counts[i])
        for hp in range(4):
            ih = i * 4 + hp
            cols = slice(hp * 128, hp * 128 + 128)
            qm = by_head(q_i[:, cols])
            r.qm[ih] = qm
            st = jnp.where(valid, mm_nt(r.kv[i, :, cols], qm), NEG_FILL)
            r.st[ih] = st
            top = jnp.max(st, axis=0, keepdims=True)
            p = jnp.exp(st - top)
            tops.append(top)
            sums.append(jnp.sum(p, axis=0, keepdims=True))
            o = merged(mm_tn(p.astype(BF), r.kv[i, :, INNER + hp * 128 : INNER + hp * 128 + 128])).astype(BF)
            for k in range(4):
                r.o_send[k, pl.ds(i * 16, 16), cols] = o[k * 16 : k * 16 + 16]
    r.stats[s] = jnp.concatenate(tops + sums, axis=0)
    st_copies = [send_all(r.stats.at[pl.ds(0, 3)], [(r.stats.at[s], r.stats.at[s], sub(k)[0]) for k in (1, 2, 3)])]
    o_sent = Sent(r.o_all.at[pl.ds(0, 3)])
    for k in (1, 2, 3):
        target, s2 = sub(k)
        o_sent.add(r.o_send.at[s2], r.o_all.at[s], target)
    o_copies = [o_sent]
    f_cot.wait()
    cot_copies = [send_all(r.lc.at[0, pl.ds(0, 3), pl.ds(2, 2)], [(own_cot, own_cot, along("x", d)) for d in (2, 1, 3)])]
    r.o_all[s] = r.o_send[s]

    for copy in lat_copies:
        copy.wait_recv()
    half = r.lc.at[c, :, pl.ds(0, 2)]
    lat_half = send(half, half, partner)

    lat_half.wait_recv()
    for h in range(2):
        xhat, _ = normalised(r.lc[h, pl.ds(xh * 2, 2), pl.ds(0, 2)].astype(F32).reshape(64, D))
        r.nls[h] = (xhat * lg[...] + ls[...]).astype(BF).reshape(2, 32, D)

    for copy in st_copies + o_copies:
        copy.wait_recv()
    stats = r.stats[...]
    peak = jnp.max(stats[:, :8], axis=0)
    weight = jnp.exp(stats[:, :8] - peak[None])
    total = jnp.sum(weight * stats[:, 8:], axis=0)
    r.lt[...] = peak + jnp.log(total)
    share = (weight / total[None]).reshape(32, 128)
    r.sct[...] = jnp.transpose(jnp.concatenate([share, jnp.zeros((96, 128), F32)], axis=0))
    low16 = low[:16]
    sc0 = r.sct[pl.ds(pl.multiple_of(s * 16, 16), 16), :]
    sc1 = r.sct[pl.ds(pl.multiple_of(64 + s * 16, 16), 16), :]
    att_rows = []
    for i in range(2):
        pairs = []
        for hp in range(4):
            ih = i * 4 + hp
            acc = jnp.zeros((16, 128), F32)
            for k in range(4):
                col = k * 8 + ih
                factor = jnp.where(low16, sc0[:, col : col + 1], sc1[:, col : col + 1])
                acc += r.o_all[k, pl.ds(i * 16, 16), hp * 128 : hp * 128 + 128].astype(F32) * factor
            pairs.append(acc)
        att_rows.append(jnp.concatenate(pairs, axis=1))
    att_own = jnp.concatenate(att_rows, axis=0).astype(BF)
    r.attg[c, x] = att_own
    mine = r.attg.at[c, x]
    att_copies = [send(mine, mine, along("x", d)) for d in (2, 1, 3)]
    halves = Sent(r.attg.at[0])
    halves.add(mine, mine, partner)
    arrivals = [halves]
    for copy in cot_copies:
        copy.wait_recv()
    half = r.lc.at[c, :, pl.ds(2, 2)]
    cot_half = send(half, half, partner)
    f_down.wait()
    f_wo.wait()
    r.dact[c] = mm_nt(r.lc[c, :, pl.ds(2, 2)].reshape(128, D), r.downs[...])
    cot_s = r.lc[c, pl.ds(xh * 2, 2), pl.ds(2, 2)].reshape(64, D)
    r.coto[...] = mm_nt(cot_s, r.wo[...]).reshape(2, 32, INNER)
    cot_half.wait_recv()
    r.cott[...] = jnp.transpose(r.lc[:, :, pl.ds(2, 2)].reshape(256, D))
    r.dact[oc] = mm_nt(r.lc[oc, :, pl.ds(2, 2)].reshape(128, D), r.downs[...])
    for d, copy in zip((2, 1, 3), att_copies):
        copy.wait_recv()
        part = r.attg.at[c, (x + 4 - d) % 4]
        halves.add(part, part, partner)

    f_up.wait()
    f_fg.wait()
    f_fs.wait()

    def feed_forward(h):
        lat_h_ = r.lc[h, :, pl.ds(0, 2)].astype(F32).reshape(128, D)
        hidden = lat_h_ + mm(r.attg[h].reshape(128, INNER), r.wo[...])
        r.hid[h] = hidden.reshape(4, 32, D)
        xh_, rs_ = normalised(hidden)
        r.xhv[h] = xh_
        nf = (xh_ * fg[...] + fs[...]).astype(BF)
        r.nf[h] = nf
        u = mm(nf, r.ups[...])
        cdf = 0.5 * (1.0 + lax.erf(u * 0.7071067811865476))
        slope = cdf + u * (jnp.exp(-0.5 * u * u) * 0.3989422804014327)
        r.act[h] = (u * cdf).astype(BF)
        dup = (r.dact[h] * slope).astype(BF)
        r.dup[h] = dup
        dn = mm_nt(dup, r.ups[...])
        r.dnv[h] = dn
        dx = ln_back(dn, xh_, rs_, fg[...])
        return dx, mm_nt(dx.astype(BF), r.wo[...])

    dx, p = feed_forward(c)
    r.dx_f[...] = dx.reshape(4, 32, D)
    r.p_f[...] = p.reshape(4, 32, INNER)
    for copy in arrivals:
        copy.wait_recv()
    dx, p = feed_forward(oc)
    r.p_s[...] = p.astype(BF)
    p_pair = send(r.p_s, r.p_r, partner)
    r.dx_s[...] = dx.astype(BF)
    dx_pair = send(r.dx_s, r.dx_r, partner)
    act_all = r.act[...].reshape(256, SLICE)
    for n in range(4):
        r.gd[n] = mm(r.cott[n * 256 : n * 256 + 256, :], act_all).astype(BF).reshape(4, 64, SLICE)
    gd_1 = [send_all(r.gd_r1, [(r.gd.at[:, (z + d) % 4], r.gd_r1.at[d - 1], along("z", d)) for d in (2, 1, 3)])]
    p_pair.wait_recv()
    p_sum = r.p_f[...] + r.p_r[...].astype(F32).reshape(4, 32, INNER)
    r.p_f[...] = p_sum
    r.p_x[...] = p_sum.astype(BF)
    p_sent = Sent(r.p_xr)
    for d in (2, 1, 3):
        src = r.p_x.at[pl.ds((x + d) % 4 // 2 * 2, 2)]
        p_sent.add(src, r.p_xr.at[d - 1], along("x", d))
    p_copies = [p_sent]
    nf_all = r.nf[...].reshape(256, D)
    dup_all = r.dup[...].reshape(256, SLICE)
    for n in range(4):
        r.gu[n] = mm_tn(nf_all[:, n * 256 : n * 256 + 256], dup_all).astype(BF).reshape(4, 64, SLICE)
    gu_1 = [send_all(r.gu_r1, [(r.gu.at[(y + d) % 4], r.gu_r1.at[d - 1], along("y", d)) for d in (2, 1, 3)])]
    dx_pair.wait_recv()
    dx_sum = r.dx_f[...] + r.dx_r[...].astype(F32).reshape(4, 32, D)
    r.dx_f[...] = dx_sum
    r.dx_f[x] += r.lc[c, x, pl.ds(2, 2)].astype(F32).reshape(32, D)
    r.dxa[c] = r.dx_f[...].astype(BF)
    dx_copies = [send_all(r.dx_xr, [(r.dxa.at[c, (x + d) % 4], r.dx_xr.at[d - 1], along("x", d)) for d in (2, 1, 3)])]
    dxa_pair = send(r.dxa.at[c], r.dxa.at[c], partner)
    dxa_pair.wait_recv()
    dxa = r.dxa[...].reshape(256, D)
    att_half = r.attg[:, :, :, pl.ds(pl.multiple_of(c * 256, 256), 256)].reshape(256, 256)
    for n in range(4):
        r.og_w[n] = mm_tn(dxa[:, n * 256 : n * 256 + 256], att_half).astype(BF).reshape(4, 4, 16, 256)
    og_1 = first_step("og")
    r.mx_s[...] = mm(r.act[oc], r.downs[...]).astype(BF)
    mx_pair = send(r.mx_s, r.mx_r, partner)
    r.mx_f[...] = mm(r.act[c], r.downs[...]).reshape(4, 32, D)

    for copy in p_copies:
        copy.wait_recv()
    da = r.coto[...] + r.p_f[pl.ds(xh * 2, 2)]
    for k in range(3):
        da += r.p_xr[k].astype(F32)
    r.dag[c] = da.astype(BF)
    da_pair = send(r.dag.at[c], r.dag.at[c], partner)
    gain_sum, shift_sum = jnp.zeros((8, D), F32), jnp.zeros((8, D), F32)
    for h in range(2):
        for t in range(0, 128, 32):
            dn = r.dnv[h, t : t + 32, :]
            gain_sum += jnp.sum((dn * r.xhv[h, t : t + 32, :]).reshape(4, 8, D), axis=0)
            shift_sum += jnp.sum(dn.reshape(4, 8, D), axis=0)
    r.vec[pl.ds(4, 1), :] = jnp.sum(gain_sum, axis=0, keepdims=True)
    r.vec[pl.ds(5, 1), :] = jnp.sum(shift_sum, axis=0, keepdims=True)
    r.vec[pl.ds(6, 2), :] = jnp.zeros((2, D), F32)

    da_pair.wait_recv()
    deltas = []
    for i in range(2):
        da_i = jnp.concatenate([r.dag[k % 2, k // 2, pl.ds(i * 16, 16), :] for k in range(4)], axis=0)
        at_i = jnp.concatenate(
            [r.attg[k % 2, xh * 2 + k // 2, pl.ds(i * 16, 16), :] for k in range(4)], axis=0
        )
        prod = da_i.astype(F32) * at_i.astype(F32)
        for hp in range(4):
            both = prod[:, hp * 128 : hp * 128 + 128]
            first = jnp.sum(jnp.where(low, both, 0.0), axis=1, keepdims=True)
            second = jnp.sum(jnp.where(low, 0.0, both), axis=1, keepdims=True)
            deltas.append(jnp.concatenate([first, second], axis=0))
    lane = lax.broadcasted_iota(jnp.int32, (128, 128), 1)
    spread = jnp.zeros((128, 128), F32)
    for ih in range(8):
        spread = jnp.where(lane == ih, deltas[ih], spread)
    r.sct[...] = jnp.transpose(spread)
    for i in range(2):
        da_i = jnp.concatenate([r.dag[k % 2, k // 2, pl.ds(i * 16, 16), :] for k in range(4)], axis=0)
        for hp in range(4):
            ih = i * 4 + hp
            cols = slice(hp * 128, hp * 128 + 128)
            vcols = slice(INNER + hp * 128, INNER + hp * 128 + 128)
            dam = by_head(da_i[:, cols])
            dpt = mm_nt(r.kv[i, :, vcols], dam)
            pt = jnp.exp(r.st[ih] - r.lt[pl.ds(ih, 1), :])
            dst = (pt * (dpt - r.sct[pl.ds(ih, 1), :])).astype(BF)
            r.dkv[i, :, cols] = mm(dst, r.qm[ih]).astype(BF)
            r.dkv[i, :, vcols] = mm(pt.astype(BF), dam).astype(BF)
            dq = merged(mm_tn(dst, r.kv[i, :, cols])).astype(BF)
            for k in range(4):
                r.dq_send[k % 2, k // 2, pl.ds(i * 16, 16), cols] = dq[k * 16 : k * 16 + 16]

    own_cols = pl.ds(pl.multiple_of(c * INNER, INNER), INNER)
    other_cols = pl.ds(pl.multiple_of(oc * INNER, INNER), INNER)
    kv_pair = send(r.dkv.at[:, :, other_cols], r.dkv_r, partner)
    own_half = pl.ds(pl.multiple_of(c * 256, 256), 256)
    other_half = pl.ds(pl.multiple_of(oc * 256, 256), 256)
    dq_pair = send(r.dq_send.at[:, :, :, other_half], r.dq_r, partner)
    dq_sent = Sent(r.dq_all.at[pl.ds(0, 3)])
    for k in (1, 2, 3):
        target, s2 = sub(k)
        dq_sent.add(r.dq_send.at[s2 % 2, s2 // 2], r.dq_all.at[s], target)
    dq_copies = [dq_sent]
    r.dq_all[s] = r.dq_send[c, xl]
    d_rows = r.dkv[:, :, own_cols].reshape(2 * ROWS, INNER)
    for n in range(4):
        r.g_own[n * 256 : n * 256 + 256, :] = mm(r.xt[c, n * 256 : n * 256 + 256, :], d_rows)
    xt_pair.wait_recv()
    kv_pair.wait_recv()

    def kv_block(n, cols):
        d_rows = r.dkv_r[:, :, cols].reshape(2 * ROWS, -1)
        at = slice(n * 256, n * 256 + 256)
        part = r.g_own[at, cols] + mm(r.xt[oc, at, :], d_rows)
        return part.astype(BF).reshape(4, 4, 16, -1)

    for n in range(4):
        r.k0_w[n] = kv_block(n, slice(0, 256))
    k0 = first_step("k0")
    dq_pair.wait_recv()
    dq_chip = r.dq_send[:, :, :, own_half].astype(F32) + r.dq_r[...].astype(F32)
    dq_chip = dq_chip.astype(BF).reshape(128, 256)
    nls = r.nls[...].reshape(128, D)
    for n in range(4):
        gq = (mm_tn(nls[:, n * 256 : n * 256 + 256], dq_chip) * SCALE).astype(BF)
        gq = gq.reshape(4, 4, 16, 256)
        r.k1_w[n, :, :, :, 128:] = gq[..., :128]
        r.k2_w[n, :, :, :, 128:] = gq[..., 128:]
        r.k1_w[n, :, :, :, :128] = kv_block(n, slice(256, 384))
        r.k2_w[n, :, :, :, :128] = kv_block(n, slice(384, 512))
    k1 = first_step("k1")
    k2 = first_step("k2")

    mx_pair.wait_recv()
    mx_sum = r.mx_f[...] + r.mx_r[...].astype(F32).reshape(4, 32, D)
    r.mx_f[...] = mx_sum
    r.mx_x[...] = mx_sum.astype(BF)
    mx_copies = [send_all(r.mx_xr, [(r.mx_x.at[(x + d) % 4], r.mx_xr.at[d - 1], along("x", d)) for d in (2, 1, 3)])]
    for copy in dx_copies:
        copy.wait_recv()
    r.dhid[...] = added(r.dx_f[x], r.dx_xr)

    for i in range(2):
        for n in range(0, D, 256):
            r.dj[i, :, n : n + 256] = mm_nt(r.dkv[i, :, :INNER], r.wk[n : n + 256, :]) + mm_nt(
                r.dkv[i, :, INNER:], r.wv[n : n + 256, :]
            )
    zero = jnp.zeros((8, D), F32)
    sums_of = (zero, zero)
    for i in range(2):

        def back_rows(t, carry, i=i):
            gain_sum, shift_sum = carry
            at = pl.ds(pl.multiple_of(t * 48, 48), 48)
            xh_ = r.mxhat[i, at, :]
            dn_ = r.dj[i, at, :]
            gmedia_o[i, at, :] = ln_back(dn_, xh_, r.mrstd[i, at, :1], mg[...])
            prod_ = dn_ * xh_
            return gain_sum + jnp.sum(prod_.reshape(6, 8, D), axis=0), shift_sum + jnp.sum(
                dn_.reshape(6, 8, D), axis=0
            )

        sums_of = lax.fori_loop(0, MED // 48, back_rows, sums_of)
    r.vec[pl.ds(0, 1), :] = jnp.sum(sums_of[0], axis=0, keepdims=True)
    r.vec[pl.ds(1, 1), :] = jnp.sum(sums_of[1], axis=0, keepdims=True)
    for copy in dq_copies:
        copy.wait_recv()
    dq = r.dq_all[0].astype(F32)
    for k in range(1, 4):
        dq += r.dq_all[k].astype(F32)
    dq = dq.astype(BF)
    dj_lat = jnp.concatenate([r.dj[0, pl.ds(MED, LATD), :], r.dj[1, pl.ds(MED, LATD), :]], axis=0)
    dnl = mm_nt(dq, r.wq[...]) * SCALE + dj_lat
    xhat, rstd = normalised(r.lc[c, x, pl.ds(0, 2)].astype(F32).reshape(32, D))
    r.vec[pl.ds(2, 1), :] = jnp.sum(dnl * xhat, axis=0, keepdims=True)
    r.vec[pl.ds(3, 1), :] = jnp.sum(dnl, axis=0, keepdims=True)
    vec_1 = send(r.vec, r.vec_r, partner)
    glat_o[...] = (r.dhid[...] + ln_back(dnl, xhat, rstd, lg[...])).reshape(2, 16, D)

    for copy in gd_1 + gu_1:
        copy.wait_recv()
    r.gd_s[...] = added(r.gd[:, z], r.gd_r1).astype(BF)
    gd_2 = [send_all(r.gd_r2, [(r.gd_s.at[(y + d) % 4], r.gd_r2.at[d - 1], along("y", d)) for d in (2, 1, 3)])]
    r.gu_s[...] = added(r.gu[y], r.gu_r1).astype(BF)
    gu_2 = [send_all(r.gu_r2, [(r.gu_s.at[(z + d) % 4], r.gu_r2.at[d - 1], along("z", d)) for d in (2, 1, 3)])]
    vec_1.wait_recv()
    for n in range(4):
        lanes = slice(n * 256, n * 256 + 256)
        r.vec_a[n] = r.vec[:, lanes] + r.vec_r[:, lanes]
    vec_2 = [send_all(r.vec_y, [(r.vec_a.at[(y + d) % 4], r.vec_y.at[d - 1], along("y", d)) for d in (2, 1, 3)])]

    og_2 = second_step("og", og_1)

    k0 = second_step("k0", k0)
    k1 = second_step("k1", k1)
    k2 = second_step("k2", k2)
    for copy in vec_2:
        copy.wait_recv()
    r.vec_b[...] = added(r.vec_a[y], r.vec_y)
    vec_sent = Sent(r.vec_p)
    for k, (d, e) in enumerate(PLANE):
        vec_sent.add(r.vec_b, r.vec_p.at[k], dev(y, (z + d) % 4, (x + e) % 4, c))
    vec_3 = [vec_sent]
    for copy in gd_2 + gu_2:
        copy.wait_recv()
    up = added(r.gu_s[z], r.gu_r2).reshape(8, 8, SLICE)
    down = added(r.gd_s[y], r.gd_r2).reshape(8, 8, SLICE)
    r.gff[...] = jnp.concatenate([up, down], axis=1).astype(BF)
    cols = pl.ds(pl.multiple_of(g * SLICE, SLICE), SLICE)
    gff_sent = Sent(r.ffo.at[:, pl.ds(0, 7 * SLICE)])
    for k in range(1, 8):
        target, g2 = grp(k)
        gff_sent.add(r.gff.at[g2], r.ffo.at[:, cols], target)
    gff_copies = [gff_sent]
    r.ffo[:, cols] = r.gff[g]
    for copy in mx_copies:
        copy.wait_recv()
    mixed_o[...] = (r.hid[c, x] + added(r.mx_f[x], r.mx_xr)).astype(BF).reshape(2, 16, D)
    mine, other = summed("og", og_2)
    go_o[:, own_half] = mine
    go_o[:, other_half] = other
    for copy in gff_copies:
        copy.wait_recv()
    gup_o[...] = r.ffo[pl.ds(0, 16), :].astype(F32)[:8]
    gdown_o[...] = r.ffo[pl.ds(0, 16), :].astype(F32)[8:]
    for copy in vec_3:
        copy.wait_recv()
    vec_o[...] = r.vec_b[...] + jnp.sum(r.vec_p[...], axis=0)
    first = c == 0
    mine, other = summed("k0", k0)
    gk_o[:, :256] = jnp.where(first, mine, other)
    gv_o[:, :256] = jnp.where(first, other, mine)
    for n, m, copies in ((0, "k1", k1), (1, "k2", k2)):
        mine, other = summed(m, copies)
        cols = slice(256 + n * 128, 384 + n * 128)
        gk_o[:, cols] = jnp.where(first, mine[:, :128], other[:, :128])
        gv_o[:, cols] = jnp.where(first, other[:, :128], mine[:, :128])
        gq_o[:, pl.ds(pl.multiple_of(c * 256 + n * 128, 128), 128)] = mine[:, 128:]
        gq_o[:, pl.ds(pl.multiple_of(oc * 256 + n * 128, 128), 128)] = other[:, 128:]
    for copy in pending.values():
        copy.wait_send()


def hand_over(mixed, gmedia, glat, vec, gq, gk, gv, go, gup, gdown, *refs):
    outs, lines, sem = refs[:15], refs[15], refs[16]
    pairs = [(gmedia, outs[1]), (glat, outs[2]), (gup, outs[13]), (gdown, outs[14]), (mixed, outs[0])]
    pairs += [(gq, outs[9]), (gk, outs[10]), (gv, outs[11]), (go, outs[12])]
    pairs += [(lines.at[i], outs[3 + i]) for i in range(6)]
    copies = [pltpu.make_async_copy(src, dst, sem.at[i]) for i, (src, dst) in enumerate(pairs)]
    for copy in copies[:9]:
        copy.start()
    place = lax.rem(lax.axis_index("dp") * 4 + lax.axis_index("pb"), 32) * 8
    turned = pltpu.roll(vec[...], lax.rem(256 - place, 256), 1)
    for i in range(6):
        lines[i] = turned[i : i + 1, :8]
    for copy in copies[9:]:
        copy.start()
    for copy in copies:
        copy.wait()


def per_device(*args):
    args = list(args)
    for i in range(3, 9):
        args[i] = args[i].reshape(1, D)
    hbm = pl.BlockSpec(memory_space=pl.ANY)
    vmem = pl.BlockSpec(memory_space=pltpu.VMEM)
    far = pl.BlockSpec(memory_space=pltpu.HBM)
    order = [0, 1, 15, 2, 3, 4, 5, 6, 7, 8, 9, 10, 11, 12, 13, 14]
    outs = pl.pallas_call(
        layer_kernel,
        out_shape=(
            pltpu.VMEM((2, 16, D), BF),
            pltpu.VMEM((2, MED, D), F32),
            pltpu.VMEM((2, 16, D), F32),
            pltpu.VMEM((8, 256), F32),
            pltpu.VMEM((8, INNER), F32),
            pltpu.VMEM((8, INNER), F32),
            pltpu.VMEM((8, INNER), F32),
            pltpu.VMEM((8, INNER), F32),
            pltpu.VMEM((8, FF), F32),
            pltpu.VMEM((8, FF), F32),
        ),
        in_specs=[hbm] * 16,
        out_specs=(vmem,) * N_OUT,
        scratch_shapes=[pltpu.VMEM(shape, dtype) for shape, dtype in SCRATCH.values()]
        + [
            pltpu.SemaphoreType.DMA((SEND_SEMS,)),
            pltpu.SemaphoreType.DMA((RECV_SEMS,)),
            pltpu.SemaphoreType.DMA((16,)),
            pltpu.SMEM((2,), jnp.int32),
        ],
        compiler_params=pltpu.CompilerParams(
            collective_id=0, has_side_effects=True, vmem_limit_bytes=52 * 2**20
        ),
    )(*[pltpu.with_memory_space_constraint(args[i], pltpu.HBM) for i in order])
    shapes = [jax.ShapeDtypeStruct(o.shape, o.dtype) for o in outs]
    mixed, gmedia, glat, _, gk, _, _, _, gup, _ = shapes
    one = jax.ShapeDtypeStruct((1, 8), F32)
    done = pl.pallas_call(
        hand_over,
        out_shape=(mixed, gmedia, glat) + (one,) * 6 + (gk,) * 4 + (gup,) * 2,
        in_specs=[vmem] * N_OUT,
        out_specs=(far,) * 15,
        scratch_shapes=[pltpu.VMEM((6, 1, 8), F32), pltpu.SemaphoreType.DMA((15,))],
        compiler_params=pltpu.CompilerParams(vmem_limit_bytes=52 * 2**20),
    )(*outs)
    vectors = tuple(v.reshape(8) for v in done[3:9])
    gq, gk, gv, go, gup, gdown = done[9:]
    return tuple(done[:3]) + vectors + (gq, gk, gv, go.T, gup, gdown.T)


def solution(mesh):
    tokens = P("dp", "pb", None)
    return jax.shard_map(
        per_device,
        mesh=mesh,
        in_specs=(tokens, tokens, P("dp")) + (P(),) * 12 + (tokens,),
        out_specs=(tokens, tokens, tokens)
        + (P(("dp", "pb")),) * 6
        + (P(("dp", "pb"), None),) * 3
        + (P(None, ("dp", "pb")), P(("dp", "pb"), None), P(None, ("dp", "pb"))),
        check_vma=False,
    )
```

```python
import functools
import itertools

import jax
import jax.numpy as jnp
from jax import lax
from jax.experimental import pallas as pl
from jax.experimental.pallas import tpu as pltpu
from jax.sharding import PartitionSpec as P

MESH = pl.DeviceIdType.MESH
BF = jnp.bfloat16
F32 = jnp.float32
D = 1024
INNER = 512
FF = 4096
MED = 144
LATD = 16
ROWS = MED + LATD
SLICE = FF // 8
EPSILON = 1e-05
NEG_FILL = -1e30
SCALE = 0.125
RECV_SEMS = 39
SEND_SEMS = 12


def mm(a, b):
    return jnp.dot(a, b, preferred_element_type=F32)


def mm_nt(a, b):
    return lax.dot_general(a, b, (((1,), (1,)), ((), ())), preferred_element_type=F32)


def mm_tn(a, b):
    return lax.dot_general(a, b, (((0,), (0,)), ((), ())), preferred_element_type=F32)


def normalised(v):
    cen = v - jnp.mean(v, axis=-1, keepdims=True)
    rstd = lax.rsqrt(jnp.mean(cen * cen, axis=-1, keepdims=True) + EPSILON)
    return cen * rstd, rstd


def ln_back(dn, xhat, rstd, gain):
    dx = dn * gain
    return rstd * (
        dx - jnp.mean(dx, axis=-1, keepdims=True) - xhat * jnp.mean(dx * xhat, axis=-1, keepdims=True)
    )


SCRATCH = dict(
    media=((2, MED, D), BF),
    norms=((6, 1, D), F32),
    mxhat=((2, MED, D), F32),
    mrstd=((2, MED, 128), F32),
    lc=((2, 4, 4, LATD, D), BF),
    wq=((D, INNER), BF),
    wk=((D, INNER), BF),
    wv=((D, INNER), BF),
    wo=((INNER, D), BF),
    ups=((D, SLICE), BF),
    downs=((SLICE, D), BF),
    xj=((2, ROWS, D), BF),
    xt=((2, D, 2 * ROWS), BF),
    kv=((2, ROWS, 2 * INNER), BF),
    qg=((4, 32, INNER), BF),
    qm=((8, 128, 128), BF),
    st=((8, ROWS, 128), F32),
    o_send=((4, 32, INNER), BF),
    o_all=((4, 32, INNER), BF),
    stats=((4, 16, 128), F32),
    sct=((128, 128), F32),
    lt=((8, 128), F32),
    attg=((2, 4, 32, INNER), BF),
    hid=((2, 4, 32, D), F32),
    nf=((2, 128, D), BF),
    cott=((D, 256), BF),
    dact=((2, 128, SLICE), F32),
    act=((2, 128, SLICE), BF),
    dup=((2, 128, SLICE), BF),
    nls=((2, 2, 32, D), BF),
    dnv=((2, 128, D), F32),
    xhv=((2, 128, D), F32),
    coto=((2, 32, INNER), F32),
    p_s=((128, INNER), BF),
    p_r=((128, INNER), BF),
    p_f=((4, 32, INNER), F32),
    p_x=((4, 32, INNER), BF),
    p_xr=((3, 2, 32, INNER), BF),
    dx_s=((128, D), BF),
    dx_r=((128, D), BF),
    dx_f=((4, 32, D), F32),
    dxa=((2, 4, 32, D), BF),
    dx_xr=((3, 32, D), BF),
    mx_s=((128, D), BF),
    mx_r=((128, D), BF),
    mx_f=((4, 32, D), F32),
    mx_x=((4, 32, D), BF),
    mx_xr=((3, 32, D), BF),
    dhid=((32, D), F32),
    dag=((2, 2, 32, INNER), BF),
    dkv=((2, ROWS, 2 * INNER), BF),
    dq_send=((2, 2, 32, INNER), BF),
    dq_all=((4, 32, INNER), BF),
    dq_r=((2, 2, 32, 256), BF),
    dj=((2, ROWS, D), F32),
    vec=((8, D), F32),
    vec_r=((8, D), F32),
    vec_a=((4, 8, 256), F32),
    vec_y=((3, 8, 256), F32),
    vec_b=((8, 256), F32),
    vec_p=((15, 8, 256), F32),
    gu=((4, 4, 64, SLICE), BF),
    gu_r1=((3, 4, 64, SLICE), BF),
    gu_s=((4, 64, SLICE), BF),
    gu_r2=((3, 64, SLICE), BF),
    gd=((4, 4, 64, SLICE), BF),
    gd_r1=((3, 4, 64, SLICE), BF),
    gd_s=((4, 64, SLICE), BF),
    gd_r2=((3, 64, SLICE), BF),
    gff=((8, 16, SLICE), BF),
    ffo=((16, FF), BF),
    dkv_r=((2, ROWS, INNER), BF),
    g_own=((D, INNER), F32),
)
FIRST = {"k0": "x", "k1": "y", "k2": "z", "og": "x"}
PLANE = sorted(itertools.product(range(4), range(4)), key=lambda d: -sum(min(a, 4 - a) for a in d))[:15]
for _n in FIRST:
    SCRATCH[f"{_n}_w"] = ((4, 4, 4, 16, 256), BF)
    SCRATCH[f"{_n}_r1"] = ((3, 4, 4, 16, 256), BF)
    SCRATCH[f"{_n}_s1"] = ((4, 4, 2, 16, 128), BF)
    SCRATCH[f"{_n}_r2"] = ((31, 16, 128), BF)
N_IN = 16
N_OUT = 10


class Refs:
    def __init__(self, names, refs):
        self.__dict__.update(zip(names, refs))

    def __getitem__(self, name):
        return self.__dict__[name]


def layer_kernel(*refs):
    (media_h, lat_h, cot_h, counts_h, mg_h, ms_h, lg_h, ls_h, fg_h, fs_h, wq_h, wk_h, wv_h, wo_h, up_h, down_h) = refs[:N_IN]
    (mixed_o, gmedia_o, glat_o, vec_o, gq_o, gk_o, gv_o, go_o, gup_o, gdown_o) = refs[N_IN : N_IN + N_OUT]
    r = Refs(SCRATCH, refs[N_IN + N_OUT : N_IN + N_OUT + len(SCRATCH)])
    ssem, rsem, lsem, counts = refs[N_IN + N_OUT + len(SCRATCH) :]
    mg, ms, lg, ls, fg, fs = (r.norms.at[k] for k in range(6))

    dp = lax.axis_index("dp")
    pb = lax.axis_index("pb")
    y = dp // 8
    z = (dp // 2) % 4
    xh = dp % 2
    xl = pb // 2
    c = pb % 2
    x = xh * 2 + xl
    g = x * 2 + c
    s = pb
    oc = 1 - c
    me = {"x": x, "y": y, "z": z}

    def dev(yy, zz, xx, cc):
        return ((yy * 4 + zz) * 2 + xx // 2, (xx % 2) * 2 + cc)

    def along(axis, d):
        at = dict(me)
        at[axis] = (me[axis] + d) % 4
        return dev(at["y"], at["z"], at["x"], c)

    def sub(k):
        xl2 = (xl + (k >> 1)) % 2
        c2 = (c + (k & 1)) % 2
        return dev(y, z, xh * 2 + xl2, c2), xl2 * 2 + c2

    def grp(k):
        x2 = (x + (k >> 1)) % 4
        c2 = (c + (k & 1)) % 2
        return dev(y, z, x2, c2), x2 * 2 + c2

    partner = dev(y, z, x, oc)
    counter = itertools.count()
    pending = {}

    class Sent:
        def __init__(self, whole):
            self.whole = whole
            self.index = next(counter)
            self.slot = self.index % SEND_SEMS
            if self.slot in pending:
                pending.pop(self.slot).wait_send()
            pending[self.slot] = self

        def copy(self, src, dst, target):
            return pltpu.make_async_remote_copy(
                src_ref=src,
                dst_ref=dst,
                send_sem=ssem.at[self.slot],
                recv_sem=rsem.at[self.index],
                device_id=target,
                device_id_type=MESH,
            )

        def add(self, src, dst, target):
            self.copy(src, dst, target).start()

        def wait_recv(self):
            self.copy(self.whole, self.whole, partner).wait_recv()

        def wait_send(self):
            self.copy(self.whole, self.whole, partner).wait_send()

    def send_all(whole, copies):
        sent = Sent(whole)
        for src, dst, target in copies:
            sent.add(src, dst, target)
        return sent

    def send(src, dst, target):
        return send_all(dst, [(src, dst, target)])

    local_counter = itertools.count()

    def fetch(src, dst):
        copy = pltpu.make_async_copy(src, dst, lsem.at[next(local_counter)])
        copy.start()
        return copy

    def index(axes, axis, at):
        return tuple(at if a == axis else slice(None) for a in axes)

    def added(own, got):
        part = own.astype(F32)
        for k in range(3):
            part += got[k].astype(F32)
        return part

    def first_step(n):
        axis, w, got = FIRST[n], r[f"{n}_w"], r[f"{n}_r1"]
        sent = Sent(got)
        for d in (2, 1, 3):
            sent.add(w.at[index("yzx", axis, (me[axis] + d) % 4)], got.at[d - 1], along(axis, d))
        return [sent]

    def second_step(n, before):
        for copy in before:
            copy.wait_recv()
        axis, out, got = FIRST[n], r[f"{n}_s1"], r[f"{n}_r2"]
        part = added(r[f"{n}_w"][index("yzx", axis, me[axis])], r[f"{n}_r1"])
        for h in range(2):
            rows = slice(h * 8, h * 8 + 8)
            both = jnp.concatenate([part[:, :, rows, :128], part[:, :, rows, 128:]], axis=2)
            out[:, :, h] = both.astype(BF)
        one, two = [a for a in "yzx" if a != axis]
        sent = Sent(got)
        for k, (d, e) in enumerate(PLANE):
            at = dict(me)
            at[one], at[two] = (me[one] + d) % 4, (me[two] + e) % 4
            block = out.at[at[one], at[two]]
            sent.add(block.at[c], got.at[k], dev(at["y"], at["z"], at["x"], c))
            sent.add(block.at[oc], got.at[15 + k], dev(at["y"], at["z"], at["x"], oc))
        sent.add(out.at[me[one], me[two], oc], got.at[30], partner)
        return [sent]

    def summed(n, before):
        for copy in before:
            copy.wait_recv()
        one, two = [a for a in "yzx" if a != FIRST[n]]
        got = r[f"{n}_r2"]
        mine = r[f"{n}_s1"][me[one], me[two], c].astype(F32)
        for k in range(15):
            mine += got[k].astype(F32)
        other = got[15].astype(F32)
        for k in range(16, 31):
            other += got[k].astype(F32)
        return [jnp.concatenate([v[:8], v[8:]], axis=1) for v in (mine, other)]

    barrier = pltpu.get_barrier_semaphore()
    greeted = [grp(k)[0] for k in range(1, 8)]
    greeted += [along(a, d) for a in ("y", "z") for d in (2, 1, 3)]
    for target in greeted:
        pl.semaphore_signal(barrier, inc=1, device_id=target, device_id_type=MESH)

    f_lat = fetch(lat_h, r.lc.at[c, x, pl.ds(0, 2)])
    f_lg, f_ls = fetch(lg_h, lg), fetch(ls_h, ls)
    f_wq = fetch(wq_h, r.wq)
    f_cot = fetch(cot_h, r.lc.at[c, x, pl.ds(2, 2)])
    f_mg, f_ms = fetch(mg_h, mg), fetch(ms_h, ms)
    f_media = fetch(media_h, r.media)
    f_wk = fetch(wk_h, r.wk)
    f_wv = fetch(wv_h, r.wv)
    f_counts = fetch(counts_h, counts)
    f_fg, f_fs = fetch(fg_h, fg), fetch(fs_h, fs)
    f_wo = fetch(wo_h, r.wo)
    f_down = fetch(down_h.at[pl.ds(g * SLICE, SLICE), :], r.downs)
    f_up = fetch(up_h.at[:, pl.ds(g * SLICE, SLICE)], r.ups)

    f_lat.wait()
    f_lg.wait()
    f_ls.wait()
    lat_own = r.lc[c, x, pl.ds(0, 2)].astype(F32).reshape(32, D)
    xhat, _ = normalised(lat_own)
    nl = (xhat * lg[...] + ls[...]).astype(BF)
    r.xj[0, pl.ds(MED, LATD), :] = nl[:16]
    r.xj[1, pl.ds(MED, LATD), :] = nl[16:]
    f_wq.wait()
    r.qg[s] = (mm(nl, r.wq[...]) * SCALE).astype(BF)

    pl.semaphore_wait(barrier, len(greeted))
    q_copies = [send_all(r.qg.at[pl.ds(0, 3)], [(r.qg.at[s], r.qg.at[s], sub(k)[0]) for k in (1, 2, 3)])]
    own_lat, own_cot = r.lc.at[c, x, pl.ds(0, 2)], r.lc.at[c, x, pl.ds(2, 2)]
    lat_copies = [send_all(r.lc.at[0, pl.ds(0, 3), pl.ds(0, 2)], [(own_lat, own_lat, along("x", d)) for d in (2, 1, 3)])]

    f_media.wait()
    f_mg.wait()
    f_ms.wait()
    for i in range(2):

        def norm_rows(t, carry, i=i):
            at = pl.ds(pl.multiple_of(t * 48, 48), 48)
            xh_, rs_ = normalised(r.media[i, at, :].astype(F32))
            r.mxhat[i, at, :] = xh_
            r.mrstd[i, at, :] = jnp.broadcast_to(rs_, (48, 128))
            r.xj[i, at, :] = (xh_ * mg[...] + ms[...]).astype(BF)
            return carry

        lax.fori_loop(0, MED // 48, norm_rows, 0)
    f_wk.wait()
    f_wv.wait()
    xj = r.xj[...].reshape(2 * ROWS, D)
    for n in range(0, INNER, 256):
        r.kv[:, :, n : n + 256] = mm(xj, r.wk[:, n : n + 256]).astype(BF).reshape(2, ROWS, 256)
        r.kv[:, :, INNER + n : INNER + n + 256] = (
            mm(xj, r.wv[:, n : n + 256]).astype(BF).reshape(2, ROWS, 256)
        )
    r.xt[c] = jnp.transpose(xj)
    xt_pair = send(r.xt.at[c], r.xt.at[c], partner)

    for copy in q_copies:
        copy.wait_recv()
    low = lax.broadcasted_iota(jnp.int32, (64, 128), 1) < 64
    row = lax.broadcasted_iota(jnp.int32, (ROWS, 128), 0)

    def by_head(v):
        v = v.astype(F32)
        return jnp.concatenate([jnp.where(low, v, 0.0), jnp.where(low, 0.0, v)], axis=0).astype(BF)

    def merged(v):
        return jnp.where(low, v[:64], v[64:])

    f_counts.wait()
    tops, sums = [], []
    o_sent = Sent(r.o_all.at[pl.ds(0, 3)])
    for i in range(2):
        q_i = jnp.concatenate([r.qg[k, pl.ds(i * 16, 16), :] for k in range(4)], axis=0)
        valid = (row >= MED) | (row + pb * MED < counts[i])
        for hp in range(4):
            ih = i * 4 + hp
            cols = slice(hp * 128, hp * 128 + 128)
            qm = by_head(q_i[:, cols])
            r.qm[ih] = qm
            st = jnp.where(valid, mm_nt(r.kv[i, :, cols], qm), NEG_FILL)
            r.st[ih] = st
            top = jnp.max(st, axis=0, keepdims=True)
            p = jnp.exp(st - top)
            tops.append(top)
            sums.append(jnp.sum(p, axis=0, keepdims=True))
            o = merged(mm_tn(p.astype(BF), r.kv[i, :, INNER + hp * 128 : INNER + hp * 128 + 128])).astype(BF)
            for k in range(4):
                r.o_send[k, pl.ds(i * 16, 16), cols] = o[k * 16 : k * 16 + 16]
        for k in (1, 2, 3):
            target, s2 = sub(k)
            at = pl.ds(i * 16, 16)
            o_sent.add(r.o_send.at[s2, at], r.o_all.at[s, at], target)
    r.stats[s] = jnp.concatenate(tops + sums, axis=0)
    st_copies = [send_all(r.stats.at[pl.ds(0, 3)], [(r.stats.at[s], r.stats.at[s], sub(k)[0]) for k in (1, 2, 3)])]
    o_copies = [o_sent]
    f_cot.wait()
    cot_copies = [send_all(r.lc.at[0, pl.ds(0, 3), pl.ds(2, 2)], [(own_cot, own_cot, along("x", d)) for d in (2, 1, 3)])]
    r.o_all[s] = r.o_send[s]

    for copy in lat_copies:
        copy.wait_recv()
    half = r.lc.at[c, :, pl.ds(0, 2)]
    lat_half = send(half, half, partner)

    lat_half.wait_recv()
    for h in range(2):
        xhat, _ = normalised(r.lc[h, pl.ds(xh * 2, 2), pl.ds(0, 2)].astype(F32).reshape(64, D))
        r.nls[h] = (xhat * lg[...] + ls[...]).astype(BF).reshape(2, 32, D)

    for copy in st_copies + o_copies:
        copy.wait_recv()
    stats = r.stats[...]
    peak = jnp.max(stats[:, :8], axis=0)
    weight = jnp.exp(stats[:, :8] - peak[None])
    total = jnp.sum(weight * stats[:, 8:], axis=0)
    r.lt[...] = peak + jnp.log(total)
    share = (weight / total[None]).reshape(32, 128)
    r.sct[...] = jnp.transpose(jnp.concatenate([share, jnp.zeros((96, 128), F32)], axis=0))
    low16 = low[:16]
    sc0 = r.sct[pl.ds(pl.multiple_of(s * 16, 16), 16), :]
    sc1 = r.sct[pl.ds(pl.multiple_of(64 + s * 16, 16), 16), :]
    att_rows = []
    for i in range(2):
        pairs = []
        for hp in range(4):
            ih = i * 4 + hp
            acc = jnp.zeros((16, 128), F32)
            for k in range(4):
                col = k * 8 + ih
                factor = jnp.where(low16, sc0[:, col : col + 1], sc1[:, col : col + 1])
                acc += r.o_all[k, pl.ds(i * 16, 16), hp * 128 : hp * 128 + 128].astype(F32) * factor
            pairs.append(acc)
        att_rows.append(jnp.concatenate(pairs, axis=1))
    att_own = jnp.concatenate(att_rows, axis=0).astype(BF)
    r.attg[c, x] = att_own
    mine = r.attg.at[c, x]
    att_copies = [send(mine, mine, along("x", d)) for d in (2, 1, 3)]
    halves = Sent(r.attg.at[0])
    halves.add(mine, mine, partner)
    arrivals = [halves]
    for copy in cot_copies:
        copy.wait_recv()
    half = r.lc.at[c, :, pl.ds(2, 2)]
    cot_half = send(half, half, partner)
    f_down.wait()
    f_wo.wait()
    r.dact[c] = mm_nt(r.lc[c, :, pl.ds(2, 2)].reshape(128, D), r.downs[...])
    cot_s = r.lc[c, pl.ds(xh * 2, 2), pl.ds(2, 2)].reshape(64, D)
    r.coto[...] = mm_nt(cot_s, r.wo[...]).reshape(2, 32, INNER)
    cot_half.wait_recv()
    r.cott[...] = jnp.transpose(r.lc[:, :, pl.ds(2, 2)].reshape(256, D))
    r.dact[oc] = mm_nt(r.lc[oc, :, pl.ds(2, 2)].reshape(128, D), r.downs[...])
    for d, copy in zip((2, 1, 3), att_copies):
        copy.wait_recv()
        part = r.attg.at[c, (x + 4 - d) % 4]
        halves.add(part, part, partner)

    f_up.wait()
    f_fg.wait()
    f_fs.wait()

    def feed_forward(h):
        lat_h_ = r.lc[h, :, pl.ds(0, 2)].astype(F32).reshape(128, D)
        hidden = lat_h_ + mm(r.attg[h].reshape(128, INNER), r.wo[...])
        r.hid[h] = hidden.reshape(4, 32, D)
        xh_, rs_ = normalised(hidden)
        r.xhv[h] = xh_
        nf = (xh_ * fg[...] + fs[...]).astype(BF)
        r.nf[h] = nf
        u = mm(nf, r.ups[...])
        cdf = 0.5 * (1.0 + lax.erf(u * 0.7071067811865476))
        slope = cdf + u * (jnp.exp(-0.5 * u * u) * 0.3989422804014327)
        r.act[h] = (u * cdf).astype(BF)
        dup = (r.dact[h] * slope).astype(BF)
        r.dup[h] = dup
        dn = mm_nt(dup, r.ups[...])
        r.dnv[h] = dn
        dx = ln_back(dn, xh_, rs_, fg[...])
        return dx, mm_nt(dx.astype(BF), r.wo[...])

    dx, p = feed_forward(c)
    r.dx_f[...] = dx.reshape(4, 32, D)
    r.p_f[...] = p.reshape(4, 32, INNER)
    for copy in arrivals:
        copy.wait_recv()
    dx, p = feed_forward(oc)
    r.p_s[...] = p.astype(BF)
    p_pair = send(r.p_s, r.p_r, partner)
    r.dx_s[...] = dx.astype(BF)
    dx_pair = send(r.dx_s, r.dx_r, partner)
    act_all = r.act[...].reshape(256, SLICE)
    for n in range(4):
        r.gd[n] = mm(r.cott[n * 256 : n * 256 + 256, :], act_all).astype(BF).reshape(4, 64, SLICE)
    gd_1 = [send_all(r.gd_r1, [(r.gd.at[:, (z + d) % 4], r.gd_r1.at[d - 1], along("z", d)) for d in (2, 1, 3)])]
    p_pair.wait_recv()
    p_sum = r.p_f[...] + r.p_r[...].astype(F32).reshape(4, 32, INNER)
    r.p_f[...] = p_sum
    r.p_x[...] = p_sum.astype(BF)
    p_sent = Sent(r.p_xr)
    for d in (2, 1, 3):
        src = r.p_x.at[pl.ds((x + d) % 4 // 2 * 2, 2)]
        p_sent.add(src, r.p_xr.at[d - 1], along("x", d))
    p_copies = [p_sent]
    nf_all = r.nf[...].reshape(256, D)
    dup_all = r.dup[...].reshape(256, SLICE)
    for n in range(4):
        r.gu[n] = mm_tn(nf_all[:, n * 256 : n * 256 + 256], dup_all).astype(BF).reshape(4, 64, SLICE)
    gu_1 = [send_all(r.gu_r1, [(r.gu.at[(y + d) % 4], r.gu_r1.at[d - 1], along("y", d)) for d in (2, 1, 3)])]
    dx_pair.wait_recv()
    dx_sum = r.dx_f[...] + r.dx_r[...].astype(F32).reshape(4, 32, D)
    r.dx_f[...] = dx_sum
    r.dx_f[x] += r.lc[c, x, pl.ds(2, 2)].astype(F32).reshape(32, D)
    r.dxa[c] = r.dx_f[...].astype(BF)
    dx_copies = [send_all(r.dx_xr, [(r.dxa.at[c, (x + d) % 4], r.dx_xr.at[d - 1], along("x", d)) for d in (2, 1, 3)])]
    dxa_pair = send(r.dxa.at[c], r.dxa.at[c], partner)
    dxa_pair.wait_recv()
    dxa = r.dxa[...].reshape(256, D)
    att_half = r.attg[:, :, :, pl.ds(pl.multiple_of(c * 256, 256), 256)].reshape(256, 256)
    for n in range(4):
        r.og_w[n] = mm_tn(dxa[:, n * 256 : n * 256 + 256], att_half).astype(BF).reshape(4, 4, 16, 256)
    og_1 = first_step("og")
    r.mx_s[...] = mm(r.act[oc], r.downs[...]).astype(BF)
    mx_pair = send(r.mx_s, r.mx_r, partner)
    r.mx_f[...] = mm(r.act[c], r.downs[...]).reshape(4, 32, D)

    for copy in p_copies:
        copy.wait_recv()
    da = r.coto[...] + r.p_f[pl.ds(xh * 2, 2)]
    for k in range(3):
        da += r.p_xr[k].astype(F32)
    r.dag[c] = da.astype(BF)
    da_pair = send(r.dag.at[c], r.dag.at[c], partner)
    gain_sum, shift_sum = jnp.zeros((8, D), F32), jnp.zeros((8, D), F32)
    for h in range(2):
        for t in range(0, 128, 32):
            dn = r.dnv[h, t : t + 32, :]
            gain_sum += jnp.sum((dn * r.xhv[h, t : t + 32, :]).reshape(4, 8, D), axis=0)
            shift_sum += jnp.sum(dn.reshape(4, 8, D), axis=0)
    r.vec[pl.ds(4, 1), :] = jnp.sum(gain_sum, axis=0, keepdims=True)
    r.vec[pl.ds(5, 1), :] = jnp.sum(shift_sum, axis=0, keepdims=True)
    r.vec[pl.ds(6, 2), :] = jnp.zeros((2, D), F32)

    da_pair.wait_recv()
    deltas = []
    for i in range(2):
        da_i = jnp.concatenate([r.dag[k % 2, k // 2, pl.ds(i * 16, 16), :] for k in range(4)], axis=0)
        at_i = jnp.concatenate(
            [r.attg[k % 2, xh * 2 + k // 2, pl.ds(i * 16, 16), :] for k in range(4)], axis=0
        )
        prod = da_i.astype(F32) * at_i.astype(F32)
        for hp in range(4):
            both = prod[:, hp * 128 : hp * 128 + 128]
            first = jnp.sum(jnp.where(low, both, 0.0), axis=1, keepdims=True)
            second = jnp.sum(jnp.where(low, 0.0, both), axis=1, keepdims=True)
            deltas.append(jnp.concatenate([first, second], axis=0))
    lane = lax.broadcasted_iota(jnp.int32, (128, 128), 1)
    spread = jnp.zeros((128, 128), F32)
    for ih in range(8):
        spread = jnp.where(lane == ih, deltas[ih], spread)
    r.sct[...] = jnp.transpose(spread)
    other_cols = pl.ds(pl.multiple_of(oc * INNER, INNER), INNER)
    kv_pair = Sent(r.dkv_r)
    for i in range(2):
        da_i = jnp.concatenate([r.dag[k % 2, k // 2, pl.ds(i * 16, 16), :] for k in range(4)], axis=0)
        for hp in range(4):
            ih = i * 4 + hp
            cols = slice(hp * 128, hp * 128 + 128)
            vcols = slice(INNER + hp * 128, INNER + hp * 128 + 128)
            dam = by_head(da_i[:, cols])
            dpt = mm_nt(r.kv[i, :, vcols], dam)
            pt = jnp.exp(r.st[ih] - r.lt[pl.ds(ih, 1), :])
            dst = (pt * (dpt - r.sct[pl.ds(ih, 1), :])).astype(BF)
            r.dkv[i, :, cols] = mm(dst, r.qm[ih]).astype(BF)
            r.dkv[i, :, vcols] = mm(pt.astype(BF), dam).astype(BF)
            dq = merged(mm_tn(dst, r.kv[i, :, cols])).astype(BF)
            for k in range(4):
                r.dq_send[k % 2, k // 2, pl.ds(i * 16, 16), cols] = dq[k * 16 : k * 16 + 16]
        kv_pair.add(r.dkv.at[i, :, other_cols], r.dkv_r.at[i], partner)

    own_cols = pl.ds(pl.multiple_of(c * INNER, INNER), INNER)
    own_half = pl.ds(pl.multiple_of(c * 256, 256), 256)
    other_half = pl.ds(pl.multiple_of(oc * 256, 256), 256)
    dq_pair = send(r.dq_send.at[:, :, :, other_half], r.dq_r, partner)
    dq_sent = Sent(r.dq_all.at[pl.ds(0, 3)])
    for k in (1, 2, 3):
        target, s2 = sub(k)
        dq_sent.add(r.dq_send.at[s2 % 2, s2 // 2], r.dq_all.at[s], target)
    dq_copies = [dq_sent]
    r.dq_all[s] = r.dq_send[c, xl]
    d_rows = r.dkv[:, :, own_cols].reshape(2 * ROWS, INNER)
    for n in range(4):
        r.g_own[n * 256 : n * 256 + 256, :] = mm(r.xt[c, n * 256 : n * 256 + 256, :], d_rows)
    xt_pair.wait_recv()
    kv_pair.wait_recv()

    def kv_block(n, cols):
        d_rows = r.dkv_r[:, :, cols].reshape(2 * ROWS, -1)
        at = slice(n * 256, n * 256 + 256)
        part = r.g_own[at, cols] + mm(r.xt[oc, at, :], d_rows)
        return part.astype(BF).reshape(4, 4, 16, -1)

    for n in range(4):
        r.k0_w[n] = kv_block(n, slice(0, 256))
    k0 = first_step("k0")
    dq_pair.wait_recv()
    dq_chip = r.dq_send[:, :, :, own_half].astype(F32) + r.dq_r[...].astype(F32)
    dq_chip = dq_chip.astype(BF).reshape(128, 256)
    nls = r.nls[...].reshape(128, D)
    for n in range(4):
        gq = (mm_tn(nls[:, n * 256 : n * 256 + 256], dq_chip) * SCALE).astype(BF)
        gq = gq.reshape(4, 4, 16, 256)
        r.k1_w[n, :, :, :, 128:] = gq[..., :128]
        r.k2_w[n, :, :, :, 128:] = gq[..., 128:]
        r.k1_w[n, :, :, :, :128] = kv_block(n, slice(256, 384))
        r.k2_w[n, :, :, :, :128] = kv_block(n, slice(384, 512))
    k1 = first_step("k1")
    k2 = first_step("k2")

    mx_pair.wait_recv()
    mx_sum = r.mx_f[...] + r.mx_r[...].astype(F32).reshape(4, 32, D)
    r.mx_f[...] = mx_sum
    r.mx_x[...] = mx_sum.astype(BF)
    mx_copies = [send_all(r.mx_xr, [(r.mx_x.at[(x + d) % 4], r.mx_xr.at[d - 1], along("x", d)) for d in (2, 1, 3)])]
    for copy in dx_copies:
        copy.wait_recv()
    r.dhid[...] = added(r.dx_f[x], r.dx_xr)

    for i in range(2):
        for n in range(0, D, 256):
            r.dj[i, :, n : n + 256] = mm_nt(r.dkv[i, :, :INNER], r.wk[n : n + 256, :]) + mm_nt(
                r.dkv[i, :, INNER:], r.wv[n : n + 256, :]
            )
    zero = jnp.zeros((8, D), F32)
    sums_of = (zero, zero)
    for i in range(2):

        def back_rows(t, carry, i=i):
            gain_sum, shift_sum = carry
            at = pl.ds(pl.multiple_of(t * 48, 48), 48)
            xh_ = r.mxhat[i, at, :]
            dn_ = r.dj[i, at, :]
            gmedia_o[i, at, :] = ln_back(dn_, xh_, r.mrstd[i, at, :1], mg[...])
            prod_ = dn_ * xh_
            return gain_sum + jnp.sum(prod_.reshape(6, 8, D), axis=0), shift_sum + jnp.sum(
                dn_.reshape(6, 8, D), axis=0
            )

        sums_of = lax.fori_loop(0, MED // 48, back_rows, sums_of)
    r.vec[pl.ds(0, 1), :] = jnp.sum(sums_of[0], axis=0, keepdims=True)
    r.vec[pl.ds(1, 1), :] = jnp.sum(sums_of[1], axis=0, keepdims=True)
    for copy in dq_copies:
        copy.wait_recv()
    dq = r.dq_all[0].astype(F32)
    for k in range(1, 4):
        dq += r.dq_all[k].astype(F32)
    dq = dq.astype(BF)
    dj_lat = jnp.concatenate([r.dj[0, pl.ds(MED, LATD), :], r.dj[1, pl.ds(MED, LATD), :]], axis=0)
    dnl = mm_nt(dq, r.wq[...]) * SCALE + dj_lat
    xhat, rstd = normalised(r.lc[c, x, pl.ds(0, 2)].astype(F32).reshape(32, D))
    r.vec[pl.ds(2, 1), :] = jnp.sum(dnl * xhat, axis=0, keepdims=True)
    r.vec[pl.ds(3, 1), :] = jnp.sum(dnl, axis=0, keepdims=True)
    vec_1 = send(r.vec, r.vec_r, partner)
    glat_o[...] = (r.dhid[...] + ln_back(dnl, xhat, rstd, lg[...])).reshape(2, 16, D)

    for copy in gd_1 + gu_1:
        copy.wait_recv()
    r.gd_s[...] = added(r.gd[:, z], r.gd_r1).astype(BF)
    gd_2 = [send_all(r.gd_r2, [(r.gd_s.at[(y + d) % 4], r.gd_r2.at[d - 1], along("y", d)) for d in (2, 1, 3)])]
    r.gu_s[...] = added(r.gu[y], r.gu_r1).astype(BF)
    gu_2 = [send_all(r.gu_r2, [(r.gu_s.at[(z + d) % 4], r.gu_r2.at[d - 1], along("z", d)) for d in (2, 1, 3)])]
    vec_1.wait_recv()
    for n in range(4):
        lanes = slice(n * 256, n * 256 + 256)
        r.vec_a[n] = r.vec[:, lanes] + r.vec_r[:, lanes]
    vec_2 = [send_all(r.vec_y, [(r.vec_a.at[(y + d) % 4], r.vec_y.at[d - 1], along("y", d)) for d in (2, 1, 3)])]

    og_2 = second_step("og", og_1)

    k0 = second_step("k0", k0)
    k1 = second_step("k1", k1)
    k2 = second_step("k2", k2)
    for copy in vec_2:
        copy.wait_recv()
    r.vec_b[...] = added(r.vec_a[y], r.vec_y)
    vec_sent = Sent(r.vec_p)
    for k, (d, e) in enumerate(PLANE):
        vec_sent.add(r.vec_b, r.vec_p.at[k], dev(y, (z + d) % 4, (x + e) % 4, c))
    vec_3 = [vec_sent]
    for copy in gd_2 + gu_2:
        copy.wait_recv()
    up = added(r.gu_s[z], r.gu_r2).reshape(8, 8, SLICE)
    down = added(r.gd_s[y], r.gd_r2).reshape(8, 8, SLICE)
    r.gff[...] = jnp.concatenate([up, down], axis=1).astype(BF)
    cols = pl.ds(pl.multiple_of(g * SLICE, SLICE), SLICE)
    gff_sent = Sent(r.ffo.at[:, pl.ds(0, 7 * SLICE)])
    for k in range(1, 8):
        target, g2 = grp(k)
        gff_sent.add(r.gff.at[g2], r.ffo.at[:, cols], target)
    gff_copies = [gff_sent]
    r.ffo[:, cols] = r.gff[g]
    for copy in mx_copies:
        copy.wait_recv()
    mixed_o[...] = (r.hid[c, x] + added(r.mx_f[x], r.mx_xr)).astype(BF).reshape(2, 16, D)
    mine, other = summed("og", og_2)
    go_o[:, own_half] = mine
    go_o[:, other_half] = other
    for copy in gff_copies:
        copy.wait_recv()
    gup_o[...] = r.ffo[pl.ds(0, 16), :].astype(F32)[:8]
    gdown_o[...] = r.ffo[pl.ds(0, 16), :].astype(F32)[8:]
    for copy in vec_3:
        copy.wait_recv()
    vec_o[...] = r.vec_b[...] + jnp.sum(r.vec_p[...], axis=0)
    first = c == 0
    mine, other = summed("k0", k0)
    gk_o[:, :256] = jnp.where(first, mine, other)
    gv_o[:, :256] = jnp.where(first, other, mine)
    for n, m, copies in ((0, "k1", k1), (1, "k2", k2)):
        mine, other = summed(m, copies)
        cols = slice(256 + n * 128, 384 + n * 128)
        gk_o[:, cols] = jnp.where(first, mine[:, :128], other[:, :128])
        gv_o[:, cols] = jnp.where(first, other[:, :128], mine[:, :128])
        gq_o[:, pl.ds(pl.multiple_of(c * 256 + n * 128, 128), 128)] = mine[:, 128:]
        gq_o[:, pl.ds(pl.multiple_of(oc * 256 + n * 128, 128), 128)] = other[:, 128:]
    for copy in pending.values():
        copy.wait_send()


def hand_over(mixed, gmedia, glat, vec, gq, gk, gv, go, gup, gdown, *refs):
    outs, lines, sem = refs[:15], refs[15], refs[16]
    pairs = [(gmedia, outs[1]), (glat, outs[2]), (gup, outs[13]), (gdown, outs[14]), (mixed, outs[0])]
    pairs += [(gq, outs[9]), (gk, outs[10]), (gv, outs[11]), (go, outs[12])]
    pairs += [(lines.at[i], outs[3 + i]) for i in range(6)]
    copies = [pltpu.make_async_copy(src, dst, sem.at[i]) for i, (src, dst) in enumerate(pairs)]
    for copy in copies[:9]:
        copy.start()
    place = lax.rem(lax.axis_index("dp") * 4 + lax.axis_index("pb"), 32) * 8
    turned = pltpu.roll(vec[...], lax.rem(256 - place, 256), 1)
    for i in range(6):
        lines[i] = turned[i : i + 1, :8]
    for copy in copies[9:]:
        copy.start()
    for copy in copies:
        copy.wait()


def per_device(*args):
    args = list(args)
    for i in range(3, 9):
        args[i] = args[i].reshape(1, D)
    hbm = pl.BlockSpec(memory_space=pl.ANY)
    vmem = pl.BlockSpec(memory_space=pltpu.VMEM)
    far = pl.BlockSpec(memory_space=pltpu.HBM)
    order = [0, 1, 15, 2, 3, 4, 5, 6, 7, 8, 9, 10, 11, 12, 13, 14]
    outs = pl.pallas_call(
        layer_kernel,
        out_shape=(
            pltpu.VMEM((2, 16, D), BF),
            pltpu.VMEM((2, MED, D), F32),
            pltpu.VMEM((2, 16, D), F32),
            pltpu.VMEM((8, 256), F32),
            pltpu.VMEM((8, INNER), F32),
            pltpu.VMEM((8, INNER), F32),
            pltpu.VMEM((8, INNER), F32),
            pltpu.VMEM((8, INNER), F32),
            pltpu.VMEM((8, FF), F32),
            pltpu.VMEM((8, FF), F32),
        ),
        in_specs=[hbm] * 16,
        out_specs=(vmem,) * N_OUT,
        scratch_shapes=[pltpu.VMEM(shape, dtype) for shape, dtype in SCRATCH.values()]
        + [
            pltpu.SemaphoreType.DMA((SEND_SEMS,)),
            pltpu.SemaphoreType.DMA((RECV_SEMS,)),
            pltpu.SemaphoreType.DMA((16,)),
            pltpu.SMEM((2,), jnp.int32),
        ],
        compiler_params=pltpu.CompilerParams(
            collective_id=0, has_side_effects=True, vmem_limit_bytes=52 * 2**20
        ),
    )(*[pltpu.with_memory_space_constraint(args[i], pltpu.HBM) for i in order])
    shapes = [jax.ShapeDtypeStruct(o.shape, o.dtype) for o in outs]
    mixed, gmedia, glat, _, gk, _, _, _, gup, _ = shapes
    one = jax.ShapeDtypeStruct((1, 8), F32)
    done = pl.pallas_call(
        hand_over,
        out_shape=(mixed, gmedia, glat) + (one,) * 6 + (gk,) * 4 + (gup,) * 2,
        in_specs=[vmem] * N_OUT,
        out_specs=(far,) * 15,
        scratch_shapes=[pltpu.VMEM((6, 1, 8), F32), pltpu.SemaphoreType.DMA((15,))],
        compiler_params=pltpu.CompilerParams(vmem_limit_bytes=52 * 2**20),
    )(*outs)
    vectors = tuple(v.reshape(8) for v in done[3:9])
    gq, gk, gv, go, gup, gdown = done[9:]
    return tuple(done[:3]) + vectors + (gq, gk, gv, go.T, gup, gdown.T)


def solution(mesh):
    tokens = P("dp", "pb", None)
    return jax.shard_map(
        per_device,
        mesh=mesh,
        in_specs=(tokens, tokens, P("dp")) + (P(),) * 12 + (tokens,),
        out_specs=(tokens, tokens, tokens)
        + (P(("dp", "pb")),) * 6
        + (P(("dp", "pb"), None),) * 3
        + (P(None, ("dp", "pb")), P(("dp", "pb"), None), P(None, ("dp", "pb"))),
        check_vma=False,
    )
```
